32 devices in a mesh: outer: 4 (over x, core), vocab: 8 (over z, y).
Axes of the slice: x: 2, y: 2, z: 4, core: 2. Of those that a mesh axis runs over, the one named last changes fastest.
Arguments:
- hidden: bfloat16 [512, 4096], P(('outer', 'vocab')), parts along dimension 0, may hold values from -96 to 96
- targets: int32 [512], P(('outer', 'vocab')), parts along dimension 0, may hold values from 0 to 16383
- head: bfloat16 [16384, 16384], P('outer', 'vocab'), parts along dimension 0, may hold values from -1 to 1
- global_frag: float32 [128, 16384], P(None, 'vocab'), may hold values from -6 to 6
- momentum: float32 [128, 16384], P(None, 'vocab'), may hold values from -6 to 6
- peer_delta: float32 [512, 16384], P('outer', 'vocab'), parts along dimension 0, may hold values from -6 to 6
Outputs:
- loss: float32 [4], P('outer'), parts along dimension 0
- hidden_grad: bfloat16 [512, 4096], P(('outer', 'vocab')), parts along dimension 0
- new_global: float32 [512, 16384], P('outer', 'vocab'), parts along dimension 0
- new_momentum: float32 [512, 16384], P('outer', 'vocab'), parts along dimension 0
The draws below stay inside these ranges and needn't reach their ends.
There are 4 independent parts, one for each index of `outer`. The reference program is written for one: setup_inputs(seed, part) draws one part's arguments, and reference() takes and returns one part's arrays. A program takes and returns all parts, laid end to end along the dimension named above; an argument that names none is the same for every part. Nothing has to cross between parts.
All inputs are finite; a program needn't handle non-finite values.
Results may differ from the reference program's by a relative error of at most 0.0031.
Values may be sent and summed in bfloat16 or wider, within the bound.
No kernel may reach another device: no remote copies, remote signals or barrier semaphores. Data moves between devices by JAX's collectives and lax.ppermute only.
A program may use at most 128 MiB of HBM per device.

```python
import jax
import jax.numpy as jnp
from jax import lax

D = 4096
FRAG = 128
REPLICAS = 4
ROWS = 128
VOCAB = 16384


def head_base(key):
    inner = jax.random.fold_in(key, 11)
    values = jnp.clip(jax.random.normal(inner, (D, VOCAB), jnp.float32), -6.0, 6.0)
    return values * D ** (-0.5)


def draw_head(key, part):
    base = head_base(key)
    return base.astype(jnp.bfloat16)


def draw_hidden(key, part):
    key = jax.random.fold_in(key, 3)
    rows_drawn = 3.0 * jnp.clip(jax.random.normal(key, (ROWS, D), jnp.float32), -5.0, 5.0)
    return rows_drawn.astype(jnp.bfloat16)


def plant(result, own_key, low, largest):
    longest = result.shape.index(max(result.shape))
    spots = []
    for shift in (0, 1):
        where = [jax.random.randint(jax.random.fold_in(own_key, axis), (), 0, length) for axis, length in enumerate(result.shape)]
        where[longest] = (where[longest] + shift) % result.shape[longest]
        spots.append(tuple(where))
    return result.at[spots[0]].set(low).at[spots[1]].set(largest)


def levels(stream_key, extent, shards, low, largest):
    def one(axis_at, shards_of):
        steps = jax.random.uniform(jax.random.fold_in(jax.random.fold_in(stream_key, 6), axis_at), (shards_of,), jnp.float32, low / len(shards), largest / len(shards))
        return jnp.repeat(jnp.exp(steps), extent[axis_at] // shards_of).reshape((-1,) + (1,) * (len(extent) - axis_at - 1))

    level = one(*shards[0])
    for cut in shards[1:]:
        level = level * one(*cut)
    return level


def centred(stream_key, extent, scale, bound, pieces=(), held_as=jnp.bfloat16):
    drawn = jax.random.normal(stream_key, extent, jnp.float32) * scale
    if len(pieces) > 0:
        drawn = levels(stream_key, extent, pieces, -0.22, 0.18) * drawn
    return jnp.clip(drawn, min=-bound, max=bound).astype(held_as)


def setup_inputs(seed: int = 0, part: int = 0) -> dict:
    splits = jax.random.split(jax.random.key(seed), 7)
    part_keys = jax.random.split(jax.random.fold_in(splits[6], part), 7)
    return {
        "hidden": draw_hidden(jax.random.fold_in(jax.random.fold_in(splits[6], part), 71), part),
        "targets": plant(jax.random.randint(part_keys[1], (ROWS,), 0, VOCAB), jax.random.fold_in(part_keys[1], 1), 0, VOCAB - 1).astype(jnp.int32),
        "head": draw_head(jax.random.fold_in(jax.random.fold_in(splits[6], part), 71), part),
        "global_frag": centred(splits[3], (FRAG, VOCAB), 1.0, 6.0, ((1, 8),), jnp.float32),
        "momentum": centred(splits[4], (FRAG, VOCAB), 1.0, 6.0, ((1, 8),), jnp.float32),
        "peer_delta": centred(part_keys[5], (FRAG, VOCAB), 1.0, 6.0, ((1, 8),), jnp.float32),
    }


def reference(hidden, targets, head, global_frag, momentum, peer_delta):
    logits = jnp.dot(hidden, head, preferred_element_type=jnp.float32)
    top = jnp.max(logits, axis=1)
    shifted = jnp.exp(logits - top[:, None])
    total = jnp.sum(shifted, axis=1)
    columns = jnp.arange(logits.shape[1], dtype=jnp.int32)
    onehot = (columns[None, :] == targets[:, None]).astype(jnp.float32)
    picked = jnp.sum(logits * onehot, axis=1)
    loss = jnp.mean(top + jnp.log(total) - picked).reshape((1,))
    dlogits = ((shifted / total[:, None] - onehot) / ROWS).astype(jnp.bfloat16)
    hidden_grad = lax.dot_general(dlogits, head, (((1,), (1,)), ((), ())), preferred_element_type=jnp.float32).astype(jnp.bfloat16)
    frag_grad = lax.dot_general(hidden[:, :FRAG], dlogits, (((0,), (0,)), ((), ())), preferred_element_type=jnp.float32)
    local_frag = head[:FRAG].astype(jnp.float32) - 1.0 * frag_grad
    pseudo = (global_frag - local_frag + peer_delta) / REPLICAS
    new_momentum = 0.9 * momentum + pseudo
    new_global = global_frag - 0.7 * (pseudo + 0.9 * new_momentum)
    return loss, hidden_grad, new_global, new_momentum
```

```python
import jax
import jax.numpy as jnp
from jax import lax
from jax.sharding import PartitionSpec as P

FRAG = 128
REPLICAS = 4
AXIS = "vocab"


def swap(value, members, step):
    return lax.ppermute(value, AXIS, [(i, i ^ step) for i in range(members)])


def gather(value, members):
    return [value] + [swap(value, members, step) for step in range(1, members)]


def body(hidden, targets, head, global_frag, momentum, peer_delta):
    members = lax.axis_size(AXIS)
    own = hidden.shape[0]
    rows = own * members
    width = head.shape[1]

    rows_all = jnp.concatenate(gather(hidden, members), axis=0)
    ids_all = jnp.concatenate(gather(targets, members), axis=0)

    logits = jnp.dot(rows_all, head, preferred_element_type=jnp.float32)
    columns = lax.axis_index(AXIS) * width + jnp.arange(width, dtype=jnp.int32)
    hit = columns[None, :] == ids_all[:, None]
    local_max = jnp.max(logits, axis=1)
    local_sum = jnp.sum(jnp.exp(logits - local_max[:, None]), axis=1)
    local_pick = jnp.sum(jnp.where(hit, logits, 0.0), axis=1)

    stats = jnp.stack([local_max, local_sum, local_pick]).reshape(3, members, own)
    seen = [stats]
    for step in range(1, members):
        there = swap(stats, members, step)
        seen.append(there[:, jnp.array([i ^ step for i in range(members)])])
    seen = jnp.stack(seen).reshape(members, 3, rows)
    top = jnp.max(seen[:, 0], axis=0)
    total = jnp.sum(seen[:, 1] * jnp.exp(seen[:, 0] - top), axis=0)
    picked = jnp.sum(seen[:, 2], axis=0)
    loss = jnp.mean(top + jnp.log(total) - picked).reshape((1,))

    onehot = hit.astype(jnp.float32)
    dlogits = ((jnp.exp(logits - top[:, None]) / total[:, None] - onehot) / rows).astype(jnp.bfloat16)
    partial_grad = lax.dot_general(
        dlogits, head, (((1,), (1,)), ((), ())), preferred_element_type=jnp.float32
    )
    summed = partial_grad[:own]
    for step in range(1, members):
        block = partial_grad[step * own : (step + 1) * own].astype(jnp.bfloat16)
        summed = summed + swap(block, members, step).astype(jnp.float32)
    hidden_grad = summed.astype(jnp.bfloat16)

    frag_grad = lax.dot_general(
        rows_all[:, :FRAG], dlogits, (((0,), (0,)), ((), ())), preferred_element_type=jnp.float32
    )
    local_frag = head[:FRAG].astype(jnp.float32) - 1.0 * frag_grad
    pseudo = (global_frag - local_frag + peer_delta) / REPLICAS
    new_momentum = 0.9 * momentum + pseudo
    new_global = global_frag - 0.7 * (pseudo + 0.9 * new_momentum)
    return (loss, hidden_grad, new_global, new_momentum)


def solution(mesh):
    in_specs = (
        P(("outer", "vocab"), None),
        P(("outer", "vocab")),
        P("outer", "vocab"),
        P(None, "vocab"),
        P(None, "vocab"),
        P("outer", "vocab"),
    )
    out_specs = (P("outer"), P(("outer", "vocab"), None), P("outer", "vocab"), P("outer", "vocab"))
    return jax.shard_map(body, mesh=mesh, in_specs=in_specs, out_specs=out_specs, check_vma=False)
```

```python
import jax
import jax.numpy as jnp
from jax import lax
from jax.sharding import PartitionSpec as P

FRAG = 128
REPLICAS = 4
AXIS = "vocab"


def gather(value):
    members = lax.axis_size(AXIS)
    copies = jnp.broadcast_to(value[None], (members,) + value.shape)
    return lax.all_to_all(copies, AXIS, split_axis=0, concat_axis=0)


def body(hidden, targets, head, global_frag, momentum, peer_delta):
    members = lax.axis_size(AXIS)
    own, depth = hidden.shape
    rows = own * members
    width = head.shape[1]

    digits = jnp.stack([targets // 256, targets % 256], axis=1).astype(jnp.bfloat16)
    packed = jnp.concatenate([hidden, jnp.pad(digits, ((0, 0), (0, 126)))], axis=1)
    packed = gather(packed).reshape(rows, depth + 128)
    rows_all = packed[:, :depth]
    digits = packed[:, depth : depth + 2].astype(jnp.int32)
    ids_all = digits[:, 0] * 256 + digits[:, 1]

    logits = jnp.dot(rows_all, head, preferred_element_type=jnp.float32)
    columns = lax.axis_index(AXIS) * width + jnp.arange(width, dtype=jnp.int32)
    hit = columns[None, :] == ids_all[:, None]
    local_max = jnp.max(logits, axis=1)
    local_sum = jnp.sum(jnp.exp(logits - local_max[:, None]), axis=1)
    local_pick = jnp.sum(jnp.where(hit, logits, 0.0), axis=1)

    seen = gather(jnp.stack([local_max, local_sum, local_pick]))
    top = jnp.max(seen[:, 0], axis=0)
    total = jnp.sum(seen[:, 1] * jnp.exp(seen[:, 0] - top), axis=0)
    picked = jnp.sum(seen[:, 2], axis=0)
    loss = jnp.mean(top + jnp.log(total) - picked).reshape((1,))

    onehot = hit.astype(jnp.float32)
    dlogits = ((jnp.exp(logits - top[:, None]) / total[:, None] - onehot) / rows).astype(jnp.bfloat16)
    partial_grad = lax.dot_general(
        dlogits, head, (((1,), (1,)), ((), ())), preferred_element_type=jnp.float32
    )
    blocks = partial_grad.astype(jnp.bfloat16).reshape(members, own, depth)
    blocks = lax.all_to_all(blocks, AXIS, split_axis=0, concat_axis=0)
    hidden_grad = jnp.sum(blocks.astype(jnp.float32), axis=0).astype(jnp.bfloat16)

    frag_grad = lax.dot_general(
        rows_all[:, :FRAG], dlogits, (((0,), (0,)), ((), ())), preferred_element_type=jnp.float32
    )
    local_frag = head[:FRAG].astype(jnp.float32) - 1.0 * frag_grad
    pseudo = (global_frag - local_frag + peer_delta) / REPLICAS
    new_momentum = 0.9 * momentum + pseudo
    new_global = global_frag - 0.7 * (pseudo + 0.9 * new_momentum)
    return (loss, hidden_grad, new_global, new_momentum)


def solution(mesh):
    in_specs = (
        P(("outer", "vocab"), None),
        P(("outer", "vocab")),
        P("outer", "vocab"),
        P(None, "vocab"),
        P(None, "vocab"),
        P("outer", "vocab"),
    )
    out_specs = (P("outer"), P(("outer", "vocab"), None), P("outer", "vocab"), P("outer", "vocab"))
    return jax.shard_map(body, mesh=mesh, in_specs=in_specs, out_specs=out_specs, check_vma=False)
```

```python
import jax
import jax.numpy as jnp
from jax import lax
from jax.sharding import PartitionSpec as P

FRAG = 128
REPLICAS = 4
AXIS = "vocab"
SEND = jnp.float16


def swap(value, step):
    return lax.ppermute(value, AXIS, [(i, i ^ step) for i in range(lax.axis_size(AXIS))])


def doubled(value, step):
    return jnp.concatenate([value, swap(value, step)], axis=0)


def far_steps():
    step = lax.axis_size(AXIS) // 2
    steps = []
    while step > 2:
        steps.append(step)
        step //= 2
    return steps


def flip_blocks(value, own):
    members = lax.axis_size(AXIS)
    me = lax.axis_index(AXIS)
    lead = value.shape[:-1]
    bits = [1, 2] + far_steps()[::-1]
    value = value.reshape(lead + (2,) * len(bits) + (own,))
    for place, bit in enumerate(bits):
        value = jnp.where((me & bit) != 0, jnp.flip(value, len(lead) + place), value)
    return value.reshape(lead + (members * own,))


def to_device_order(value, own):
    value = flip_blocks(value, own)
    return reverse_bits(value, own)


def to_xor_order(value, own):
    return flip_blocks(reverse_bits(value, own), own)


def reverse_bits(value, own):
    lead = value.shape[:-1]
    count = len(far_steps()) + 2
    value = value.reshape(lead + (2,) * count + (own,))
    first = len(lead)
    order = list(range(first)) + list(range(first + count - 1, first - 1, -1)) + [first + count]
    return value.transpose(order).reshape(lead + (-1,))


def gather_rows(hidden, digits):
    half = hidden.shape[1] // 2
    for step in far_steps():
        hidden, digits = doubled(hidden, step), doubled(digits, step)
    left = jnp.concatenate([hidden[:, :half], digits], axis=1)
    right = hidden[:, half:]
    near = right.shape[0]
    left = doubled(left, 2)
    right = doubled(right, 1)
    left = doubled(left, 1)
    other = swap(right, 2)
    right = jnp.concatenate([right[:near], other[:near], right[near:], other[near:]], axis=0)
    return left[:, :half], right, left[:, half:]


def scatter_sums(left, right, scale):
    rows = left.shape[0]
    quarter = rows // 4

    def code(value):
        return (value * scale).astype(SEND)

    def decode(value):
        return value.astype(jnp.float32) * (1.0 / scale)

    left = left[: rows // 2] + decode(swap(code(left[rows // 2 :]), 1))
    right = right.reshape(2, 2, quarter, -1)
    right = right[:, 0] + decode(swap(code(right[:, 1]), 2))
    left = left[:quarter] + decode(swap(code(left[quarter:]), 2))
    right = right[0] + decode(swap(code(right[1]), 1))
    both = jnp.concatenate([left, right], axis=1)
    for step in far_steps()[::-1]:
        keep = both.shape[0] // 2
        both = both[:keep] + decode(swap(code(both[keep:]), step))
    return both


def body(hidden, targets, head, global_frag, momentum, peer_delta):
    members = lax.axis_size(AXIS)
    own, depth = hidden.shape
    half = depth // 2
    rows = own * members
    width = head.shape[1]

    digits = jnp.stack([targets // 256, targets % 256], axis=1).astype(jnp.bfloat16)
    digits = jnp.pad(digits, ((0, 0), (0, 126)))
    left, right, digits = gather_rows(hidden, digits)
    digits = digits[:, :2].astype(jnp.int32)
    ids_all = digits[:, 0] * 256 + digits[:, 1]

    logits = jnp.dot(left, head[:half], preferred_element_type=jnp.float32)
    logits = logits + jnp.dot(right, head[half:], preferred_element_type=jnp.float32)
    columns = lax.axis_index(AXIS) * width + jnp.arange(width, dtype=jnp.int32)
    hit = columns[None, :] == ids_all[:, None]
    local_max = jnp.max(logits, axis=1)
    local_sum = jnp.sum(jnp.exp(logits - local_max[:, None]), axis=1)
    local_pick = jnp.sum(jnp.where(hit, logits, 0.0), axis=1)

    stats = to_device_order(jnp.stack([local_max, local_sum, local_pick]), own)
    seen = lax.all_to_all(
        jnp.broadcast_to(stats[None], (members,) + stats.shape), AXIS, split_axis=0, concat_axis=0
    )
    top = jnp.max(seen[:, 0], axis=0)
    total = jnp.sum(seen[:, 1] * jnp.exp(seen[:, 0] - top), axis=0)
    picked = jnp.sum(seen[:, 2], axis=0)
    loss = jnp.mean(top + jnp.log(total) - picked).reshape((1,))
    top, total = to_xor_order(jnp.stack([top, total]), own)

    onehot = hit.astype(jnp.float32)
    dlogits = ((jnp.exp(logits - top[:, None]) / total[:, None] - onehot) / rows).astype(jnp.bfloat16)

    def grad(part):
        return lax.dot_general(
            dlogits, part, (((1,), (1,)), ((), ())), preferred_element_type=jnp.float32
        )

    hidden_grad = scatter_sums(grad(head[:half]), grad(head[half:]), 2.0**14 * rows).astype(jnp.bfloat16)

    frag_grad = lax.dot_general(
        left[:, :FRAG], dlogits, (((0,), (0,)), ((), ())), preferred_element_type=jnp.float32
    )
    local_frag = head[:FRAG].astype(jnp.float32) - 1.0 * frag_grad
    pseudo = (global_frag - local_frag + peer_delta) / REPLICAS
    new_momentum = 0.9 * momentum + pseudo
    new_global = global_frag - 0.7 * (pseudo + 0.9 * new_momentum)
    return (loss, hidden_grad, new_global, new_momentum)


def solution(mesh):
    in_specs = (
        P(("outer", "vocab"), None),
        P(("outer", "vocab")),
        P("outer", "vocab"),
        P(None, "vocab"),
        P(None, "vocab"),
        P("outer", "vocab"),
    )
    out_specs = (P("outer"), P(("outer", "vocab"), None), P("outer", "vocab"), P("outer", "vocab"))
    return jax.shard_map(body, mesh=mesh, in_specs=in_specs, out_specs=out_specs, check_vma=False)
```

```python
import jax
import jax.numpy as jnp
from jax import lax
from jax.experimental import pallas as pl
from jax.experimental.pallas import tpu as pltpu
from jax.sharding import PartitionSpec as P

FRAG = 128
REPLICAS = 4
AXIS = "vocab"
SEND = jnp.float16


def resident(head):
    cuts = 4
    block = head.shape[0] // cuts

    def kernel(source, target, sems):
        copies = []
        for i in range(cuts):
            part = pl.ds(i * block, block)
            copies.append(pltpu.make_async_copy(source.at[part], target.at[part], sems.at[i]))
        for copy in copies:
            copy.start()
        for copy in copies:
            copy.wait()

    size = head.size * head.dtype.itemsize
    return pl.pallas_call(
        kernel,
        out_shape=pltpu.VMEM(head.shape, head.dtype),
        in_specs=[pl.BlockSpec(memory_space=pltpu.HBM)],
        out_specs=pl.BlockSpec(memory_space=pltpu.VMEM),
        scratch_shapes=[pltpu.SemaphoreType.DMA((cuts,))],
        compiler_params=pltpu.CompilerParams(vmem_limit_bytes=size + 2**20),
        cost_estimate=pl.CostEstimate(flops=0, bytes_accessed=size, transcendentals=0),
    )(head)


def swap(value, step):
    return lax.ppermute(value, AXIS, [(i, i ^ step) for i in range(lax.axis_size(AXIS))])


def doubled(value, step):
    return jnp.concatenate([value, swap(value, step)], axis=0)


def far_steps():
    step = lax.axis_size(AXIS) // 2
    steps = []
    while step > 2:
        steps.append(step)
        step //= 2
    return steps


def flip_blocks(value, own):
    members = lax.axis_size(AXIS)
    me = lax.axis_index(AXIS)
    lead = value.shape[:-1]
    bits = [1, 2] + far_steps()[::-1]
    value = value.reshape(lead + (2,) * len(bits) + (own,))
    for place, bit in enumerate(bits):
        value = jnp.where((me & bit) != 0, jnp.flip(value, len(lead) + place), value)
    return value.reshape(lead + (members * own,))


def to_device_order(value, own):
    value = flip_blocks(value, own)
    return reverse_bits(value, own)


def to_xor_order(value, own):
    return flip_blocks(reverse_bits(value, own), own)


def reverse_bits(value, own):
    lead = value.shape[:-1]
    count = len(far_steps()) + 2
    value = value.reshape(lead + (2,) * count + (own,))
    first = len(lead)
    order = list(range(first)) + list(range(first + count - 1, first - 1, -1)) + [first + count]
    return value.transpose(order).reshape(lead + (-1,))


def gather_rows(hidden, digits):
    half = hidden.shape[1] // 2
    for step in far_steps():
        hidden, digits = doubled(hidden, step), doubled(digits, step)
    left = jnp.concatenate([hidden[:, :half], digits], axis=1)
    right = hidden[:, half:]
    near = right.shape[0]
    left = doubled(left, 2)
    right = doubled(right, 1)
    left = doubled(left, 1)
    other = swap(right, 2)
    right = jnp.concatenate([right[:near], other[:near], right[near:], other[near:]], axis=0)
    return left[:, :half], right, left[:, half:]


def scatter_sums(left, right, scale):
    rows = left.shape[0]
    quarter = rows // 4

    def code(value):
        return (value * scale).astype(SEND)

    def decode(value):
        return value.astype(jnp.float32) * (1.0 / scale)

    left = left[: rows // 2] + decode(swap(code(left[rows // 2 :]), 1))
    right = right.reshape(2, 2, quarter, -1)
    right = right[:, 0] + decode(swap(code(right[:, 1]), 2))
    left = left[:quarter] + decode(swap(code(left[quarter:]), 2))
    right = right[0] + decode(swap(code(right[1]), 1))
    both = jnp.concatenate([left, right], axis=1)
    for step in far_steps()[::-1]:
        keep = both.shape[0] // 2
        both = both[:keep] + decode(swap(code(both[keep:]), step))
    return both


def body(hidden, targets, head, global_frag, momentum, peer_delta):
    members = lax.axis_size(AXIS)
    own, depth = hidden.shape
    half = depth // 2
    rows = own * members
    width = head.shape[1]

    digits = jnp.stack([targets // 256, targets % 256], axis=1).astype(jnp.bfloat16)
    digits = jnp.pad(digits, ((0, 0), (0, 126)))
    left, right, digits = gather_rows(hidden, digits)
    digits = digits[:, :2].astype(jnp.int32)
    ids_all = digits[:, 0] * 256 + digits[:, 1]

    near = resident(head)
    logits = jnp.dot(left, near[:half], preferred_element_type=jnp.float32)
    logits = logits + jnp.dot(right, near[half:], preferred_element_type=jnp.float32)
    columns = lax.axis_index(AXIS) * width + jnp.arange(width, dtype=jnp.int32)
    hit = columns[None, :] == ids_all[:, None]
    local_max = jnp.max(logits, axis=1)
    raised = jnp.exp(logits - local_max[:, None])
    local_sum = jnp.sum(raised, axis=1)
    local_pick = jnp.sum(jnp.where(hit, logits, 0.0), axis=1)

    stats = to_device_order(jnp.stack([local_max, local_sum, local_pick]), own)
    seen = lax.all_to_all(
        jnp.broadcast_to(stats[None], (members,) + stats.shape), AXIS, split_axis=0, concat_axis=0
    )
    top = jnp.max(seen[:, 0], axis=0)
    total = jnp.sum(seen[:, 1] * jnp.exp(seen[:, 0] - top), axis=0)
    picked = jnp.sum(seen[:, 2], axis=0)
    loss = jnp.mean(top + jnp.log(total) - picked).reshape((1,))
    top, total = to_xor_order(jnp.stack([top, total]), own)

    both = jnp.concatenate([jnp.where(hit, 0.0, raised), hit.astype(jnp.float32)]).astype(jnp.bfloat16)
    both = lax.optimization_barrier(both)

    soft = jnp.exp(local_max - top) / (total * rows)
    hard = ((jnp.exp(local_pick - top) / total - 1.0) / rows).astype(jnp.bfloat16).astype(jnp.float32)

    def grad(part):
        terms = lax.dot_general(
            both, part, (((1,), (1,)), ((), ())), preferred_element_type=jnp.float32
        )
        terms = lax.optimization_barrier(terms)
        return soft[:, None] * terms[:rows] + hard[:, None] * terms[rows:]

    hidden_grad = scatter_sums(grad(near[:half]), grad(near[half:]), 2.0**14 * rows).astype(jnp.bfloat16)

    onehot = hit.astype(jnp.float32)
    dlogits = ((jnp.exp(logits - top[:, None]) / total[:, None] - onehot) / rows).astype(jnp.bfloat16)
    frag_grad = lax.dot_general(
        left[:, :FRAG], dlogits, (((0,), (0,)), ((), ())), preferred_element_type=jnp.float32
    )
    local_frag = head[:FRAG].astype(jnp.float32) - 1.0 * frag_grad
    pseudo = (global_frag - local_frag + peer_delta) / REPLICAS
    new_momentum = 0.9 * momentum + pseudo
    new_global = global_frag - 0.7 * (pseudo + 0.9 * new_momentum)
    return (loss, hidden_grad, new_global, new_momentum)


def solution(mesh):
    in_specs = (
        P(("outer", "vocab"), None),
        P(("outer", "vocab")),
        P("outer", "vocab"),
        P(None, "vocab"),
        P(None, "vocab"),
        P("outer", "vocab"),
    )
    out_specs = (P("outer"), P(("outer", "vocab"), None), P("outer", "vocab"), P("outer", "vocab"))
    return jax.shard_map(body, mesh=mesh, in_specs=in_specs, out_specs=out_specs, check_vma=False)
```

```python
import functools

import jax
import jax.numpy as jnp
from jax import lax
from jax.experimental import pallas as pl
from jax.experimental.pallas import tpu as pltpu
from jax.sharding import PartitionSpec as P

FRAG = 128
REPLICAS = 4
AXIS = "vocab"
SEND = jnp.float16
LANES = 128
VMEM = pl.BlockSpec(memory_space=pltpu.VMEM)


def call(kernel, outs, operands, flops=0, scratch=(), sources=None, vmem=16 * 2**20):
    outs = [pltpu.VMEM(shape, dtype) for shape, dtype in outs]
    places = sources or [pltpu.VMEM] * len(operands)
    moved = sum(x.size * x.dtype.itemsize for x in operands)
    return pl.pallas_call(
        kernel,
        out_shape=outs,
        in_specs=[pl.BlockSpec(memory_space=place) for place in places],
        out_specs=[VMEM] * len(outs),
        scratch_shapes=list(scratch),
        compiler_params=pltpu.CompilerParams(vmem_limit_bytes=vmem),
        cost_estimate=pl.CostEstimate(flops=flops, bytes_accessed=moved, transcendentals=0),
    )(*[pltpu.with_memory_space_constraint(x, place) for x, place in zip(operands, places)])


def load_kernel(source, target, sems):
    block = source.shape[0] // sems.shape[0]
    copies = []
    for i in range(sems.shape[0]):
        part = pl.ds(i * block, block)
        copies.append(pltpu.make_async_copy(source.at[part], target.at[part], sems.at[i]))
    for copy in copies:
        copy.start()
    for copy in copies:
        copy.wait()


def resident(head):
    return call(
        load_kernel, [(head.shape, head.dtype)], [head],
        scratch=[pltpu.SemaphoreType.DMA((4,))], sources=[pltpu.HBM],
    )[0]


TILE = 512


def first_kernel(rows_ref, near_ref, out_ref):
    depth = rows_ref.shape[1]

    @pl.loop(0, out_ref.shape[1] // TILE)
    def _(i):
        part = pl.ds(pl.multiple_of(i * TILE, TILE), TILE)
        out_ref[:, part] = jnp.dot(
            rows_ref[...], near_ref[:depth, part], preferred_element_type=jnp.float32
        )


def xor_blocks(value, own):
    me = lax.axis_index(AXIS)
    lane = lax.broadcasted_iota(jnp.int32, value.shape, 1)
    size = value.shape[1]
    group, bit = size // 2, 1
    while group >= own:
        up, down = pltpu.roll(value, group, 1), pltpu.roll(value, size - group, 1)
        swapped = jnp.where((lane & group) != 0, up, down)
        value = jnp.where((me & bit) != 0, swapped, value)
        group, bit = group // 2, bit * 2
    return value


def second_kernel(own, rows_ref, before_ref, digits_ref, near_ref,
                  logits_ref, both_ref, mine_ref, shared_ref, columns_ref):
    rows, depth = rows_ref.shape
    width = logits_ref.shape[1]
    first = near_ref.shape[0] - depth

    @pl.loop(0, width // TILE)
    def _(i):
        part = pl.ds(pl.multiple_of(i * TILE, TILE), TILE)
        logits_ref[:, part] = before_ref[:, part] + jnp.dot(
            rows_ref[...], near_ref[first:, part], preferred_element_type=jnp.float32
        )

    chunk = 32
    offset = lax.axis_index(AXIS) * width

    @pl.loop(0, rows // chunk)
    def _(i):
        part = pl.ds(pl.multiple_of(i * chunk, chunk), chunk)
        logits = logits_ref[part, :]
        digits = digits_ref[part, :].astype(jnp.float32)
        ids = (digits[:, 0:1] * 256.0 + digits[:, 1:2]).astype(jnp.int32) - offset
        hit = lax.broadcasted_iota(jnp.int32, logits.shape, 1) == ids
        top = jnp.max(logits, axis=1, keepdims=True)
        raised = jnp.exp(logits - top)
        total = jnp.sum(raised, axis=1, keepdims=True)
        pick = jnp.sum(jnp.where(hit, logits, 0.0), axis=1, keepdims=True)
        both_ref[part, :] = jnp.where(hit, 0.0, raised).astype(jnp.bfloat16)
        other = pl.ds(pl.multiple_of(rows + i * chunk, chunk), chunk)
        both_ref[other, :] = jnp.where(hit, 1.0, 0.0).astype(jnp.bfloat16)
        place = lax.broadcasted_iota(jnp.int32, (chunk, LANES), 1)
        columns_ref[part, :] = jnp.where(place == 0, top, jnp.where(place == 1, total, pick))

    mine = columns_ref[...].T[:8]
    mine_ref[...] = mine
    shared_ref[...] = xor_blocks(mine, own)


def grad_kernel(both_ref, near_ref, terms_ref):
    tile = 1024

    @pl.loop(0, near_ref.shape[0] // tile)
    def _(i):
        part = pl.ds(pl.multiple_of(i * tile, tile), tile)
        turned = lax.dot_general(
            near_ref[part, :], both_ref[...], (((1,), (1,)), ((), ())),
            preferred_element_type=jnp.float32,
        )
        terms_ref[:, part] = turned.T


def join_kernel(own, scale, seen_ref, mine_ref, terms_ref,
                left_send_ref, right_send_ref, left_ref, right_ref, lines_ref, loss_ref):
    rows = mine_ref.shape[1]
    half = terms_ref.shape[1] // 2
    seen = seen_ref[...]
    top = jnp.max(seen[:, 0], axis=0, keepdims=True)
    total = jnp.sum(seen[:, 1] * jnp.exp(seen[:, 0] - top), axis=0, keepdims=True)
    picked = jnp.sum(seen[:, 2], axis=0, keepdims=True)
    loss = jnp.sum(top + jnp.log(total) - picked, axis=1, keepdims=True) / rows
    loss_ref[...] = jnp.broadcast_to(loss, loss_ref.shape)

    place = lax.broadcasted_iota(jnp.int32, (8, rows), 0)
    lines = xor_blocks(jnp.where(place == 0, top, total), own)
    lines_ref[...] = lines
    top, total = lines[0:1], lines[1:2]
    soft = jnp.exp(mine_ref[0:1, :] - top) / (total * rows)
    hard = (jnp.exp(mine_ref[2:3, :] - top) / total - 1.0) / rows
    hard = hard.astype(jnp.bfloat16).astype(jnp.float32)
    soft = jnp.broadcast_to(soft, (LANES, rows)).T[:, 0:1]
    hard = jnp.broadcast_to(hard, (LANES, rows)).T[:, 0:1]

    def joined(first, count, columns):
        part, other = pl.ds(first, count), pl.ds(rows + first, count)
        return (
            soft[first : first + count] * terms_ref[part, columns]
            + hard[first : first + count] * terms_ref[other, columns]
        )

    quarter = rows // 4
    for cut in range(4):
        first = cut * quarter
        value = joined(first, quarter, pl.ds(0, half))
        if cut >= 2:
            left_send_ref[pl.ds(first - 2 * quarter, quarter), :] = value * scale
        else:
            left_ref[pl.ds(first, quarter), :] = value
        value = joined(first, quarter, pl.ds(half, half))
        slot = pl.ds((cut // 2) * quarter, quarter)
        if cut % 2:
            right_send_ref[slot, :] = value * scale
        else:
            right_ref[slot, :] = value


def swap(value, step):
    return lax.ppermute(value, AXIS, [(i, i ^ step) for i in range(lax.axis_size(AXIS))])


def doubled(value, step):
    return jnp.concatenate([value, swap(value, step)], axis=0)


def far_steps():
    step = lax.axis_size(AXIS) // 2
    steps = []
    while step > 2:
        steps.append(step)
        step //= 2
    return steps


def gather_rows(hidden, digits):
    half = hidden.shape[1] // 2
    for step in far_steps():
        hidden, digits = doubled(hidden, step), doubled(digits, step)
    left = jnp.concatenate([hidden[:, :half], digits], axis=1)
    right = hidden[:, half:]
    near = right.shape[0]
    left = doubled(left, 2)
    right = doubled(right, 1)
    left = doubled(left, 1)
    other = swap(right, 2)
    right = jnp.concatenate([right[:near], other[:near], right[near:], other[near:]], axis=0)
    return left[:, :half], right, left[:, half:]


def scatter_sums(left_send, right_send, left, right, scale):
    quarter = left.shape[0] // 2

    def code(value):
        return (value * scale).astype(SEND)

    def decode(value):
        return value.astype(jnp.float32) * (1.0 / scale)

    left = left + decode(swap(left_send.astype(SEND), 1))
    right = right + decode(swap(right_send.astype(SEND), 2))
    left = left[:quarter] + decode(swap(code(left[quarter:]), 2))
    right = right[:quarter] + decode(swap(code(right[quarter:]), 1))
    both = jnp.concatenate([left, right], axis=1)
    for step in far_steps()[::-1]:
        keep = both.shape[0] // 2
        both = both[:keep] + decode(swap(code(both[keep:]), step))
    return both


def body(hidden, targets, head, global_frag, momentum, peer_delta):
    members = lax.axis_size(AXIS)
    own, depth = hidden.shape
    half = depth // 2
    rows = own * members
    width = head.shape[1]

    digits = jnp.stack([targets // 256, targets % 256], axis=1).astype(jnp.bfloat16)
    digits = jnp.pad(digits, ((0, 0), (0, 126)))
    left, right, digits = gather_rows(hidden, digits)

    near = resident(head)
    work = 2 * rows * half * width
    logits = call(first_kernel, [((rows, width), jnp.float32)], [left, near], work)[0]
    logits, both, mine, shared = call(
        functools.partial(second_kernel, own),
        [((rows, width), jnp.float32), ((2 * rows, width), jnp.bfloat16),
         ((8, rows), jnp.float32), ((8, rows), jnp.float32)],
        [right, logits, digits, near], work,
        scratch=[pltpu.VMEM((rows, LANES), jnp.float32)],
    )

    seen = lax.all_to_all(
        jnp.broadcast_to(shared[None], (members,) + shared.shape), AXIS, split_axis=0, concat_axis=0
    )

    terms = call(grad_kernel, [((2 * rows, depth), jnp.float32)], [both, near], 8 * work)[0]

    scale = 2.0**14 * rows
    cut = (rows // 2, half)
    left_send, right_send, left_keep, right_keep, lines, loss = call(
        functools.partial(join_kernel, own, scale),
        [(cut, jnp.float32)] * 4
        + [((8, rows), jnp.float32), ((8, LANES), jnp.float32)],
        [seen, mine, terms],
    )
    hidden_grad = scatter_sums(left_send, right_send, left_keep, right_keep, scale).astype(jnp.bfloat16)
    loss = loss[0, :1]

    top, total = lines[0], lines[1]
    digits = digits[:, :2].astype(jnp.int32)
    ids_all = digits[:, 0] * 256 + digits[:, 1]
    columns = lax.axis_index(AXIS) * width + jnp.arange(width, dtype=jnp.int32)
    onehot = (columns[None, :] == ids_all[:, None]).astype(jnp.float32)
    dlogits = ((jnp.exp(logits - top[:, None]) / total[:, None] - onehot) / rows).astype(jnp.bfloat16)
    frag_grad = lax.dot_general(
        left[:, :FRAG], dlogits, (((0,), (0,)), ((), ())), preferred_element_type=jnp.float32
    )
    local_frag = head[:FRAG].astype(jnp.float32) - 1.0 * frag_grad
    pseudo = (global_frag - local_frag + peer_delta) / REPLICAS
    new_momentum = 0.9 * momentum + pseudo
    new_global = global_frag - 0.7 * (pseudo + 0.9 * new_momentum)
    return (loss, hidden_grad, new_global, new_momentum)


def solution(mesh):
    in_specs = (
        P(("outer", "vocab"), None),
        P(("outer", "vocab")),
        P("outer", "vocab"),
        P(None, "vocab"),
        P(None, "vocab"),
        P("outer", "vocab"),
    )
    out_specs = (P("outer"), P(("outer", "vocab"), None), P("outer", "vocab"), P("outer", "vocab"))
    return jax.shard_map(body, mesh=mesh, in_specs=in_specs, out_specs=out_specs, check_vma=False)
```

```python
import functools

import jax
import jax.numpy as jnp
from jax import lax
from jax.experimental import pallas as pl
from jax.experimental.pallas import tpu as pltpu
from jax.sharding import PartitionSpec as P

FRAG = 128
REPLICAS = 4
AXIS = "vocab"
SEND = jnp.float16
LANES = 128
VMEM = pl.BlockSpec(memory_space=pltpu.VMEM)


def call(kernel, outs, operands, flops=0, scratch=(), sources=None, vmem=16 * 2**20):
    outs = [pltpu.VMEM(shape, dtype) for shape, dtype in outs]
    places = sources or [pltpu.VMEM] * len(operands)
    moved = sum(x.size * x.dtype.itemsize for x in operands)
    return pl.pallas_call(
        kernel,
        out_shape=outs,
        in_specs=[pl.BlockSpec(memory_space=place) for place in places],
        out_specs=[VMEM] * len(outs),
        scratch_shapes=list(scratch),
        compiler_params=pltpu.CompilerParams(vmem_limit_bytes=vmem),
        cost_estimate=pl.CostEstimate(flops=flops, bytes_accessed=moved, transcendentals=0),
    )(*[pltpu.with_memory_space_constraint(x, place) for x, place in zip(operands, places)])


def load_kernel(source, target, sems):
    block = source.shape[0] // sems.shape[0]
    copies = []
    for i in range(sems.shape[0]):
        part = pl.ds(i * block, block)
        copies.append(pltpu.make_async_copy(source.at[part], target.at[part], sems.at[i]))
    for copy in copies:
        copy.start()
    for copy in copies:
        copy.wait()


def resident(head):
    return call(
        load_kernel, [(head.shape, head.dtype)], [head],
        scratch=[pltpu.SemaphoreType.DMA((4,))], sources=[pltpu.HBM],
    )[0]


TILE = 512


def first_kernel(rows_ref, near_ref, out_ref):
    depth = rows_ref.shape[1]

    @pl.loop(0, out_ref.shape[1] // TILE)
    def _(i):
        part = pl.ds(pl.multiple_of(i * TILE, TILE), TILE)
        out_ref[:, part] = jnp.dot(
            rows_ref[...], near_ref[:depth, part], preferred_element_type=jnp.float32
        )


def ids_of(digits):
    digits = digits.astype(jnp.float32)
    return (digits[:, 0:1] * 256.0 + digits[:, 1:2]).astype(jnp.int32)


def block_group(step, size):
    return size // (2 * step)


def swap_blocks(value, group):
    size = value.shape[1]
    lane = lax.broadcasted_iota(jnp.int32, value.shape, 1)
    up, down = pltpu.roll(value, group, 1), pltpu.roll(value, size - group, 1)
    return jnp.where((lane & group) != 0, up, down)


def shared_order(value, members):
    me = lax.axis_index(AXIS)
    step = 1
    while step < members:
        swapped = swap_blocks(value, block_group(step, value.shape[1]))
        value = jnp.where((me & step) != 0, swapped, value)
        step *= 2
    return value


def as_columns(line):
    return jnp.broadcast_to(line, (LANES, line.shape[1])).T[:, 0:1]


def second_kernel(rows_ref, before_ref, near_ref, logits_ref, both_ref, mine_ref, columns_ref):
    rows = rows_ref.shape[0]
    depth = rows_ref.shape[1] - LANES
    width = logits_ref.shape[1]
    first = near_ref.shape[0] - depth

    @pl.loop(0, width // TILE)
    def _(i):
        part = pl.ds(pl.multiple_of(i * TILE, TILE), TILE)
        logits_ref[:, part] = before_ref[:, part] + jnp.dot(
            rows_ref[:, :depth], near_ref[first:, part], preferred_element_type=jnp.float32
        )

    chunk = 32
    offset = lax.axis_index(AXIS) * width

    @pl.loop(0, rows // chunk)
    def _(i):
        part = pl.ds(pl.multiple_of(i * chunk, chunk), chunk)
        logits = logits_ref[part, :]
        ids = ids_of(rows_ref[part, depth:]) - offset
        hit = lax.broadcasted_iota(jnp.int32, logits.shape, 1) == ids
        top = jnp.max(logits, axis=1, keepdims=True)
        raised = jnp.exp(logits - top)
        total = jnp.sum(raised, axis=1, keepdims=True)
        pick = jnp.sum(jnp.where(hit, logits, 0.0), axis=1, keepdims=True)
        both_ref[part, :] = jnp.where(hit, 0.0, raised).astype(jnp.bfloat16)
        other = pl.ds(pl.multiple_of(rows + i * chunk, chunk), chunk)
        both_ref[other, :] = jnp.where(hit, 1.0, 0.0).astype(jnp.bfloat16)
        place = lax.broadcasted_iota(jnp.int32, (chunk, LANES), 1)
        columns_ref[part, :] = jnp.where(place == 0, top, jnp.where(place == 1, total, pick))

    mine_ref[...] = columns_ref[...].T[:8]


def merge_kernel(step, mine_ref, other_ref, out_ref):
    size = mine_ref.shape[1]
    mine, other = mine_ref[...], swap_blocks(other_ref[...], block_group(step, size))
    upper = (lax.axis_index(AXIS) & step) != 0
    one, two = jnp.where(upper, other, mine), jnp.where(upper, mine, other)
    top = jnp.maximum(one[0:1], two[0:1])
    total = one[1:2] * jnp.exp(one[0:1] - top) + two[1:2] * jnp.exp(two[0:1] - top)
    pick = one[2:3] + two[2:3]
    place = lax.broadcasted_iota(jnp.int32, mine.shape, 0)
    out_ref[...] = jnp.where(place == 0, top, jnp.where(place == 1, total, pick))


def grad_kernel(first, both_ref, near_ref, terms_ref):
    turned = lax.dot_general(
        near_ref[pl.ds(first, terms_ref.shape[1]), :], both_ref[...], (((1,), (1,)), ((), ())),
        preferred_element_type=jnp.float32,
    )
    terms_ref[...] = turned.T


def join_kernel(members, scale, lines_ref, mine_ref, *refs):
    *terms_refs, left_send_ref, right_send_ref, left_ref, right_ref, loss_ref = refs
    rows = mine_ref.shape[1]
    lines = lines_ref[...]
    same = shared_order(lines, members)
    loss = jnp.sum(same[0:1] + jnp.log(same[1:2]) - same[2:3], axis=1, keepdims=True) / rows
    loss_ref[...] = jnp.broadcast_to(loss, loss_ref.shape)

    top, total = lines[0:1], lines[1:2]
    soft = as_columns(jnp.exp(mine_ref[0:1, :] - top) / (total * rows))
    hard = (jnp.exp(mine_ref[2:3, :] - top) / total - 1.0) / rows
    hard = as_columns(hard.astype(jnp.bfloat16).astype(jnp.float32))

    quarter = rows // 4
    for place, terms_ref in enumerate(terms_refs):
        width = terms_ref.shape[1]
        in_left = place < len(terms_refs) // 2
        columns = pl.ds(place % (len(terms_refs) // 2) * width, width)
        for cut in range(4):
            first = cut * quarter
            value = (
                soft[first : first + quarter] * terms_ref[pl.ds(first, quarter), :]
                + hard[first : first + quarter] * terms_ref[pl.ds(rows + first, quarter), :]
            )
            near, far = (cut % 2, cut // 2) if in_left else (cut // 2, cut % 2)
            slot = pl.ds(near * quarter, quarter)
            if far:
                (left_send_ref if in_left else right_send_ref)[slot, columns] = value * scale
            else:
                (left_ref if in_left else right_ref)[slot, columns] = value


def frag_kernel(rows_ref, digits_ref, lines_ref, logits_ref, head_ref, global_ref, momentum_ref,
                peer_ref, new_global_ref, new_momentum_ref):
    rows, tile = logits_ref.shape
    top, total = as_columns(lines_ref[0:1, :]), as_columns(lines_ref[1:2, :])
    offset = (lax.axis_index(AXIS) * pl.num_programs(0) + pl.program_id(0)) * tile
    hit = lax.broadcasted_iota(jnp.int32, (rows, tile), 1) == ids_of(digits_ref[...]) - offset
    shares = jnp.exp(logits_ref[...] - top) / total
    dlogits = ((shares - jnp.where(hit, 1.0, 0.0)) / rows).astype(jnp.bfloat16)
    turned = rows_ref[...].astype(jnp.float32).T.astype(jnp.bfloat16)
    frag_grad = jnp.dot(turned, dlogits, preferred_element_type=jnp.float32)
    local_frag = head_ref[...].astype(jnp.float32) - 1.0 * frag_grad
    pseudo = (global_ref[...] - local_frag + peer_ref[...]) / REPLICAS
    new_momentum = 0.9 * momentum_ref[...] + pseudo
    new_momentum_ref[...] = new_momentum
    new_global_ref[...] = global_ref[...] - 0.7 * (pseudo + 0.9 * new_momentum)


def frag_update(left, right, lines, logits, near, global_frag, momentum, peer_delta):
    rows, width = logits.shape
    last = right.shape[1] // LANES - 1
    tile = pl.BlockSpec((FRAG, TILE), lambda i: (0, i))
    return pl.pallas_call(
        frag_kernel,
        grid=(width // TILE,),
        out_shape=[jax.ShapeDtypeStruct((FRAG, width), jnp.float32)] * 2,
        in_specs=[
            pl.BlockSpec((rows, FRAG), lambda i: (0, 0)),
            pl.BlockSpec((rows, LANES), lambda i: (0, last)),
            pl.BlockSpec((8, rows), lambda i: (0, 0)),
            pl.BlockSpec((rows, TILE), lambda i: (0, i)),
            tile, tile, tile, tile,
        ],
        out_specs=[tile, tile],
        compiler_params=pltpu.CompilerParams(vmem_limit_bytes=16 * 2**20),
        cost_estimate=pl.CostEstimate(
            flops=2 * rows * FRAG * width, bytes_accessed=24 * FRAG * width, transcendentals=0
        ),
    )(
        left, right, lines, pltpu.with_memory_space_constraint(logits, pltpu.VMEM),
        pltpu.with_memory_space_constraint(near, pltpu.VMEM), global_frag, momentum, peer_delta,
    )


def swap(value, step):
    return lax.ppermute(value, AXIS, [(i, i ^ step) for i in range(lax.axis_size(AXIS))])


def doubled(value, step):
    return jnp.concatenate([value, swap(value, step)], axis=0)


def far_steps():
    step = lax.axis_size(AXIS) // 2
    steps = []
    while step > 2:
        steps.append(step)
        step //= 2
    return steps


def gather_rows(hidden, digits):
    half = hidden.shape[1] // 2
    for step in far_steps():
        hidden, digits = doubled(hidden, step), doubled(digits, step)
    left = doubled(doubled(hidden[:, :half], 2), 1)
    right = doubled(jnp.concatenate([hidden[:, half:], digits], axis=1), 1)
    near = right.shape[0] // 2
    other = swap(right, 2)
    right = jnp.concatenate([right[:near], other[:near], right[near:], other[near:]], axis=0)
    return left, right


def scatter_sums(left_send, right_send, left, right, scale):
    quarter = left.shape[0] // 2

    def code(value):
        return (value * scale).astype(SEND)

    def decode(value):
        return value.astype(jnp.float32) * (1.0 / scale)

    left = left + decode(swap(left_send.astype(SEND), 1))
    right = right + decode(swap(right_send.astype(SEND), 2))
    left = left[:quarter] + decode(swap(code(left[quarter:]), 2))
    right = right[:quarter] + decode(swap(code(right[quarter:]), 1))
    both = jnp.concatenate([left, right], axis=1)
    for step in far_steps()[::-1]:
        keep = both.shape[0] // 2
        both = both[:keep] + decode(swap(code(both[keep:]), step))
    return both


def body(hidden, targets, head, global_frag, momentum, peer_delta):
    members = lax.axis_size(AXIS)
    own, depth = hidden.shape
    half = depth // 2
    rows = own * members
    width = head.shape[1]

    digits = jnp.stack([targets // 256, targets % 256], axis=1).astype(jnp.bfloat16)
    digits = jnp.pad(digits, ((0, 0), (0, 126)))
    left, right = gather_rows(hidden, digits)

    near = resident(head)
    work = 2 * rows * half * width
    logits = call(first_kernel, [((rows, width), jnp.float32)], [left, near], work)[0]
    logits, both, mine = call(
        second_kernel,
        [((rows, width), jnp.float32), ((2 * rows, width), jnp.bfloat16), ((8, rows), jnp.float32)],
        [right, logits, near], work,
        scratch=[pltpu.VMEM((rows, LANES), jnp.float32)],
    )

    lines = mine
    for step in far_steps() + [2, 1]:
        lines = call(
            functools.partial(merge_kernel, step), [((8, rows), jnp.float32)], [lines, swap(lines, step)]
        )[0]

    cuts = 4
    terms = [
        call(
            functools.partial(grad_kernel, i * depth // cuts),
            [((2 * rows, depth // cuts), jnp.float32)], [both, near], 8 * work // cuts,
        )[0]
        for i in range(cuts)
    ]

    scale = 2.0**14 * rows
    *parts, loss = call(
        functools.partial(join_kernel, members, scale),
        [((rows // 2, half), jnp.float32)] * 4 + [((8, LANES), jnp.float32)],
        [lines, mine] + terms,
    )
    hidden_grad = scatter_sums(*parts, scale).astype(jnp.bfloat16)
    new_global, new_momentum = frag_update(
        left, right, lines, logits, near, global_frag, momentum, peer_delta
    )
    return (loss[0, :1], hidden_grad, new_global, new_momentum)


def solution(mesh):
    in_specs = (
        P(("outer", "vocab"), None),
        P(("outer", "vocab")),
        P("outer", "vocab"),
        P(None, "vocab"),
        P(None, "vocab"),
        P("outer", "vocab"),
    )
    out_specs = (P("outer"), P(("outer", "vocab"), None), P("outer", "vocab"), P("outer", "vocab"))
    return jax.shard_map(body, mesh=mesh, in_specs=in_specs, out_specs=out_specs, check_vma=False)
```

```python
import functools

import jax
import jax.numpy as jnp
from jax import lax
from jax.experimental import pallas as pl
from jax.experimental.pallas import tpu as pltpu
from jax.sharding import PartitionSpec as P

FRAG = 128
REPLICAS = 4
AXIS = "vocab"
SEND = jnp.float16
LANES = 128
VMEM = pl.BlockSpec(memory_space=pltpu.VMEM)


def call(kernel, outs, operands, flops=0, scratch=(), sources=None, vmem=16 * 2**20):
    outs = [pltpu.VMEM(shape, dtype) for shape, dtype in outs]
    places = sources or [pltpu.VMEM] * len(operands)
    moved = sum(x.size * x.dtype.itemsize for x in operands)
    return pl.pallas_call(
        kernel,
        out_shape=outs,
        in_specs=[pl.BlockSpec(memory_space=place) for place in places],
        out_specs=[VMEM] * len(outs),
        scratch_shapes=list(scratch),
        compiler_params=pltpu.CompilerParams(vmem_limit_bytes=vmem),
        cost_estimate=pl.CostEstimate(flops=flops, bytes_accessed=moved, transcendentals=0),
    )(*[pltpu.with_memory_space_constraint(x, place) for x, place in zip(operands, places)])


def load_kernel(source, target, token_ref, sems):
    block = source.shape[0] // sems.shape[0]
    copies = []
    for i in range(sems.shape[0]):
        part = pl.ds(i * block, block)
        copies.append(pltpu.make_async_copy(source.at[part], target.at[part], sems.at[i]))
    for copy in copies:
        copy.start()
    for copy in copies:
        copy.wait()
    token_ref[...] = jnp.zeros_like(token_ref)


def resident(head):
    return call(
        load_kernel, [(head.shape, head.dtype), ((8, LANES), jnp.float32)], [head],
        scratch=[pltpu.SemaphoreType.DMA((4,))], sources=[pltpu.HBM],
    )


TILE = 512


def pack_kernel(targets_ref, rows_ref, out_ref):
    own, depth = rows_ref.shape
    place = lax.broadcasted_iota(jnp.int32, (own, LANES), 0)
    ids = jnp.zeros((own, LANES), jnp.int32)
    for i in range(own):
        ids = jnp.where(place == i, targets_ref[i], ids)
    lane = lax.broadcasted_iota(jnp.int32, (own, LANES), 1)
    digits = jnp.where(lane == 0, ids // 256, ids % 256)
    out_ref[:, :depth] = rows_ref[...]
    out_ref[:, depth:] = digits.astype(jnp.float32).astype(jnp.bfloat16)


def ids_of(digits):
    digits = digits.astype(jnp.float32)
    return (digits[:, 0:1] * 256.0 + digits[:, 1:2]).astype(jnp.int32)


def swap_blocks(value, group):
    size = value.shape[1]
    lane = lax.broadcasted_iota(jnp.int32, value.shape, 1)
    up, down = pltpu.roll(value, group, 1), pltpu.roll(value, size - group, 1)
    return jnp.where((lane & group) != 0, up, down)


def shared_order(value, members):
    me = lax.axis_index(AXIS)
    step = 1
    while step < members:
        swapped = swap_blocks(value, value.shape[1] // members * step)
        value = jnp.where((me & step) != 0, swapped, value)
        step *= 2
    return value


def as_columns(line):
    return jnp.broadcast_to(line, (LANES, line.shape[1])).T[:, 0:1]


def rows_kernel(rows_ref, near_ref, *refs):
    before_ref, (logits_ref, both_ref, stats_ref) = (None, refs) if len(refs) == 3 else (refs[0], refs[1:4])
    rows = rows_ref.shape[0]
    depth, width = near_ref.shape

    @pl.loop(0, width // TILE)
    def _(i):
        part = pl.ds(pl.multiple_of(i * TILE, TILE), TILE)
        logits_ref[:, part] = jnp.dot(
            rows_ref[:, :depth], near_ref[:, part], preferred_element_type=jnp.float32
        )

    chunk = 32
    offset = lax.axis_index(AXIS) * width
    columns_ref = stats_ref if before_ref is None else refs[4]
    first = 0 if before_ref is None else before_ref.shape[0]

    @pl.loop(0, rows // chunk)
    def _(i):
        part = pl.ds(pl.multiple_of(i * chunk, chunk), chunk)
        logits = logits_ref[part, :]
        ids = ids_of(rows_ref[part, depth:]) - offset
        hit = lax.broadcasted_iota(jnp.int32, logits.shape, 1) == ids
        top = jnp.max(logits, axis=1, keepdims=True)
        raised = jnp.exp(logits - top)
        total = jnp.sum(raised, axis=1, keepdims=True)
        pick = jnp.sum(jnp.where(hit, logits, 0.0), axis=1, keepdims=True)
        both_ref[part, :] = jnp.where(hit, 0.0, raised).astype(jnp.bfloat16)
        other = pl.ds(pl.multiple_of(rows + i * chunk, chunk), chunk)
        both_ref[other, :] = jnp.where(hit, 1.0, 0.0).astype(jnp.bfloat16)
        place = lax.broadcasted_iota(jnp.int32, (chunk, LANES), 1)
        slot = pl.ds(pl.multiple_of(first + i * chunk, chunk), chunk)
        columns_ref[slot, :] = jnp.where(place == 0, top, jnp.where(place == 1, total, pick))

    if before_ref is not None:
        columns_ref[pl.ds(0, first), :] = before_ref[...]
        stats_ref[...] = columns_ref[...].T[:8]


def merge_kernel(step, members, mine_ref, other_ref, out_ref):
    mine = mine_ref[...]
    other = swap_blocks(other_ref[...], mine.shape[1] // members * step)
    upper = (lax.axis_index(AXIS) & step) != 0
    one, two = jnp.where(upper, other, mine), jnp.where(upper, mine, other)
    top = jnp.maximum(one[0:1], two[0:1])
    total = one[1:2] * jnp.exp(one[0:1] - top) + two[1:2] * jnp.exp(two[0:1] - top)
    pick = one[2:3] + two[2:3]
    place = lax.broadcasted_iota(jnp.int32, mine.shape, 0)
    out_ref[...] = jnp.where(place == 0, top, jnp.where(place == 1, total, pick))


def grad_kernel(first, one_ref, two_ref, near_ref, terms_ref):
    both = jnp.concatenate([one_ref[...], two_ref[...]], axis=0)
    turned = lax.dot_general(
        near_ref[pl.ds(first, terms_ref.shape[1]), :], both, (((1,), (1,)), ((), ())),
        preferred_element_type=jnp.float32,
    )
    terms_ref[...] = turned.T


def join_kernel(members, scale, lines_ref, mine_ref, *refs):
    *terms_refs, out_ref, loss_ref = refs
    rows = mine_ref.shape[1]
    lines = lines_ref[...]
    same = shared_order(lines, members)
    loss = jnp.sum(same[0:1] + jnp.log(same[1:2]) - same[2:3], axis=1, keepdims=True) / rows
    loss_ref[...] = jnp.broadcast_to(loss, loss_ref.shape)

    top, total = lines[0:1], lines[1:2]
    soft = as_columns(jnp.exp(mine_ref[0:1, :] - top) / (total * rows)) * scale
    hard = (jnp.exp(mine_ref[2:3, :] - top) / total - 1.0) / rows
    hard = as_columns(hard.astype(jnp.bfloat16).astype(jnp.float32)) * scale

    near = rows // members * 4
    chunk = min(near, rows - near, 64)
    for place, terms_ref in enumerate(terms_refs):
        columns = pl.ds(place * terms_ref.shape[1], terms_ref.shape[1])
        for first in range(0, rows, chunk):
            at, other = (first, near) if first < near else (near + first, rows - near)
            out_ref[pl.ds(first, chunk), columns] = (
                soft[first : first + chunk] * terms_ref[pl.ds(at, chunk), :]
                + hard[first : first + chunk] * terms_ref[pl.ds(at + other, chunk), :]
            )


def frag_kernel(rows_ref, digits_ref, lines_ref, one_ref, two_ref, head_ref, global_ref, momentum_ref,
                peer_ref, new_global_ref, new_momentum_ref):
    logits = jnp.concatenate([one_ref[...], two_ref[...]], axis=0)
    rows, tile = logits.shape
    top, total = as_columns(lines_ref[0:1, :]), as_columns(lines_ref[1:2, :])
    offset = (lax.axis_index(AXIS) * pl.num_programs(0) + pl.program_id(0)) * tile
    hit = lax.broadcasted_iota(jnp.int32, (rows, tile), 1) == ids_of(digits_ref[...]) - offset
    shares = jnp.exp(logits - top) / total
    dlogits = ((shares - jnp.where(hit, 1.0, 0.0)) / rows).astype(jnp.bfloat16)
    turned = rows_ref[...].astype(jnp.float32).T.astype(jnp.bfloat16)
    frag_grad = jnp.dot(turned, dlogits, preferred_element_type=jnp.float32)
    local_frag = head_ref[...].astype(jnp.float32) - 1.0 * frag_grad
    pseudo = (global_ref[...] - local_frag + peer_ref[...]) / REPLICAS
    new_momentum = 0.9 * momentum_ref[...] + pseudo
    new_momentum_ref[...] = new_momentum
    new_global_ref[...] = global_ref[...] - 0.7 * (pseudo + 0.9 * new_momentum)


def frag_update(rows_all, lines, logits, near, global_frag, momentum, peer_delta):
    rows = rows_all.shape[0]
    width = near.shape[1]
    last = rows_all.shape[1] // LANES - 1
    tile = pl.BlockSpec((FRAG, TILE), lambda i: (0, i))
    return pl.pallas_call(
        frag_kernel,
        grid=(width // TILE,),
        out_shape=[jax.ShapeDtypeStruct((FRAG, width), jnp.float32)] * 2,
        in_specs=[
            pl.BlockSpec((rows, FRAG), lambda i: (0, 0)),
            pl.BlockSpec((rows, LANES), lambda i: (0, last)),
            pl.BlockSpec((8, rows), lambda i: (0, 0)),
        ]
        + [pl.BlockSpec((x.shape[0], TILE), lambda i: (0, i)) for x in logits]
        + [tile] * 4,
        out_specs=[tile, tile],
        compiler_params=pltpu.CompilerParams(vmem_limit_bytes=16 * 2**20),
        cost_estimate=pl.CostEstimate(
            flops=2 * rows * FRAG * width, bytes_accessed=24 * FRAG * width, transcendentals=0
        ),
    )(
        rows_all, rows_all, lines,
        *[pltpu.with_memory_space_constraint(x, pltpu.VMEM) for x in logits],
        pltpu.with_memory_space_constraint(near, pltpu.VMEM), global_frag, momentum, peer_delta,
    )


def swap(value, step):
    return lax.ppermute(value, AXIS, [(i, i ^ step) for i in range(lax.axis_size(AXIS))])


def far_steps():
    step = 4
    steps = []
    while step < lax.axis_size(AXIS):
        steps.append(step)
        step *= 2
    return steps


def gather_rows(packed, token):
    own = packed.shape[0]
    held = packed
    for step in far_steps()[:1]:
        held = jnp.concatenate([held, swap(held, step)], axis=0)
    packed, _ = lax.optimization_barrier((packed, token))
    near = [packed] + [swap(packed, step) for step in (3, 2, 1)][::-1]
    for step in far_steps()[1:]:
        held = jnp.concatenate([held, swap(held, step)], axis=0)
    far = held[own:]
    far = jnp.stack([far] + [swap(far, step) for step in (3, 2, 1)][::-1])
    count = far.shape[1] // own
    far = far.reshape(4, count, own, -1).swapaxes(0, 1).reshape(4 * count * own, -1)
    return jnp.concatenate(near, axis=0), far


def scatter_sums(grads, own):
    members = grads.shape[0] // own
    blocks = [grads[i * own : (i + 1) * own] for i in range(members)]

    def moved(parts, step):
        value = jnp.concatenate([part.astype(SEND) for part in parts], axis=0)
        value = swap(value, step).astype(jnp.float32)
        return [value[i * own : (i + 1) * own] for i in range(len(parts))]

    sums = blocks[::4]
    for part in (list(range(1, members // 4)), [0]):
        for step in (3, 2, 1):
            for i, value in zip(part, moved([blocks[4 * i + step] for i in part], step)):
                sums[i] = sums[i] + value
    for step in far_steps()[::-1]:
        keep = len(sums) // 2
        sums = [a + b for a, b in zip(sums[:keep], moved(sums[keep:], step))]
    return sums[0]


def body(hidden, targets, head, global_frag, momentum, peer_delta):
    members = lax.axis_size(AXIS)
    own, depth = hidden.shape
    rows = own * members
    width = head.shape[1]

    packed = call(
        pack_kernel, [((own, depth + LANES), hidden.dtype)], [targets, hidden],
        sources=[pltpu.SMEM, pltpu.VMEM],
    )[0]
    near, token = resident(head)
    rows_near, rows_far = gather_rows(packed, token)

    def part(held, *before):
        count = held.shape[0]
        stats = (8, rows) if before else (count, LANES)
        return call(
            rows_kernel,
            [((count, width), jnp.float32), ((2 * count, width), jnp.bfloat16), (stats, jnp.float32)],
            [held, near, *before], 2 * count * depth * width,
            scratch=[pltpu.VMEM((rows, LANES), jnp.float32)] if before else [],
        )

    logits_near, both_near, columns = part(rows_near)
    logits_far, both_far, mine = part(rows_far, columns)

    lines = mine
    for step in far_steps()[::-1] + [2, 1]:
        lines = call(
            functools.partial(merge_kernel, step, members),
            [((8, rows), jnp.float32)], [lines, swap(lines, step)],
        )[0]

    cuts = 4
    terms = [
        call(
            functools.partial(grad_kernel, i * depth // cuts),
            [((2 * rows, depth // cuts), jnp.float32)], [both_near, both_far, near],
            4 * rows * depth * width // cuts,
        )[0]
        for i in range(cuts)
    ]

    scale = 2.0**14 * rows
    grads, loss = call(
        functools.partial(join_kernel, members, scale),
        [((rows, depth), jnp.float32), ((8, LANES), jnp.float32)],
        [lines, mine] + terms,
    )
    hidden_grad = (scatter_sums(grads, own) * (1.0 / scale)).astype(jnp.bfloat16)
    new_global, new_momentum = frag_update(
        jnp.concatenate([rows_near, rows_far], axis=0), lines, [logits_near, logits_far], near,
        global_frag, momentum, peer_delta,
    )
    return (loss[0, :1], hidden_grad, new_global, new_momentum)


def solution(mesh):
    in_specs = (
        P(("outer", "vocab"), None),
        P(("outer", "vocab")),
        P("outer", "vocab"),
        P(None, "vocab"),
        P(None, "vocab"),
        P("outer", "vocab"),
    )
    out_specs = (P("outer"), P(("outer", "vocab"), None), P("outer", "vocab"), P("outer", "vocab"))
    return jax.shard_map(body, mesh=mesh, in_specs=in_specs, out_specs=out_specs, check_vma=False)
```

```python
import functools

import jax
import jax.numpy as jnp
from jax import lax
from jax.experimental import pallas as pl
from jax.experimental.pallas import tpu as pltpu
from jax.sharding import PartitionSpec as P

FRAG = 128
REPLICAS = 4
AXIS = "vocab"
SEND = jnp.float16
LANES = 128
VMEM = pl.BlockSpec(memory_space=pltpu.VMEM)


def call(kernel, outs, operands, flops=0, scratch=(), sources=None, vmem=16 * 2**20):
    outs = [pltpu.VMEM(shape, dtype) for shape, dtype in outs]
    places = sources or [pltpu.VMEM] * len(operands)
    moved = sum(x.size * x.dtype.itemsize for x in operands)
    return pl.pallas_call(
        kernel,
        out_shape=outs,
        in_specs=[pl.BlockSpec(memory_space=place) for place in places],
        out_specs=[VMEM] * len(outs),
        scratch_shapes=list(scratch),
        compiler_params=pltpu.CompilerParams(vmem_limit_bytes=vmem),
        cost_estimate=pl.CostEstimate(flops=flops, bytes_accessed=moved, transcendentals=0),
    )(*[pltpu.with_memory_space_constraint(x, place) for x, place in zip(operands, places)])


def load_kernel(source, target, sems):
    block = source.shape[0] // sems.shape[0]
    copies = []
    for i in range(sems.shape[0]):
        part = pl.ds(i * block, block)
        copies.append(pltpu.make_async_copy(source.at[part], target.at[part], sems.at[i]))
    for copy in copies:
        copy.start()
    for copy in copies:
        copy.wait()


def resident(head):
    return call(
        load_kernel, [(head.shape, head.dtype)], [head],
        scratch=[pltpu.SemaphoreType.DMA((4,))], sources=[pltpu.HBM],
    )[0]


TILE = 512
WIDE = 1024


def pack_kernel(targets, rows, out_ref, targets_ref, sems):
    own, depth = rows.shape
    ids_copy = pltpu.make_async_copy(targets, targets_ref, sems.at[0])
    rows_copy = pltpu.make_async_copy(rows, out_ref.at[:, pl.ds(0, depth)], sems.at[1])
    ids_copy.start()
    rows_copy.start()
    ids_copy.wait()
    place = lax.broadcasted_iota(jnp.int32, (own, LANES), 0)
    ids = jnp.zeros((own, LANES), jnp.int32)
    for i in range(own):
        ids = jnp.where(place == i, targets_ref[i], ids)
    lane = lax.broadcasted_iota(jnp.int32, (own, LANES), 1)
    digits = jnp.where(lane == 0, ids // 256, ids % 256)
    out_ref[:, depth:] = digits.astype(jnp.float32).astype(jnp.bfloat16)
    rows_copy.wait()


def ids_of(digits):
    digits = digits.astype(jnp.float32)
    return (digits[:, 0:1] * 256.0 + digits[:, 1:2]).astype(jnp.int32)


def swap_blocks(value, group):
    size = value.shape[1]
    lane = lax.broadcasted_iota(jnp.int32, value.shape, 1)
    up, down = pltpu.roll(value, group, 1), pltpu.roll(value, size - group, 1)
    return jnp.where((lane & group) != 0, up, down)


def shared_order(value, members):
    me = lax.axis_index(AXIS)
    step = 1
    while step < members:
        swapped = swap_blocks(value, value.shape[1] // members * step)
        value = jnp.where((me & step) != 0, swapped, value)
        step *= 2
    return value


def as_columns(line):
    return jnp.broadcast_to(line, (LANES, line.shape[1])).T[:, 0:1]


def rows_kernel(rows_ref, near_ref, *refs):
    before_ref, (logits_ref, both_ref, stats_ref) = (None, refs) if len(refs) == 3 else (refs[0], refs[1:4])
    rows = rows_ref.shape[0]
    depth, width = near_ref.shape

    @pl.loop(0, width // WIDE)
    def _(i):
        part = pl.ds(pl.multiple_of(i * WIDE, WIDE), WIDE)
        logits_ref[:, part] = jnp.dot(
            rows_ref[:, :depth], near_ref[:, part], preferred_element_type=jnp.float32
        )

    chunk = 32
    offset = lax.axis_index(AXIS) * width
    columns_ref = stats_ref if before_ref is None else refs[4]
    first = 0 if before_ref is None else before_ref.shape[0]

    @pl.loop(0, rows // chunk)
    def _(i):
        part = pl.ds(pl.multiple_of(i * chunk, chunk), chunk)
        logits = logits_ref[part, :]
        ids = ids_of(rows_ref[part, depth:]) - offset
        hit = lax.broadcasted_iota(jnp.int32, logits.shape, 1) == ids
        top = jnp.max(logits, axis=1, keepdims=True)
        raised = jnp.exp(logits - top)
        total = jnp.sum(raised, axis=1, keepdims=True)
        pick = jnp.sum(jnp.where(hit, logits, 0.0), axis=1, keepdims=True)
        both_ref[part, :] = jnp.where(hit, 0.0, raised).astype(jnp.bfloat16)
        other = pl.ds(pl.multiple_of(rows + i * chunk, chunk), chunk)
        both_ref[other, :] = jnp.where(hit, 1.0, 0.0).astype(jnp.bfloat16)
        place = lax.broadcasted_iota(jnp.int32, (chunk, LANES), 1)
        slot = pl.ds(pl.multiple_of(first + i * chunk, chunk), chunk)
        columns_ref[slot, :] = jnp.where(place == 0, top, jnp.where(place == 1, total, pick))

    if before_ref is not None:
        columns_ref[pl.ds(0, first), :] = before_ref[...]
        stats_ref[...] = columns_ref[...].T[:8]


def merge_kernel(steps, members, mine_ref, *refs):
    *other_refs, out_ref = refs
    block = mine_ref.shape[1] // members
    me = lax.axis_index(AXIS)
    groups = [mine_ref[...]]
    for step, other_ref in zip(steps, other_refs):
        other, bit = other_ref[...], 1
        while bit <= step:
            if step & bit:
                other = swap_blocks(other, block * bit)
            bit *= 2
        groups.append(other)
    unit, bit = steps[0], 1
    while bit < len(groups):
        upper = (me & (unit * bit)) != 0
        groups = [jnp.where(upper, groups[i ^ bit], group) for i, group in enumerate(groups)]
        bit *= 2
    top = functools.reduce(jnp.maximum, [group[0:1] for group in groups])
    total = sum(group[1:2] * jnp.exp(group[0:1] - top) for group in groups)
    pick = sum(group[2:3] for group in groups)
    place = lax.broadcasted_iota(jnp.int32, out_ref.shape, 0)
    out_ref[...] = jnp.where(place == 0, top, jnp.where(place == 1, total, pick))


def grad_kernel(first, one_ref, two_ref, near_ref, terms_ref):
    both = jnp.concatenate([one_ref[...], two_ref[...]], axis=0)
    turned = lax.dot_general(
        near_ref[pl.ds(first, terms_ref.shape[1]), :], both, (((1,), (1,)), ((), ())),
        preferred_element_type=jnp.float32,
    )
    terms_ref[...] = turned.T


def join_kernel(members, scale, lines_ref, mine_ref, *refs):
    *terms_refs, out_ref, loss_ref = refs
    rows = mine_ref.shape[1]
    lines = lines_ref[...]
    same = shared_order(lines, members)
    loss = jnp.sum(same[0:1] + jnp.log(same[1:2]) - same[2:3], axis=1, keepdims=True) / rows
    loss_ref[...] = jnp.broadcast_to(loss, loss_ref.shape)

    top, total = lines[0:1], lines[1:2]
    soft = as_columns(jnp.exp(mine_ref[0:1, :] - top) / (total * rows)) * scale
    hard = (jnp.exp(mine_ref[2:3, :] - top) / total - 1.0) / rows
    hard = as_columns(hard.astype(jnp.bfloat16).astype(jnp.float32)) * scale

    near = rows // members * 4
    chunk = min(near, rows - near, 64)
    for place, terms_ref in enumerate(terms_refs):
        columns = pl.ds(place * terms_ref.shape[1], terms_ref.shape[1])
        for first in range(0, rows, chunk):
            at, other = (first, near) if first < near else (near + first, rows - near)
            out_ref[pl.ds(first, chunk), columns] = (
                soft[first : first + chunk] * terms_ref[pl.ds(at, chunk), :]
                + hard[first : first + chunk] * terms_ref[pl.ds(at + other, chunk), :]
            )


def frag_kernel(rows_ref, digits_ref, lines_ref, one_ref, two_ref, head_ref, global_ref, momentum_ref,
                peer_ref, new_global_ref, new_momentum_ref):
    logits = jnp.concatenate([one_ref[...], two_ref[...]], axis=0)
    rows, tile = logits.shape
    top, total = as_columns(lines_ref[0:1, :]), as_columns(lines_ref[1:2, :])
    offset = (lax.axis_index(AXIS) * pl.num_programs(0) + pl.program_id(0)) * tile
    hit = lax.broadcasted_iota(jnp.int32, (rows, tile), 1) == ids_of(digits_ref[...]) - offset
    shares = jnp.exp(logits - top) / total
    dlogits = ((shares - jnp.where(hit, 1.0, 0.0)) / rows).astype(jnp.bfloat16)
    turned = rows_ref[...].astype(jnp.float32).T.astype(jnp.bfloat16)
    frag_grad = jnp.dot(turned, dlogits, preferred_element_type=jnp.float32)
    local_frag = head_ref[...].astype(jnp.float32) - 1.0 * frag_grad
    pseudo = (global_ref[...] - local_frag + peer_ref[...]) / REPLICAS
    new_momentum = 0.9 * momentum_ref[...] + pseudo
    new_momentum_ref[...] = new_momentum
    new_global_ref[...] = global_ref[...] - 0.7 * (pseudo + 0.9 * new_momentum)


def frag_update(rows_all, lines, logits, near, global_frag, momentum, peer_delta):
    rows = rows_all.shape[0]
    width = near.shape[1]
    last = rows_all.shape[1] // LANES - 1
    tile = pl.BlockSpec((FRAG, TILE), lambda i: (0, i))
    return pl.pallas_call(
        frag_kernel,
        grid=(width // TILE,),
        out_shape=[jax.ShapeDtypeStruct((FRAG, width), jnp.float32)] * 2,
        in_specs=[
            pl.BlockSpec((rows, FRAG), lambda i: (0, 0)),
            pl.BlockSpec((rows, LANES), lambda i: (0, last)),
            pl.BlockSpec((8, rows), lambda i: (0, 0)),
        ]
        + [pl.BlockSpec((x.shape[0], TILE), lambda i: (0, i)) for x in logits]
        + [tile] * 4,
        out_specs=[tile, tile],
        compiler_params=pltpu.CompilerParams(vmem_limit_bytes=16 * 2**20),
        cost_estimate=pl.CostEstimate(
            flops=2 * rows * FRAG * width, bytes_accessed=24 * FRAG * width, transcendentals=0
        ),
    )(
        rows_all, rows_all, lines,
        *[pltpu.with_memory_space_constraint(x, pltpu.VMEM) for x in logits],
        pltpu.with_memory_space_constraint(near, pltpu.VMEM), global_frag, momentum, peer_delta,
    )


def swap(value, step):
    return lax.ppermute(value, AXIS, [(i, i ^ step) for i in range(lax.axis_size(AXIS))])


def far_steps():
    step = 4
    steps = []
    while step < lax.axis_size(AXIS):
        steps.append(step)
        step *= 2
    return steps


def gather_rows(packed):
    own = packed.shape[0]
    held = packed
    for step in far_steps()[:1]:
        held = jnp.concatenate([held, swap(held, step)], axis=0)
    near = [packed] + [swap(packed, step) for step in (3, 2, 1)][::-1]
    for step in far_steps()[1:]:
        held = jnp.concatenate([held, swap(held, step)], axis=0)
    far = held[own:]
    far = jnp.stack([far] + [swap(far, step) for step in (3, 2, 1)][::-1])
    count = far.shape[1] // own
    far = far.reshape(4, count, own, -1).swapaxes(0, 1).reshape(4 * count * own, -1)
    return jnp.concatenate(near, axis=0), far


def scatter_sums(grads, own):
    members = grads.shape[0] // own
    blocks = [grads[i * own : (i + 1) * own] for i in range(members)]

    def moved(parts, step):
        value = jnp.concatenate([part.astype(SEND) for part in parts], axis=0)
        value = swap(value, step).astype(jnp.float32)
        return [value[i * own : (i + 1) * own] for i in range(len(parts))]

    sums = blocks[::4]
    for part in (list(range(1, members // 4)), [0]):
        for step in (3, 2, 1):
            for i, value in zip(part, moved([blocks[4 * i + step] for i in part], step)):
                sums[i] = sums[i] + value
    for step in far_steps()[::-1]:
        keep = len(sums) // 2
        sums = [a + b for a, b in zip(sums[:keep], moved(sums[keep:], step))]
    return sums[0]


def body(hidden, targets, head, global_frag, momentum, peer_delta):
    members = lax.axis_size(AXIS)
    own, depth = hidden.shape
    rows = own * members
    width = head.shape[1]

    packed = call(
        pack_kernel, [((own, depth + LANES), hidden.dtype)], [targets, hidden],
        scratch=[pltpu.SMEM(targets.shape, targets.dtype), pltpu.SemaphoreType.DMA((2,))],
        sources=[pltpu.HBM, pltpu.HBM],
    )[0]
    rows_near, rows_far = gather_rows(packed)
    near = resident(head)

    def part(held, *before):
        count = held.shape[0]
        stats = (8, rows) if before else (count, LANES)
        return call(
            rows_kernel,
            [((count, width), jnp.float32), ((2 * count, width), jnp.bfloat16), (stats, jnp.float32)],
            [held, near, *before], 2 * count * depth * width,
            scratch=[pltpu.VMEM((rows, LANES), jnp.float32)] if before else [],
        )

    logits_near, both_near, columns = part(rows_near)
    logits_far, both_far, mine = part(rows_far, columns)

    lines = mine
    for steps in [[step] for step in far_steps()] + [[1, 2, 3]]:
        lines = call(
            functools.partial(merge_kernel, steps, members),
            [((8, rows), jnp.float32)], [lines] + [swap(lines, step) for step in steps],
        )[0]

    cuts = 4
    terms = [
        call(
            functools.partial(grad_kernel, i * depth // cuts),
            [((2 * rows, depth // cuts), jnp.float32)], [both_near, both_far, near],
            4 * rows * depth * width // cuts,
        )[0]
        for i in range(cuts)
    ]

    scale = 2.0**14 * rows
    grads, loss = call(
        functools.partial(join_kernel, members, scale),
        [((rows, depth), jnp.float32), ((8, LANES), jnp.float32)],
        [lines, mine] + terms,
    )
    hidden_grad = (scatter_sums(grads, own) * (1.0 / scale)).astype(jnp.bfloat16)
    new_global, new_momentum = frag_update(
        jnp.concatenate([rows_near, rows_far], axis=0), lines, [logits_near, logits_far], near,
        global_frag, momentum, peer_delta,
    )
    return (loss[0, :1], hidden_grad, new_global, new_momentum)


def solution(mesh):
    in_specs = (
        P(("outer", "vocab"), None),
        P(("outer", "vocab")),
        P("outer", "vocab"),
        P(None, "vocab"),
        P(None, "vocab"),
        P("outer", "vocab"),
    )
    out_specs = (P("outer"), P(("outer", "vocab"), None), P("outer", "vocab"), P("outer", "vocab"))
    return jax.shard_map(body, mesh=mesh, in_specs=in_specs, out_specs=out_specs, check_vma=False)
```

```python
import functools

import jax
import jax.numpy as jnp
from jax import lax
from jax.experimental import pallas as pl
from jax.experimental.pallas import tpu as pltpu
from jax.sharding import PartitionSpec as P

FRAG = 128
REPLICAS = 4
AXIS = "vocab"
SEND = jnp.float16
LANES = 128
VMEM = pl.BlockSpec(memory_space=pltpu.VMEM)


def call(kernel, outs, operands, flops=0, scratch=(), sources=None, vmem=16 * 2**20):
    outs = [pltpu.VMEM(shape, dtype) for shape, dtype in outs]
    places = sources or [pltpu.VMEM] * len(operands)
    moved = sum(x.size * x.dtype.itemsize for x in operands)
    return pl.pallas_call(
        kernel,
        out_shape=outs,
        in_specs=[pl.BlockSpec(memory_space=place) for place in places],
        out_specs=[VMEM] * len(outs),
        scratch_shapes=list(scratch),
        compiler_params=pltpu.CompilerParams(vmem_limit_bytes=vmem),
        cost_estimate=pl.CostEstimate(flops=flops, bytes_accessed=moved, transcendentals=0),
    )(*[pltpu.with_memory_space_constraint(x, place) for x, place in zip(operands, places)])


def load_kernel(source, target, sems):
    block = source.shape[0] // sems.shape[0]
    copies = []
    for i in range(sems.shape[0]):
        part = pl.ds(i * block, block)
        copies.append(pltpu.make_async_copy(source.at[part], target.at[part], sems.at[i]))
    for copy in copies:
        copy.start()
    for copy in copies:
        copy.wait()


def resident(head):
    return call(
        load_kernel, [(head.shape, head.dtype)], [head],
        scratch=[pltpu.SemaphoreType.DMA((4,))], sources=[pltpu.HBM],
    )[0]


TILE = 512
WIDE = 1024


def pack_kernel(targets, rows, out_ref, targets_ref, sems):
    own, depth = rows.shape
    ids_copy = pltpu.make_async_copy(targets, targets_ref, sems.at[0])
    rows_copy = pltpu.make_async_copy(rows, out_ref.at[:, pl.ds(0, depth)], sems.at[1])
    ids_copy.start()
    rows_copy.start()
    ids_copy.wait()
    place = lax.broadcasted_iota(jnp.int32, (own, LANES), 0)
    ids = jnp.zeros((own, LANES), jnp.int32)
    for i in range(own):
        ids = jnp.where(place == i, targets_ref[i], ids)
    lane = lax.broadcasted_iota(jnp.int32, (own, LANES), 1)
    digits = jnp.where(lane == 0, ids // 256, ids % 256)
    out_ref[:, depth:] = digits.astype(jnp.float32).astype(jnp.bfloat16)
    rows_copy.wait()


def ids_of(digits):
    digits = digits.astype(jnp.float32)
    return (digits[:, 0:1] * 256.0 + digits[:, 1:2]).astype(jnp.int32)


def swap_blocks(value, group):
    size = value.shape[1]
    lane = lax.broadcasted_iota(jnp.int32, value.shape, 1)
    up, down = pltpu.roll(value, group, 1), pltpu.roll(value, size - group, 1)
    return jnp.where((lane & group) != 0, up, down)


def shared_order(value, members):
    me = lax.axis_index(AXIS)
    step = 1
    while step < members:
        swapped = swap_blocks(value, value.shape[1] // members * step)
        value = jnp.where((me & step) != 0, swapped, value)
        step *= 2
    return value


def as_columns(line):
    return jnp.broadcast_to(line, (LANES, line.shape[1])).T[:, 0:1]


def rows_kernel(rows_ref, near_ref, *refs):
    before_ref, (logits_ref, both_ref, stats_ref) = (None, refs) if len(refs) == 3 else (refs[0], refs[1:4])
    rows = rows_ref.shape[0]
    depth, width = near_ref.shape

    @pl.loop(0, width // WIDE)
    def _(i):
        part = pl.ds(pl.multiple_of(i * WIDE, WIDE), WIDE)
        logits_ref[:, part] = jnp.dot(
            rows_ref[:, :depth], near_ref[:, part], preferred_element_type=jnp.float32
        )

    chunk = 32
    offset = lax.axis_index(AXIS) * width
    columns_ref = stats_ref if before_ref is None else refs[4]
    first = 0 if before_ref is None else before_ref.shape[0]

    @pl.loop(0, rows // chunk)
    def _(i):
        part = pl.ds(pl.multiple_of(i * chunk, chunk), chunk)
        logits = logits_ref[part, :]
        ids = ids_of(rows_ref[part, depth:]) - offset
        hit = lax.broadcasted_iota(jnp.int32, logits.shape, 1) == ids
        top = jnp.max(logits, axis=1, keepdims=True)
        raised = jnp.exp(logits - top)
        total = jnp.sum(raised, axis=1, keepdims=True)
        pick = jnp.sum(jnp.where(hit, logits, 0.0), axis=1, keepdims=True)
        both_ref[part, :] = jnp.where(hit, 0.0, raised).astype(jnp.bfloat16)
        other = pl.ds(pl.multiple_of(rows + i * chunk, chunk), chunk)
        both_ref[other, :] = jnp.where(hit, 1.0, 0.0).astype(jnp.bfloat16)
        place = lax.broadcasted_iota(jnp.int32, (chunk, LANES), 1)
        slot = pl.ds(pl.multiple_of(first + i * chunk, chunk), chunk)
        columns_ref[slot, :] = jnp.where(place == 0, top, jnp.where(place == 1, total, pick))

    if before_ref is not None:
        columns_ref[pl.ds(0, first), :] = before_ref[...]
        stats_ref[...] = columns_ref[...].T[:8]


def merge_kernel(steps, members, mine_ref, *refs):
    *other_refs, out_ref = refs
    block = mine_ref.shape[1] // members
    me = lax.axis_index(AXIS)
    groups = [mine_ref[...]]
    for step, other_ref in zip(steps, other_refs):
        other, bit = other_ref[...], 1
        while bit <= step:
            if step & bit:
                other = swap_blocks(other, block * bit)
            bit *= 2
        groups.append(other)
    unit, bit = steps[0], 1
    while bit < len(groups):
        upper = (me & (unit * bit)) != 0
        groups = [jnp.where(upper, groups[i ^ bit], group) for i, group in enumerate(groups)]
        bit *= 2
    top = functools.reduce(jnp.maximum, [group[0:1] for group in groups])
    total = sum(group[1:2] * jnp.exp(group[0:1] - top) for group in groups)
    pick = sum(group[2:3] for group in groups)
    place = lax.broadcasted_iota(jnp.int32, out_ref.shape, 0)
    out_ref[...] = jnp.where(place == 0, top, jnp.where(place == 1, total, pick))


def grad_kernel(first, one_ref, two_ref, near_ref, *refs):
    terms_ref = refs[-1]
    tile = 1024
    both = jnp.concatenate([one_ref[...], two_ref[...]], axis=0)
    for place in range(0, terms_ref.shape[1], tile):
        turned = lax.dot_general(
            near_ref[pl.ds(first + place, tile), :], both, (((1,), (1,)), ((), ())),
            preferred_element_type=jnp.float32,
        )
        terms_ref[:, pl.ds(place, tile)] = turned.T


def join_kernel(scale, first, lines_ref, mine_ref, *refs):
    *terms_refs, out_ref = refs
    rows = mine_ref.shape[1]
    top, total = lines_ref[0:1, :], lines_ref[1:2, :]
    soft = as_columns(jnp.exp(mine_ref[0:1, :] - top) / (total * rows)) * scale
    hard = (jnp.exp(mine_ref[2:3, :] - top) / total - 1.0) / rows
    hard = as_columns(hard.astype(jnp.bfloat16).astype(jnp.float32)) * scale

    count = out_ref.shape[0]
    chunk = min(count, 64)
    for place, terms_ref in enumerate(terms_refs):
        columns = pl.ds(place * terms_ref.shape[1], terms_ref.shape[1])
        for i in range(0, count, chunk):
            part = slice(first + i, first + i + chunk)
            out_ref[pl.ds(i, chunk), columns] = (
                soft[part] * terms_ref[pl.ds(2 * first + i, chunk), :]
                + hard[part] * terms_ref[pl.ds(2 * first + count + i, chunk), :]
            )


def loss_kernel(members, lines_ref, loss_ref):
    rows = lines_ref.shape[1]
    lines = shared_order(lines_ref[...], members)
    loss = jnp.sum(lines[0:1] + jnp.log(lines[1:2]) - lines[2:3], axis=1, keepdims=True) / rows
    loss_ref[...] = jnp.broadcast_to(loss, loss_ref.shape)


def frag_kernel(rows_ref, digits_ref, lines_ref, one_ref, two_ref, head_ref, global_ref, momentum_ref,
                peer_ref, new_global_ref, new_momentum_ref):
    logits = jnp.concatenate([one_ref[...], two_ref[...]], axis=0)
    rows, tile = logits.shape
    top, total = as_columns(lines_ref[0:1, :]), as_columns(lines_ref[1:2, :])
    offset = (lax.axis_index(AXIS) * pl.num_programs(0) + pl.program_id(0)) * tile
    hit = lax.broadcasted_iota(jnp.int32, (rows, tile), 1) == ids_of(digits_ref[...]) - offset
    shares = jnp.exp(logits - top) / total
    dlogits = ((shares - jnp.where(hit, 1.0, 0.0)) / rows).astype(jnp.bfloat16)
    turned = rows_ref[...].astype(jnp.float32).T.astype(jnp.bfloat16)
    frag_grad = jnp.dot(turned, dlogits, preferred_element_type=jnp.float32)
    local_frag = head_ref[...].astype(jnp.float32) - 1.0 * frag_grad
    pseudo = (global_ref[...] - local_frag + peer_ref[...]) / REPLICAS
    new_momentum = 0.9 * momentum_ref[...] + pseudo
    new_momentum_ref[...] = new_momentum
    new_global_ref[...] = global_ref[...] - 0.7 * (pseudo + 0.9 * new_momentum)


def frag_update(rows_all, lines, logits, near, global_frag, momentum, peer_delta):
    rows = rows_all.shape[0]
    width = near.shape[1]
    last = rows_all.shape[1] // LANES - 1
    tile = pl.BlockSpec((FRAG, TILE), lambda i: (0, i))
    return pl.pallas_call(
        frag_kernel,
        grid=(width // TILE,),
        out_shape=[jax.ShapeDtypeStruct((FRAG, width), jnp.float32)] * 2,
        in_specs=[
            pl.BlockSpec((rows, FRAG), lambda i: (0, 0)),
            pl.BlockSpec((rows, LANES), lambda i: (0, last)),
            pl.BlockSpec((8, rows), lambda i: (0, 0)),
        ]
        + [pl.BlockSpec((x.shape[0], TILE), lambda i: (0, i)) for x in logits]
        + [tile] * 4,
        out_specs=[tile, tile],
        compiler_params=pltpu.CompilerParams(vmem_limit_bytes=16 * 2**20),
        cost_estimate=pl.CostEstimate(
            flops=2 * rows * FRAG * width, bytes_accessed=24 * FRAG * width, transcendentals=0
        ),
    )(
        rows_all, rows_all, lines,
        *[pltpu.with_memory_space_constraint(x, pltpu.VMEM) for x in logits],
        pltpu.with_memory_space_constraint(near, pltpu.VMEM), global_frag, momentum, peer_delta,
    )


def swap(value, step):
    return lax.ppermute(value, AXIS, [(i, i ^ step) for i in range(lax.axis_size(AXIS))])


def far_steps():
    step = 4
    steps = []
    while step < lax.axis_size(AXIS):
        steps.append(step)
        step *= 2
    return steps


def gather_rows(packed):
    own = packed.shape[0]
    held = packed
    for step in far_steps()[:1]:
        held = jnp.concatenate([held, swap(held, step)], axis=0)
    near = [packed] + [swap(packed, step) for step in (3, 2, 1)][::-1]
    for step in far_steps()[1:]:
        held = jnp.concatenate([held, swap(held, step)], axis=0)
    far = held[own:]
    far = jnp.stack([far] + [swap(far, step) for step in (3, 2, 1)][::-1])
    count = far.shape[1] // own
    far = far.reshape(4, count, own, -1).swapaxes(0, 1).reshape(4 * count * own, -1)
    return jnp.concatenate(near, axis=0), far


def scatter_sums(grads_near, grads_far, own):
    blocks = [
        grads[i * own : (i + 1) * own]
        for grads in (grads_near, grads_far)
        for i in range(grads.shape[0] // own)
    ]
    members = len(blocks)

    def moved(parts, step):
        value = jnp.concatenate([part.astype(SEND) for part in parts], axis=0)
        value = swap(value, step).astype(jnp.float32)
        return [value[i * own : (i + 1) * own] for i in range(len(parts))]

    sums = blocks[::4]
    for part in (list(range(1, members // 4)), [0]):
        for step in (3, 2, 1):
            for i, value in zip(part, moved([blocks[4 * i + step] for i in part], step)):
                sums[i] = sums[i] + value
    for step in far_steps()[::-1]:
        keep = len(sums) // 2
        sums = [a + b for a, b in zip(sums[:keep], moved(sums[keep:], step))]
    return sums[0]


def body(hidden, targets, head, global_frag, momentum, peer_delta):
    members = lax.axis_size(AXIS)
    own, depth = hidden.shape
    rows = own * members
    width = head.shape[1]

    packed = call(
        pack_kernel, [((own, depth + LANES), hidden.dtype)], [targets, hidden],
        scratch=[pltpu.SMEM(targets.shape, targets.dtype), pltpu.SemaphoreType.DMA((2,))],
        sources=[pltpu.HBM, pltpu.HBM],
    )[0]
    rows_near, rows_far = gather_rows(packed)
    near = resident(head)

    def part(held, *before):
        count = held.shape[0]
        stats = (8, rows) if before else (count, LANES)
        return call(
            rows_kernel,
            [((count, width), jnp.float32), ((2 * count, width), jnp.bfloat16), (stats, jnp.float32)],
            [held, near, *before], 2 * count * depth * width,
            scratch=[pltpu.VMEM((rows, LANES), jnp.float32)] if before else [],
        )

    logits_near, both_near, columns = part(rows_near)
    logits_far, both_far, mine = part(rows_far, columns)

    lines = mine
    for steps in [[step] for step in far_steps()] + [[1, 2, 3]]:
        before = lines
        lines = call(
            functools.partial(merge_kernel, steps, members),
            [((8, rows), jnp.float32)], [lines] + [swap(lines, step) for step in steps],
        )[0]

    terms = [
        call(
            functools.partial(grad_kernel, first),
            [((2 * rows, depth // 2), jnp.float32)], [both_near, both_far, near, *after],
            2 * rows * depth * width,
        )[0]
        for first, after in ((0, []), (depth // 2, [before]))
    ]

    scale = 2.0**14 * rows
    grads_far, grads_near = (
        call(
            functools.partial(join_kernel, scale, first),
            [((count, depth), jnp.float32)], [lines, mine] + terms,
        )[0]
        for first, count in ((4 * own, rows - 4 * own), (0, 4 * own))
    )
    hidden_grad = (scatter_sums(grads_near, grads_far, own) * (1.0 / scale)).astype(jnp.bfloat16)
    loss = call(functools.partial(loss_kernel, members), [((8, LANES), jnp.float32)], [lines])[0]
    new_global, new_momentum = frag_update(
        jnp.concatenate([rows_near, rows_far], axis=0), lines, [logits_near, logits_far], near,
        global_frag, momentum, peer_delta,
    )
    return (loss[0, :1], hidden_grad, new_global, new_momentum)


def solution(mesh):
    in_specs = (
        P(("outer", "vocab"), None),
        P(("outer", "vocab")),
        P("outer", "vocab"),
        P(None, "vocab"),
        P(None, "vocab"),
        P("outer", "vocab"),
    )
    out_specs = (P("outer"), P(("outer", "vocab"), None), P("outer", "vocab"), P("outer", "vocab"))
    return jax.shard_map(body, mesh=mesh, in_specs=in_specs, out_specs=out_specs, check_vma=False)
```

```python
import functools

import jax
import jax.numpy as jnp
from jax import lax
from jax.experimental import pallas as pl
from jax.experimental.pallas import tpu as pltpu
from jax.sharding import PartitionSpec as P

FRAG = 128
REPLICAS = 4
AXIS = "vocab"
SEND = jnp.float16
LANES = 128
VMEM = pl.BlockSpec(memory_space=pltpu.VMEM)


def call(kernel, outs, operands, flops=0, scratch=(), sources=None, vmem=16 * 2**20, aliases={}):
    outs = [pltpu.VMEM(shape, dtype) for shape, dtype in outs]
    places = sources or [pltpu.VMEM] * len(operands)
    moved = sum(x.size * x.dtype.itemsize for x in operands)
    return pl.pallas_call(
        kernel,
        out_shape=outs,
        in_specs=[pl.BlockSpec(memory_space=place) for place in places],
        out_specs=[VMEM] * len(outs),
        scratch_shapes=list(scratch),
        input_output_aliases=aliases,
        compiler_params=pltpu.CompilerParams(vmem_limit_bytes=vmem),
        cost_estimate=pl.CostEstimate(flops=flops, bytes_accessed=moved, transcendentals=0),
    )(*[pltpu.with_memory_space_constraint(x, place) for x, place in zip(operands, places)])


def late_sender():
    return lax.rem(lax.axis_index("outer"), 2) == 1


def load(source, target, sems):
    block = source.shape[0] // sems.shape[0]
    copies = []
    for i in range(sems.shape[0]):
        part = pl.ds(i * block, block)
        copies.append(pltpu.make_async_copy(source.at[part], target.at[part], sems.at[i]))
    for copy in copies:
        copy.start()
    for copy in copies:
        copy.wait()


def load_kernel(source, held, target, sems):
    @pl.when(jnp.logical_not(late_sender()))
    def _():
        load(source, target, sems)


TILE = 512
WIDE = 1024


def pack_kernel(targets, rows, head, out_ref, near_ref, targets_ref, sems, head_sems):
    own, depth = rows.shape
    ids_copy = pltpu.make_async_copy(targets, targets_ref, sems.at[0])
    rows_copy = pltpu.make_async_copy(rows, out_ref.at[:, pl.ds(0, depth)], sems.at[1])
    ids_copy.start()
    rows_copy.start()
    ids_copy.wait()
    place = lax.broadcasted_iota(jnp.int32, (own, LANES), 0)
    ids = jnp.zeros((own, LANES), jnp.int32)
    for i in range(own):
        ids = jnp.where(place == i, targets_ref[i], ids)
    lane = lax.broadcasted_iota(jnp.int32, (own, LANES), 1)
    digits = jnp.where(lane == 0, ids // 256, ids % 256)
    out_ref[:, depth:] = digits.astype(jnp.float32).astype(jnp.bfloat16)
    rows_copy.wait()

    @pl.when(late_sender())
    def _():
        load(head, near_ref, head_sems)


def ids_of(digits):
    digits = digits.astype(jnp.float32)
    return (digits[:, 0:1] * 256.0 + digits[:, 1:2]).astype(jnp.int32)


def swap_blocks(value, group):
    size = value.shape[1]
    lane = lax.broadcasted_iota(jnp.int32, value.shape, 1)
    up, down = pltpu.roll(value, group, 1), pltpu.roll(value, size - group, 1)
    return jnp.where((lane & group) != 0, up, down)


def shared_order(value, members):
    me = lax.axis_index(AXIS)
    step = 1
    while step < members:
        swapped = swap_blocks(value, value.shape[1] // members * step)
        value = jnp.where((me & step) != 0, swapped, value)
        step *= 2
    return value


def as_columns(line):
    return jnp.broadcast_to(line, (LANES, line.shape[1])).T[:, 0:1]


def rows_kernel(rows_ref, near_ref, *refs):
    before_ref, (logits_ref, both_ref, stats_ref) = (None, refs) if len(refs) == 3 else (refs[0], refs[1:4])
    rows = rows_ref.shape[0]
    depth, width = near_ref.shape

    @pl.loop(0, width // WIDE)
    def _(i):
        part = pl.ds(pl.multiple_of(i * WIDE, WIDE), WIDE)
        logits_ref[:, part] = jnp.dot(
            rows_ref[:, :depth], near_ref[:, part], preferred_element_type=jnp.float32
        )

    chunk = 32
    offset = lax.axis_index(AXIS) * width
    columns_ref = stats_ref if before_ref is None else refs[4]
    first = 0 if before_ref is None else before_ref.shape[0]

    @pl.loop(0, rows // chunk)
    def _(i):
        part = pl.ds(pl.multiple_of(i * chunk, chunk), chunk)
        logits = logits_ref[part, :]
        ids = ids_of(rows_ref[part, depth:]) - offset
        hit = lax.broadcasted_iota(jnp.int32, logits.shape, 1) == ids
        top = jnp.max(logits, axis=1, keepdims=True)
        raised = jnp.exp(logits - top)
        total = jnp.sum(raised, axis=1, keepdims=True)
        pick = jnp.sum(jnp.where(hit, logits, 0.0), axis=1, keepdims=True)
        both_ref[part, :] = jnp.where(hit, 0.0, raised).astype(jnp.bfloat16)
        other = pl.ds(pl.multiple_of(rows + i * chunk, chunk), chunk)
        both_ref[other, :] = jnp.where(hit, 1.0, 0.0).astype(jnp.bfloat16)
        place = lax.broadcasted_iota(jnp.int32, (chunk, LANES), 1)
        slot = pl.ds(pl.multiple_of(first + i * chunk, chunk), chunk)
        columns_ref[slot, :] = jnp.where(place == 0, top, jnp.where(place == 1, total, pick))

    if before_ref is not None:
        columns_ref[pl.ds(0, first), :] = before_ref[...]
        stats_ref[...] = columns_ref[...].T[:8]


def merge_kernel(steps, members, mine_ref, *refs):
    *other_refs, out_ref = refs
    block = mine_ref.shape[1] // members
    me = lax.axis_index(AXIS)
    groups = [mine_ref[...]]
    for step, other_ref in zip(steps, other_refs):
        other, bit = other_ref[...], 1
        while bit <= step:
            if step & bit:
                other = swap_blocks(other, block * bit)
            bit *= 2
        groups.append(other)
    unit, bit = steps[0], 1
    while bit < len(groups):
        upper = (me & (unit * bit)) != 0
        groups = [jnp.where(upper, groups[i ^ bit], group) for i, group in enumerate(groups)]
        bit *= 2
    top = functools.reduce(jnp.maximum, [group[0:1] for group in groups])
    total = sum(group[1:2] * jnp.exp(group[0:1] - top) for group in groups)
    pick = sum(group[2:3] for group in groups)
    place = lax.broadcasted_iota(jnp.int32, out_ref.shape, 0)
    out_ref[...] = jnp.where(place == 0, top, jnp.where(place == 1, total, pick))


def grad_kernel(first, one_ref, two_ref, near_ref, *refs):
    terms_ref = refs[-1]
    tile = 1024
    both = jnp.concatenate([one_ref[...], two_ref[...]], axis=0)
    for place in range(0, terms_ref.shape[1], tile):
        turned = lax.dot_general(
            near_ref[pl.ds(first + place, tile), :], both, (((1,), (1,)), ((), ())),
            preferred_element_type=jnp.float32,
        )
        terms_ref[:, pl.ds(place, tile)] = turned.T


def join_kernel(scale, first, lines_ref, mine_ref, *refs):
    *terms_refs, out_ref = refs
    rows = mine_ref.shape[1]
    top, total = lines_ref[0:1, :], lines_ref[1:2, :]
    soft = as_columns(jnp.exp(mine_ref[0:1, :] - top) / (total * rows)) * scale
    hard = (jnp.exp(mine_ref[2:3, :] - top) / total - 1.0) / rows
    hard = as_columns(hard.astype(jnp.bfloat16).astype(jnp.float32)) * scale

    count = out_ref.shape[0]
    chunk = min(count, 64)
    for place, terms_ref in enumerate(terms_refs):
        columns = pl.ds(place * terms_ref.shape[1], terms_ref.shape[1])
        for i in range(0, count, chunk):
            part = slice(first + i, first + i + chunk)
            out_ref[pl.ds(i, chunk), columns] = (
                soft[part] * terms_ref[pl.ds(2 * first + i, chunk), :]
                + hard[part] * terms_ref[pl.ds(2 * first + count + i, chunk), :]
            )


def loss_kernel(members, lines_ref, loss_ref):
    rows = lines_ref.shape[1]
    lines = shared_order(lines_ref[...], members)
    loss = jnp.sum(lines[0:1] + jnp.log(lines[1:2]) - lines[2:3], axis=1, keepdims=True) / rows
    loss_ref[...] = jnp.broadcast_to(loss, loss_ref.shape)


def frag_kernel(rows_ref, digits_ref, lines_ref, one_ref, two_ref, head_ref, global_ref, momentum_ref,
                peer_ref, new_global_ref, new_momentum_ref):
    logits = jnp.concatenate([one_ref[...], two_ref[...]], axis=0)
    rows, tile = logits.shape
    top, total = as_columns(lines_ref[0:1, :]), as_columns(lines_ref[1:2, :])
    offset = (lax.axis_index(AXIS) * pl.num_programs(0) + pl.program_id(0)) * tile
    hit = lax.broadcasted_iota(jnp.int32, (rows, tile), 1) == ids_of(digits_ref[...]) - offset
    shares = jnp.exp(logits - top) / total
    dlogits = ((shares - jnp.where(hit, 1.0, 0.0)) / rows).astype(jnp.bfloat16)
    turned = rows_ref[...].astype(jnp.float32).T.astype(jnp.bfloat16)
    frag_grad = jnp.dot(turned, dlogits, preferred_element_type=jnp.float32)
    local_frag = head_ref[...].astype(jnp.float32) - 1.0 * frag_grad
    pseudo = (global_ref[...] - local_frag + peer_ref[...]) / REPLICAS
    new_momentum = 0.9 * momentum_ref[...] + pseudo
    new_momentum_ref[...] = new_momentum
    new_global_ref[...] = global_ref[...] - 0.7 * (pseudo + 0.9 * new_momentum)


def frag_update(rows_all, lines, logits, near, global_frag, momentum, peer_delta):
    rows = rows_all.shape[0]
    width = near.shape[1]
    last = rows_all.shape[1] // LANES - 1
    tile = pl.BlockSpec((FRAG, TILE), lambda i: (0, i))
    return pl.pallas_call(
        frag_kernel,
        grid=(width // TILE,),
        out_shape=[jax.ShapeDtypeStruct((FRAG, width), jnp.float32)] * 2,
        in_specs=[
            pl.BlockSpec((rows, FRAG), lambda i: (0, 0)),
            pl.BlockSpec((rows, LANES), lambda i: (0, last)),
            pl.BlockSpec((8, rows), lambda i: (0, 0)),
        ]
        + [pl.BlockSpec((x.shape[0], TILE), lambda i: (0, i)) for x in logits]
        + [tile] * 4,
        out_specs=[tile, tile],
        compiler_params=pltpu.CompilerParams(vmem_limit_bytes=16 * 2**20),
        cost_estimate=pl.CostEstimate(
            flops=2 * rows * FRAG * width, bytes_accessed=24 * FRAG * width, transcendentals=0
        ),
    )(
        rows_all, rows_all, lines,
        *[pltpu.with_memory_space_constraint(x, pltpu.VMEM) for x in logits],
        pltpu.with_memory_space_constraint(near, pltpu.VMEM), global_frag, momentum, peer_delta,
    )


def swap(value, step):
    return lax.ppermute(value, AXIS, [(i, i ^ step) for i in range(lax.axis_size(AXIS))])


def far_steps():
    step = 4
    steps = []
    while step < lax.axis_size(AXIS):
        steps.append(step)
        step *= 2
    return steps


def gather_rows(packed):
    own = packed.shape[0]
    held = packed
    for step in far_steps()[:1]:
        held = jnp.concatenate([held, swap(held, step)], axis=0)
    near = [packed] + [swap(packed, step) for step in (3, 2, 1)][::-1]
    for step in far_steps()[1:]:
        held = jnp.concatenate([held, swap(held, step)], axis=0)
    far = held[own:]
    far = jnp.stack([far] + [swap(far, step) for step in (3, 2, 1)][::-1])
    count = far.shape[1] // own
    far = far.reshape(4, count, own, -1).swapaxes(0, 1).reshape(4 * count * own, -1)
    return jnp.concatenate(near, axis=0), far


def scatter_sums(grads_near, grads_far, own):
    blocks = [
        grads[i * own : (i + 1) * own]
        for grads in (grads_near, grads_far)
        for i in range(grads.shape[0] // own)
    ]
    members = len(blocks)

    def moved(parts, step):
        value = jnp.concatenate([part.astype(SEND) for part in parts], axis=0)
        value = swap(value, step).astype(jnp.float32)
        return [value[i * own : (i + 1) * own] for i in range(len(parts))]

    sums = blocks[::4]
    for part in (list(range(1, members // 4)), [0]):
        for step in (3, 2, 1):
            for i, value in zip(part, moved([blocks[4 * i + step] for i in part], step)):
                sums[i] = sums[i] + value
    for step in far_steps()[::-1]:
        keep = len(sums) // 2
        sums = [a + b for a, b in zip(sums[:keep], moved(sums[keep:], step))]
    return sums[0]


def body(hidden, targets, head, global_frag, momentum, peer_delta):
    members = lax.axis_size(AXIS)
    own, depth = hidden.shape
    rows = own * members
    width = head.shape[1]

    packed, near = call(
        pack_kernel, [((own, depth + LANES), hidden.dtype), (head.shape, head.dtype)],
        [targets, hidden, head],
        scratch=[
            pltpu.SMEM(targets.shape, targets.dtype),
            pltpu.SemaphoreType.DMA((2,)),
            pltpu.SemaphoreType.DMA((4,)),
        ],
        sources=[pltpu.HBM] * 3,
    )
    rows_near, rows_far = gather_rows(packed)
    near = call(
        load_kernel, [(head.shape, head.dtype)], [head, near],
        scratch=[pltpu.SemaphoreType.DMA((4,))], sources=[pltpu.HBM, pltpu.VMEM], aliases={1: 0},
    )[0]

    def part(held, *before):
        count = held.shape[0]
        stats = (8, rows) if before else (count, LANES)
        return call(
            rows_kernel,
            [((count, width), jnp.float32), ((2 * count, width), jnp.bfloat16), (stats, jnp.float32)],
            [held, near, *before], 2 * count * depth * width,
            scratch=[pltpu.VMEM((rows, LANES), jnp.float32)] if before else [],
        )

    logits_near, both_near, columns = part(rows_near)
    logits_far, both_far, mine = part(rows_far, columns)

    lines = mine
    for steps in [[step] for step in far_steps()] + [[1, 2, 3]]:
        before = lines
        lines = call(
            functools.partial(merge_kernel, steps, members),
            [((8, rows), jnp.float32)], [lines] + [swap(lines, step) for step in steps],
        )[0]

    terms = [
        call(
            functools.partial(grad_kernel, first),
            [((2 * rows, depth // 2), jnp.float32)], [both_near, both_far, near, *after],
            2 * rows * depth * width,
        )[0]
        for first, after in ((0, []), (depth // 2, [before]))
    ]

    scale = 2.0**14 * rows
    grads_far, grads_near = (
        call(
            functools.partial(join_kernel, scale, first),
            [((count, depth), jnp.float32)], [lines, mine] + terms,
        )[0]
        for first, count in ((4 * own, rows - 4 * own), (0, 4 * own))
    )
    hidden_grad = (scatter_sums(grads_near, grads_far, own) * (1.0 / scale)).astype(jnp.bfloat16)
    loss = call(functools.partial(loss_kernel, members), [((8, LANES), jnp.float32)], [lines])[0]
    new_global, new_momentum = frag_update(
        jnp.concatenate([rows_near, rows_far], axis=0), lines, [logits_near, logits_far], near,
        global_frag, momentum, peer_delta,
    )
    return (loss[0, :1], hidden_grad, new_global, new_momentum)


def solution(mesh):
    in_specs = (
        P(("outer", "vocab"), None),
        P(("outer", "vocab")),
        P("outer", "vocab"),
        P(None, "vocab"),
        P(None, "vocab"),
        P("outer", "vocab"),
    )
    out_specs = (P("outer"), P(("outer", "vocab"), None), P("outer", "vocab"), P("outer", "vocab"))
    return jax.shard_map(body, mesh=mesh, in_specs=in_specs, out_specs=out_specs, check_vma=False)
```

```python
import functools

import jax
import jax.numpy as jnp
from jax import lax
from jax.experimental import pallas as pl
from jax.experimental.pallas import tpu as pltpu
from jax.sharding import PartitionSpec as P

FRAG = 128
REPLICAS = 4
AXIS = "vocab"
SEND = jnp.float16
LANES = 128
VMEM = pl.BlockSpec(memory_space=pltpu.VMEM)


def call(kernel, outs, operands, flops=0, scratch=(), sources=None, vmem=16 * 2**20, aliases={}):
    outs = [pltpu.VMEM(shape, dtype) for shape, dtype in outs]
    places = sources or [pltpu.VMEM] * len(operands)
    moved = sum(x.size * x.dtype.itemsize for x in operands)
    return pl.pallas_call(
        kernel,
        out_shape=outs,
        in_specs=[pl.BlockSpec(memory_space=place) for place in places],
        out_specs=[VMEM] * len(outs),
        scratch_shapes=list(scratch),
        input_output_aliases=aliases,
        compiler_params=pltpu.CompilerParams(vmem_limit_bytes=vmem),
        cost_estimate=pl.CostEstimate(flops=flops, bytes_accessed=moved, transcendentals=0),
    )(*[pltpu.with_memory_space_constraint(x, place) for x, place in zip(operands, places)])


def head_copies(source, target, sems, half):
    block = source.shape[0] // sems.shape[0]
    columns = pl.ds(half * (source.shape[1] // 2), source.shape[1] // 2)
    copies = []
    for i in range(sems.shape[0]):
        part = pl.ds(i * block, block)
        copies.append(pltpu.make_async_copy(source.at[part, columns], target.at[part, columns], sems.at[i]))
    return copies


def load_kernel(head, near_ref, sems):
    copies = head_copies(head, near_ref, sems, 0)
    for copy in copies:
        copy.start()
    for copy in copies:
        copy.wait()


TILE = 512
WIDE = 1024


def pack_kernel(targets, rows, out_ref, targets_ref, sems):
    own, depth = rows.shape
    ids_copy = pltpu.make_async_copy(targets, targets_ref, sems.at[0])
    rows_copy = pltpu.make_async_copy(rows, out_ref.at[:, pl.ds(0, depth)], sems.at[1])
    ids_copy.start()
    rows_copy.start()
    ids_copy.wait()
    place = lax.broadcasted_iota(jnp.int32, (own, LANES), 0)
    ids = jnp.zeros((own, LANES), jnp.int32)
    for i in range(own):
        ids = jnp.where(place == i, targets_ref[i], ids)
    lane = lax.broadcasted_iota(jnp.int32, (own, LANES), 1)
    digits = jnp.where(lane == 0, ids // 256, ids % 256)
    out_ref[:, depth:] = digits.astype(jnp.float32).astype(jnp.bfloat16)
    rows_copy.wait()


def ids_of(digits):
    digits = digits.astype(jnp.float32)
    return (digits[:, 0:1] * 256.0 + digits[:, 1:2]).astype(jnp.int32)


def swap_blocks(value, group):
    size = value.shape[1]
    lane = lax.broadcasted_iota(jnp.int32, value.shape, 1)
    up, down = pltpu.roll(value, group, 1), pltpu.roll(value, size - group, 1)
    return jnp.where((lane & group) != 0, up, down)


def shared_order(value, members):
    me = lax.axis_index(AXIS)
    step = 1
    while step < members:
        swapped = swap_blocks(value, value.shape[1] // members * step)
        value = jnp.where((me & step) != 0, swapped, value)
        step *= 2
    return value


def as_columns(line):
    return jnp.broadcast_to(line, (LANES, line.shape[1])).T[:, 0:1]


def logits_of(rows_ref, near_ref, logits_ref, first, count):
    depth = near_ref.shape[0]

    @pl.loop(0, count // WIDE)
    def _(i):
        part = pl.ds(pl.multiple_of(first + i * WIDE, WIDE), WIDE)
        logits_ref[:, part] = jnp.dot(
            rows_ref[:, :depth], near_ref[:, part], preferred_element_type=jnp.float32
        )


def softmax_of(rows_ref, logits_ref, both_ref, columns_ref, first):
    rows, width = logits_ref.shape
    digits = rows_ref.shape[1] - LANES
    chunk = 32
    offset = lax.axis_index(AXIS) * width

    @pl.loop(0, rows // chunk)
    def _(i):
        part = pl.ds(pl.multiple_of(i * chunk, chunk), chunk)
        logits = logits_ref[part, :]
        ids = ids_of(rows_ref[part, digits:]) - offset
        hit = lax.broadcasted_iota(jnp.int32, logits.shape, 1) == ids
        top = jnp.max(logits, axis=1, keepdims=True)
        raised = jnp.exp(logits - top)
        total = jnp.sum(raised, axis=1, keepdims=True)
        pick = jnp.sum(jnp.where(hit, logits, 0.0), axis=1, keepdims=True)
        both_ref[part, :] = jnp.where(hit, 0.0, raised).astype(jnp.bfloat16)
        other = pl.ds(pl.multiple_of(rows + i * chunk, chunk), chunk)
        both_ref[other, :] = jnp.where(hit, 1.0, 0.0).astype(jnp.bfloat16)
        place = lax.broadcasted_iota(jnp.int32, (chunk, LANES), 1)
        slot = pl.ds(pl.multiple_of(first + i * chunk, chunk), chunk)
        columns_ref[slot, :] = jnp.where(place == 0, top, jnp.where(place == 1, total, pick))


def first_kernel(packed_ref, head, held_ref, near_ref, logits_ref, both_ref, columns_ref, sems):
    half = near_ref.shape[1] // 2
    copies = head_copies(head, near_ref, sems, 1)
    for copy in copies:
        copy.start()
    logits_of(packed_ref, near_ref, logits_ref, 0, half)
    for copy in copies:
        copy.wait()
    logits_of(packed_ref, near_ref, logits_ref, half, half)
    softmax_of(packed_ref, logits_ref, both_ref, columns_ref, 0)


def second_kernel(rows_ref, near_ref, before_ref, logits_ref, both_ref, lines_ref, columns_ref):
    first = before_ref.shape[0]
    logits_of(rows_ref, near_ref, logits_ref, 0, near_ref.shape[1])
    softmax_of(rows_ref, logits_ref, both_ref, columns_ref, first)
    columns_ref[pl.ds(0, first), :] = before_ref[...]
    lines_ref[...] = columns_ref[...].T[:8]


def merge_kernel(steps, members, mine_ref, *refs):
    *other_refs, out_ref = refs
    block = mine_ref.shape[1] // members
    me = lax.axis_index(AXIS)
    groups = [mine_ref[...]]
    for step, other_ref in zip(steps, other_refs):
        other, bit = other_ref[...], 1
        while bit <= step:
            if step & bit:
                other = swap_blocks(other, block * bit)
            bit *= 2
        groups.append(other)
    unit, bit = steps[0], 1
    while bit < len(groups):
        upper = (me & (unit * bit)) != 0
        groups = [jnp.where(upper, groups[i ^ bit], group) for i, group in enumerate(groups)]
        bit *= 2
    top = functools.reduce(jnp.maximum, [group[0:1] for group in groups])
    total = sum(group[1:2] * jnp.exp(group[0:1] - top) for group in groups)
    pick = sum(group[2:3] for group in groups)
    place = lax.broadcasted_iota(jnp.int32, out_ref.shape, 0)
    out_ref[...] = jnp.where(place == 0, top, jnp.where(place == 1, total, pick))


def grad_kernel(first, one_ref, two_ref, near_ref, *refs):
    terms_ref = refs[-1]
    tile = 1024
    both = jnp.concatenate([one_ref[...], two_ref[...]], axis=0)
    for place in range(0, terms_ref.shape[1], tile):
        turned = lax.dot_general(
            near_ref[pl.ds(first + place, tile), :], both, (((1,), (1,)), ((), ())),
            preferred_element_type=jnp.float32,
        )
        terms_ref[:, pl.ds(place, tile)] = turned.T


def join_kernel(scale, first, lines_ref, mine_ref, *refs):
    *terms_refs, out_ref = refs
    rows = mine_ref.shape[1]
    top, total = lines_ref[0:1, :], lines_ref[1:2, :]
    soft = as_columns(jnp.exp(mine_ref[0:1, :] - top) / (total * rows)) * scale
    hard = (jnp.exp(mine_ref[2:3, :] - top) / total - 1.0) / rows
    hard = as_columns(hard.astype(jnp.bfloat16).astype(jnp.float32)) * scale

    count = out_ref.shape[0]
    chunk = min(count, 64)
    for place, terms_ref in enumerate(terms_refs):
        columns = pl.ds(place * terms_ref.shape[1], terms_ref.shape[1])
        for i in range(0, count, chunk):
            part = slice(first + i, first + i + chunk)
            out_ref[pl.ds(i, chunk), columns] = (
                soft[part] * terms_ref[pl.ds(2 * first + i, chunk), :]
                + hard[part] * terms_ref[pl.ds(2 * first + count + i, chunk), :]
            )


def loss_kernel(members, lines_ref, loss_ref):
    rows = lines_ref.shape[1]
    lines = shared_order(lines_ref[...], members)
    loss = jnp.sum(lines[0:1] + jnp.log(lines[1:2]) - lines[2:3], axis=1, keepdims=True) / rows
    loss_ref[...] = jnp.broadcast_to(loss, loss_ref.shape)


def frag_kernel(rows_one_ref, rows_two_ref, ids_one_ref, ids_two_ref, lines_ref, one_ref, two_ref, head_ref,
                global_ref, momentum_ref, peer_ref, new_global_ref, new_momentum_ref):
    logits = jnp.concatenate([one_ref[...], two_ref[...]], axis=0)
    held = jnp.concatenate([rows_one_ref[...], rows_two_ref[...]], axis=0)
    ids = jnp.concatenate([ids_of(ids_one_ref[...]), ids_of(ids_two_ref[...])], axis=0)
    rows, tile = logits.shape
    top, total = as_columns(lines_ref[0:1, :]), as_columns(lines_ref[1:2, :])
    offset = (lax.axis_index(AXIS) * pl.num_programs(0) + pl.program_id(0)) * tile
    hit = lax.broadcasted_iota(jnp.int32, (rows, tile), 1) == ids - offset
    shares = jnp.exp(logits - top) / total
    dlogits = ((shares - jnp.where(hit, 1.0, 0.0)) / rows).astype(jnp.bfloat16)
    turned = held.astype(jnp.float32).T.astype(jnp.bfloat16)
    frag_grad = jnp.dot(turned, dlogits, preferred_element_type=jnp.float32)
    local_frag = head_ref[...].astype(jnp.float32) - 1.0 * frag_grad
    pseudo = (global_ref[...] - local_frag + peer_ref[...]) / REPLICAS
    new_momentum = 0.9 * momentum_ref[...] + pseudo
    new_momentum_ref[...] = new_momentum
    new_global_ref[...] = global_ref[...] - 0.7 * (pseudo + 0.9 * new_momentum)


def frag_update(held, ids, lines, logits, near, global_frag, momentum, peer_delta):
    rows = lines.shape[1]
    width = near.shape[1]
    tile = pl.BlockSpec((FRAG, TILE), lambda i: (0, i))

    return pl.pallas_call(
        frag_kernel,
        grid=(width // TILE,),
        out_shape=[jax.ShapeDtypeStruct((FRAG, width), jnp.float32)] * 2,
        in_specs=[pl.BlockSpec((x.shape[0], FRAG), lambda i: (0, 0)) for x in held]
        + [
            pl.BlockSpec((x.shape[0], LANES), lambda i, last=x.shape[1] // LANES - 1: (0, last))
            for x in ids
        ]
        + [pl.BlockSpec((8, rows), lambda i: (0, 0))]
        + [pl.BlockSpec((x.shape[0], TILE), lambda i: (0, i)) for x in logits]
        + [tile] * 4,
        out_specs=[tile, tile],
        compiler_params=pltpu.CompilerParams(vmem_limit_bytes=16 * 2**20),
        cost_estimate=pl.CostEstimate(
            flops=2 * rows * FRAG * width, bytes_accessed=24 * FRAG * width, transcendentals=0
        ),
    )(
        *held, *ids, lines, *[pltpu.with_memory_space_constraint(x, pltpu.VMEM) for x in logits],
        pltpu.with_memory_space_constraint(near, pltpu.VMEM), global_frag, momentum, peer_delta,
    )


def swap(value, step):
    return lax.ppermute(value, AXIS, [(i, i ^ step) for i in range(lax.axis_size(AXIS))])


def far_steps():
    step = 4
    steps = []
    while step < lax.axis_size(AXIS):
        steps.append(step)
        step *= 2
    return steps


def gather_rows(packed):
    own = packed.shape[0]
    held = packed
    for step in far_steps():
        held = jnp.concatenate([held, swap(held, step)], axis=0)
    far = held[own:]
    near = jnp.concatenate([packed] + [swap(packed, step) for step in (1, 2, 3)], axis=0)
    far = jnp.stack([far] + [swap(far, step) for step in (1, 2, 3)])
    count = far.shape[1] // own
    return near, far.reshape(4, count, own, -1).swapaxes(0, 1).reshape(4 * count * own, -1)


def scatter_sums(grads_near, grads_far, own):
    blocks = [
        grads[i * own : (i + 1) * own]
        for grads in (grads_near, grads_far)
        for i in range(grads.shape[0] // own)
    ]
    members = len(blocks)

    def moved(parts, step):
        value = jnp.concatenate([part.astype(SEND) for part in parts], axis=0)
        value = swap(value, step).astype(jnp.float32)
        return [value[i * own : (i + 1) * own] for i in range(len(parts))]

    sums = blocks[::4]
    for part in (list(range(1, members // 4)), [0]):
        for step in (3, 2, 1):
            for i, value in zip(part, moved([blocks[4 * i + step] for i in part], step)):
                sums[i] = sums[i] + value
    for step in far_steps()[::-1]:
        keep = len(sums) // 2
        sums = [a + b for a, b in zip(sums[:keep], moved(sums[keep:], step))]
    return sums[0]


def body(hidden, targets, head, global_frag, momentum, peer_delta):
    members = lax.axis_size(AXIS)
    own, depth = hidden.shape
    rows = own * members
    width = head.shape[1]

    packed = call(
        pack_kernel, [((own, depth + LANES), hidden.dtype)], [targets, hidden],
        scratch=[pltpu.SMEM(targets.shape, targets.dtype), pltpu.SemaphoreType.DMA((2,))],
        sources=[pltpu.HBM, pltpu.HBM],
    )[0]
    rows_near, rows_far = gather_rows(packed)
    near = call(
        load_kernel, [(head.shape, head.dtype)], [head],
        scratch=[pltpu.SemaphoreType.DMA((4,))], sources=[pltpu.HBM],
    )[0]

    count = 4 * own
    near, logits_near, both_near, columns = call(
        first_kernel,
        [(head.shape, head.dtype), ((count, width), jnp.float32), ((2 * count, width), jnp.bfloat16),
         ((count, LANES), jnp.float32)],
        [rows_near, head, near], 2 * count * depth * width,
        scratch=[pltpu.SemaphoreType.DMA((4,))],
        sources=[pltpu.VMEM, pltpu.HBM, pltpu.VMEM], aliases={2: 0},
    )
    count = rows - 4 * own
    logits_far, both_far, mine = call(
        second_kernel,
        [((count, width), jnp.float32), ((2 * count, width), jnp.bfloat16), ((8, rows), jnp.float32)],
        [rows_far, near, columns], 2 * count * depth * width,
        scratch=[pltpu.VMEM((rows, LANES), jnp.float32)],
    )

    lines = mine
    for steps in [[step] for step in far_steps()] + [[1, 2, 3]]:
        before = lines
        lines = call(
            functools.partial(merge_kernel, steps, members),
            [((8, rows), jnp.float32)], [lines] + [swap(lines, step) for step in steps],
        )[0]

    terms = [
        call(
            functools.partial(grad_kernel, first),
            [((2 * rows, depth // 2), jnp.float32)], [both_near, both_far, near, *after],
            2 * rows * depth * width,
        )[0]
        for first, after in ((0, []), (depth // 2, [before]))
    ]

    scale = 2.0**14 * rows
    grads_far, grads_near = (
        call(
            functools.partial(join_kernel, scale, first),
            [((count, depth), jnp.float32)], [lines, mine] + terms,
        )[0]
        for first, count in ((4 * own, rows - 4 * own), (0, 4 * own))
    )
    hidden_grad = (scatter_sums(grads_near, grads_far, own) * (1.0 / scale)).astype(jnp.bfloat16)
    loss = call(functools.partial(loss_kernel, members), [((8, LANES), jnp.float32)], [lines])[0]
    new_global, new_momentum = frag_update(
        [rows_near, rows_far], [rows_near, rows_far], lines, [logits_near, logits_far], near,
        global_frag, momentum, peer_delta,
    )
    return (loss[0, :1], hidden_grad, new_global, new_momentum)


def solution(mesh):
    in_specs = (
        P(("outer", "vocab"), None),
        P(("outer", "vocab")),
        P("outer", "vocab"),
        P(None, "vocab"),
        P(None, "vocab"),
        P("outer", "vocab"),
    )
    out_specs = (P("outer"), P(("outer", "vocab"), None), P("outer", "vocab"), P("outer", "vocab"))
    return jax.shard_map(body, mesh=mesh, in_specs=in_specs, out_specs=out_specs, check_vma=False)
```

```python
import functools

import jax
import jax.numpy as jnp
from jax import lax
from jax.experimental import pallas as pl
from jax.experimental.pallas import tpu as pltpu
from jax.sharding import PartitionSpec as P

FRAG = 128
REPLICAS = 4
AXIS = "vocab"
SEND = jnp.float16
LANES = 128
VMEM = pl.BlockSpec(memory_space=pltpu.VMEM)


def call(kernel, outs, operands, flops=0, scratch=(), sources=None, vmem=16 * 2**20, aliases={}):
    outs = [pltpu.VMEM(shape, dtype) for shape, dtype in outs]
    places = sources or [pltpu.VMEM] * len(operands)
    moved = sum(x.size * x.dtype.itemsize for x in operands)
    return pl.pallas_call(
        kernel,
        out_shape=outs,
        in_specs=[pl.BlockSpec(memory_space=place) for place in places],
        out_specs=[VMEM] * len(outs),
        scratch_shapes=list(scratch),
        input_output_aliases=aliases,
        compiler_params=pltpu.CompilerParams(vmem_limit_bytes=vmem),
        cost_estimate=pl.CostEstimate(flops=flops, bytes_accessed=moved, transcendentals=0),
    )(*[pltpu.with_memory_space_constraint(x, place) for x, place in zip(operands, places)])


TILE = 512
WIDE = 1024


def pack_kernel(targets, rows, out_ref, targets_ref, sems):
    own, depth = rows.shape
    ids_copy = pltpu.make_async_copy(targets, targets_ref, sems.at[0])
    rows_copy = pltpu.make_async_copy(rows, out_ref.at[:, pl.ds(0, depth)], sems.at[1])
    ids_copy.start()
    rows_copy.start()
    ids_copy.wait()
    place = lax.broadcasted_iota(jnp.int32, (own, LANES), 0)
    ids = jnp.zeros((own, LANES), jnp.int32)
    for i in range(own):
        ids = jnp.where(place == i, targets_ref[i], ids)
    lane = lax.broadcasted_iota(jnp.int32, (own, LANES), 1)
    digits = jnp.where(lane == 0, ids // 256, ids % 256)
    out_ref[:, depth:] = digits.astype(jnp.float32).astype(jnp.bfloat16)
    rows_copy.wait()


def ids_of(digits):
    digits = digits.astype(jnp.float32)
    return (digits[:, 0:1] * 256.0 + digits[:, 1:2]).astype(jnp.int32)


def swap_blocks(value, group):
    size = value.shape[1]
    lane = lax.broadcasted_iota(jnp.int32, value.shape, 1)
    up, down = pltpu.roll(value, group, 1), pltpu.roll(value, size - group, 1)
    return jnp.where((lane & group) != 0, up, down)


def shared_order(value, members):
    me = lax.axis_index(AXIS)
    step = 1
    while step < members:
        swapped = swap_blocks(value, value.shape[1] // members * step)
        value = jnp.where((me & step) != 0, swapped, value)
        step *= 2
    return value


def as_columns(line):
    return jnp.broadcast_to(line, (LANES, line.shape[1])).T[:, 0:1]


def logits_of(rows_ref, near_ref, logits_ref, first, count):
    depth = near_ref.shape[0]

    @pl.loop(0, count // WIDE)
    def _(i):
        part = pl.ds(pl.multiple_of(first + i * WIDE, WIDE), WIDE)
        logits_ref[:, part] = jnp.dot(
            rows_ref[:, :depth], near_ref[:, part], preferred_element_type=jnp.float32
        )


def softmax_of(rows_ref, logits_ref, both_ref, columns_ref, first):
    rows, width = logits_ref.shape
    digits = rows_ref.shape[1] - LANES
    chunk = 32
    offset = lax.axis_index(AXIS) * width

    @pl.loop(0, rows // chunk)
    def _(i):
        part = pl.ds(pl.multiple_of(i * chunk, chunk), chunk)
        logits = logits_ref[part, :]
        ids = ids_of(rows_ref[part, digits:]) - offset
        hit = lax.broadcasted_iota(jnp.int32, logits.shape, 1) == ids
        top = jnp.max(logits, axis=1, keepdims=True)
        raised = jnp.exp(logits - top)
        total = jnp.sum(raised, axis=1, keepdims=True)
        pick = jnp.sum(jnp.where(hit, logits, 0.0), axis=1, keepdims=True)
        both_ref[part, :] = jnp.where(hit, 0.0, raised).astype(jnp.bfloat16)
        other = pl.ds(pl.multiple_of(rows + i * chunk, chunk), chunk)
        both_ref[other, :] = jnp.where(hit, 1.0, 0.0).astype(jnp.bfloat16)
        place = lax.broadcasted_iota(jnp.int32, (chunk, LANES), 1)
        slot = pl.ds(pl.multiple_of(first + i * chunk, chunk), chunk)
        columns_ref[slot, :] = jnp.where(place == 0, top, jnp.where(place == 1, total, pick))


def first_kernel(packed_ref, near_ref, logits_ref, both_ref, columns_ref):
    logits_of(packed_ref, near_ref, logits_ref, 0, near_ref.shape[1])
    softmax_of(packed_ref, logits_ref, both_ref, columns_ref, 0)


def second_kernel(rows_ref, near_ref, before_ref, logits_ref, both_ref, lines_ref, columns_ref):
    first = before_ref.shape[0]
    logits_of(rows_ref, near_ref, logits_ref, 0, near_ref.shape[1])
    softmax_of(rows_ref, logits_ref, both_ref, columns_ref, first)
    columns_ref[pl.ds(0, first), :] = before_ref[...]
    lines_ref[...] = columns_ref[...].T[:8]


def merge_kernel(steps, members, mine_ref, *refs):
    *other_refs, out_ref = refs
    block = mine_ref.shape[1] // members
    me = lax.axis_index(AXIS)
    groups = [mine_ref[...]]
    for step, other_ref in zip(steps, other_refs):
        other, bit = other_ref[...], 1
        while bit <= step:
            if step & bit:
                other = swap_blocks(other, block * bit)
            bit *= 2
        groups.append(other)
    unit, bit = steps[0], 1
    while bit < len(groups):
        upper = (me & (unit * bit)) != 0
        groups = [jnp.where(upper, groups[i ^ bit], group) for i, group in enumerate(groups)]
        bit *= 2
    top = functools.reduce(jnp.maximum, [group[0:1] for group in groups])
    total = sum(group[1:2] * jnp.exp(group[0:1] - top) for group in groups)
    pick = sum(group[2:3] for group in groups)
    place = lax.broadcasted_iota(jnp.int32, out_ref.shape, 0)
    out_ref[...] = jnp.where(place == 0, top, jnp.where(place == 1, total, pick))


def grad_kernel(first, one_ref, two_ref, near_ref, *refs):
    terms_ref = refs[-1]
    tile = 1024
    both = jnp.concatenate([one_ref[...], two_ref[...]], axis=0)
    for place in range(0, terms_ref.shape[1], tile):
        turned = lax.dot_general(
            near_ref[pl.ds(first + place, tile), :], both, (((1,), (1,)), ((), ())),
            preferred_element_type=jnp.float32,
        )
        terms_ref[:, pl.ds(place, tile)] = turned.T


def join_kernel(scale, first, lines_ref, mine_ref, *refs):
    *terms_refs, out_ref = refs
    rows = mine_ref.shape[1]
    top, total = lines_ref[0:1, :], lines_ref[1:2, :]
    soft = as_columns(jnp.exp(mine_ref[0:1, :] - top) / (total * rows)) * scale
    hard = (jnp.exp(mine_ref[2:3, :] - top) / total - 1.0) / rows
    hard = as_columns(hard.astype(jnp.bfloat16).astype(jnp.float32)) * scale

    count = out_ref.shape[0]
    chunk = min(count, 64)
    for place, terms_ref in enumerate(terms_refs):
        columns = pl.ds(place * terms_ref.shape[1], terms_ref.shape[1])
        for i in range(0, count, chunk):
            part = slice(first + i, first + i + chunk)
            out_ref[pl.ds(i, chunk), columns] = (
                soft[part] * terms_ref[pl.ds(2 * first + i, chunk), :]
                + hard[part] * terms_ref[pl.ds(2 * first + count + i, chunk), :]
            )


def loss_kernel(members, lines_ref, loss_ref):
    rows = lines_ref.shape[1]
    lines = shared_order(lines_ref[...], members)
    loss = jnp.sum(lines[0:1] + jnp.log(lines[1:2]) - lines[2:3], axis=1, keepdims=True) / rows
    loss_ref[...] = jnp.broadcast_to(loss, loss_ref.shape)


def frag_kernel(rows_one_ref, rows_two_ref, ids_one_ref, ids_two_ref, lines_ref, one_ref, two_ref, head_ref,
                global_ref, momentum_ref, peer_ref, new_global_ref, new_momentum_ref):
    logits = jnp.concatenate([one_ref[...], two_ref[...]], axis=0)
    held = jnp.concatenate([rows_one_ref[...], rows_two_ref[...]], axis=0)
    ids = jnp.concatenate([ids_of(ids_one_ref[...]), ids_of(ids_two_ref[...])], axis=0)
    rows, tile = logits.shape
    top, total = as_columns(lines_ref[0:1, :]), as_columns(lines_ref[1:2, :])
    offset = (lax.axis_index(AXIS) * pl.num_programs(0) + pl.program_id(0)) * tile
    hit = lax.broadcasted_iota(jnp.int32, (rows, tile), 1) == ids - offset
    shares = jnp.exp(logits - top) / total
    dlogits = ((shares - jnp.where(hit, 1.0, 0.0)) / rows).astype(jnp.bfloat16)
    turned = held.astype(jnp.float32).T.astype(jnp.bfloat16)
    frag_grad = jnp.dot(turned, dlogits, preferred_element_type=jnp.float32)
    local_frag = head_ref[...].astype(jnp.float32) - 1.0 * frag_grad
    pseudo = (global_ref[...] - local_frag + peer_ref[...]) / REPLICAS
    new_momentum = 0.9 * momentum_ref[...] + pseudo
    new_momentum_ref[...] = new_momentum
    new_global_ref[...] = global_ref[...] - 0.7 * (pseudo + 0.9 * new_momentum)


def frag_update(held, ids, lines, logits, near, global_frag, momentum, peer_delta):
    rows = lines.shape[1]
    width = near.shape[1]
    tile = pl.BlockSpec((FRAG, TILE), lambda i: (0, i))

    return pl.pallas_call(
        frag_kernel,
        grid=(width // TILE,),
        out_shape=[jax.ShapeDtypeStruct((FRAG, width), jnp.float32)] * 2,
        in_specs=[pl.BlockSpec((x.shape[0], FRAG), lambda i: (0, 0)) for x in held]
        + [
            pl.BlockSpec((x.shape[0], LANES), lambda i, last=x.shape[1] // LANES - 1: (0, last))
            for x in ids
        ]
        + [pl.BlockSpec((8, rows), lambda i: (0, 0))]
        + [pl.BlockSpec((x.shape[0], TILE), lambda i: (0, i)) for x in logits]
        + [tile] * 4,
        out_specs=[tile, tile],
        compiler_params=pltpu.CompilerParams(vmem_limit_bytes=16 * 2**20),
        cost_estimate=pl.CostEstimate(
            flops=2 * rows * FRAG * width, bytes_accessed=24 * FRAG * width, transcendentals=0
        ),
    )(
        *held, *ids, lines, *[pltpu.with_memory_space_constraint(x, pltpu.VMEM) for x in logits],
        pltpu.with_memory_space_constraint(near, pltpu.VMEM), global_frag, momentum, peer_delta,
    )


def swap(value, step):
    return lax.ppermute(value, AXIS, [(i, i ^ step) for i in range(lax.axis_size(AXIS))])


def far_steps():
    step = 4
    steps = []
    while step < lax.axis_size(AXIS):
        steps.append(step)
        step *= 2
    return steps


def relay_kernel(far_ref, near_ref, out_ref):
    out_ref[...] = far_ref[...]


def gather_rows(packed, near):
    own = packed.shape[0]
    held = packed
    for step in far_steps():
        held = jnp.concatenate([held, swap(held, step)], axis=0)
    far = held[own:]
    far = call(relay_kernel, [(far.shape, far.dtype)], [far, near])[0]
    near = jnp.concatenate([packed] + [swap(packed, step) for step in (1, 2, 3)], axis=0)
    far = jnp.stack([far] + [swap(far, step) for step in (1, 2, 3)])
    count = far.shape[1] // own
    return near, far.reshape(4, count, own, -1).swapaxes(0, 1).reshape(4 * count * own, -1)


def scatter_sums(grads_near, grads_far, own):
    blocks = [
        grads[i * own : (i + 1) * own]
        for grads in (grads_near, grads_far)
        for i in range(grads.shape[0] // own)
    ]
    members = len(blocks)

    def moved(parts, step):
        value = jnp.concatenate([part.astype(SEND) for part in parts], axis=0)
        value = swap(value, step).astype(jnp.float32)
        return [value[i * own : (i + 1) * own] for i in range(len(parts))]

    sums = blocks[::4]
    for part in (list(range(1, members // 4)), [0]):
        for step in (3, 2, 1):
            for i, value in zip(part, moved([blocks[4 * i + step] for i in part], step)):
                sums[i] = sums[i] + value
    for step in far_steps()[::-1]:
        keep = len(sums) // 2
        sums = [a + b for a, b in zip(sums[:keep], moved(sums[keep:], step))]
    return sums[0]


def body(hidden, targets, head, global_frag, momentum, peer_delta):
    members = lax.axis_size(AXIS)
    own, depth = hidden.shape
    rows = own * members
    width = head.shape[1]

    packed = call(
        pack_kernel, [((own, depth + LANES), hidden.dtype)], [targets, hidden],
        scratch=[pltpu.SMEM(targets.shape, targets.dtype), pltpu.SemaphoreType.DMA((2,))],
        sources=[pltpu.HBM, pltpu.HBM],
    )[0]
    near = swap(head, 0)
    rows_near, rows_far = gather_rows(packed, near)

    count = 4 * own
    logits_near, both_near, columns = call(
        first_kernel,
        [((count, width), jnp.float32), ((2 * count, width), jnp.bfloat16),
         ((count, LANES), jnp.float32)],
        [rows_near, near], 2 * count * depth * width,
    )
    count = rows - 4 * own
    logits_far, both_far, mine = call(
        second_kernel,
        [((count, width), jnp.float32), ((2 * count, width), jnp.bfloat16), ((8, rows), jnp.float32)],
        [rows_far, near, columns], 2 * count * depth * width,
        scratch=[pltpu.VMEM((rows, LANES), jnp.float32)],
    )

    lines = mine
    for steps in [[step] for step in far_steps()] + [[1, 2, 3]]:
        before = lines
        lines = call(
            functools.partial(merge_kernel, steps, members),
            [((8, rows), jnp.float32)], [lines] + [swap(lines, step) for step in steps],
        )[0]

    terms = [
        call(
            functools.partial(grad_kernel, first),
            [((2 * rows, depth // 2), jnp.float32)], [both_near, both_far, near, *after],
            2 * rows * depth * width,
        )[0]
        for first, after in ((0, []), (depth // 2, [before]))
    ]

    scale = 2.0**14 * rows
    grads_far, grads_near = (
        call(
            functools.partial(join_kernel, scale, first),
            [((count, depth), jnp.float32)], [lines, mine] + terms,
        )[0]
        for first, count in ((4 * own, rows - 4 * own), (0, 4 * own))
    )
    hidden_grad = (scatter_sums(grads_near, grads_far, own) * (1.0 / scale)).astype(jnp.bfloat16)
    loss = call(functools.partial(loss_kernel, members), [((8, LANES), jnp.float32)], [lines])[0]
    new_global, new_momentum = frag_update(
        [rows_near, rows_far], [rows_near, rows_far], lines, [logits_near, logits_far], near,
        global_frag, momentum, peer_delta,
    )
    return (loss[0, :1], hidden_grad, new_global, new_momentum)


def solution(mesh):
    in_specs = (
        P(("outer", "vocab"), None),
        P(("outer", "vocab")),
        P("outer", "vocab"),
        P(None, "vocab"),
        P(None, "vocab"),
        P("outer", "vocab"),
    )
    out_specs = (P("outer"), P(("outer", "vocab"), None), P("outer", "vocab"), P("outer", "vocab"))
    return jax.shard_map(body, mesh=mesh, in_specs=in_specs, out_specs=out_specs, check_vma=False)
```

```python
import functools

import jax
import jax.numpy as jnp
from jax import lax
from jax.experimental import pallas as pl
from jax.experimental.pallas import tpu as pltpu
from jax.sharding import PartitionSpec as P

FRAG = 128
REPLICAS = 4
AXIS = "vocab"
SEND = jnp.float16
LANES = 128
VMEM = pl.BlockSpec(memory_space=pltpu.VMEM)


def call(kernel, outs, operands, flops=0, scratch=(), sources=None, vmem=16 * 2**20, aliases={}):
    outs = [pltpu.VMEM(shape, dtype) for shape, dtype in outs]
    places = sources or [pltpu.VMEM] * len(operands)
    moved = sum(x.size * x.dtype.itemsize for x in operands)
    return pl.pallas_call(
        kernel,
        out_shape=outs,
        in_specs=[pl.BlockSpec(memory_space=place) for place in places],
        out_specs=[VMEM] * len(outs),
        scratch_shapes=list(scratch),
        input_output_aliases=aliases,
        compiler_params=pltpu.CompilerParams(vmem_limit_bytes=vmem),
        cost_estimate=pl.CostEstimate(flops=flops, bytes_accessed=moved, transcendentals=0),
    )(*[pltpu.with_memory_space_constraint(x, place) for x, place in zip(operands, places)])


def head_copies(source, target, sems, half):
    block = source.shape[0] // sems.shape[0]
    columns = pl.ds(half * (source.shape[1] // 2), source.shape[1] // 2)
    copies = []
    for i in range(sems.shape[0]):
        part = pl.ds(i * block, block)
        copies.append(pltpu.make_async_copy(source.at[part, columns], target.at[part, columns], sems.at[i]))
    return copies


def load_kernel(head, near_ref, sems):
    copies = head_copies(head, near_ref, sems, 0)
    for copy in copies:
        copy.start()
    for copy in copies:
        copy.wait()


TILE = 512
WIDE = 1024


def pack_kernel(targets, rows, out_ref, targets_ref, sems):
    own, depth = rows.shape
    ids_copy = pltpu.make_async_copy(targets, targets_ref, sems.at[0])
    rows_copy = pltpu.make_async_copy(rows, out_ref.at[:, pl.ds(0, depth)], sems.at[1])
    ids_copy.start()
    rows_copy.start()
    ids_copy.wait()
    place = lax.broadcasted_iota(jnp.int32, (own, LANES), 0)
    ids = jnp.zeros((own, LANES), jnp.int32)
    for i in range(own):
        ids = jnp.where(place == i, targets_ref[i], ids)
    lane = lax.broadcasted_iota(jnp.int32, (own, LANES), 1)
    digits = jnp.where(lane == 0, ids // 256, ids % 256)
    out_ref[:, depth:] = digits.astype(jnp.float32).astype(jnp.bfloat16)
    rows_copy.wait()


def ids_of(digits):
    digits = digits.astype(jnp.float32)
    return (digits[:, 0:1] * 256.0 + digits[:, 1:2]).astype(jnp.int32)


def swap_blocks(value, group):
    size = value.shape[1]
    lane = lax.broadcasted_iota(jnp.int32, value.shape, 1)
    up, down = pltpu.roll(value, group, 1), pltpu.roll(value, size - group, 1)
    return jnp.where((lane & group) != 0, up, down)


def shared_order(value, members):
    me = lax.axis_index(AXIS)
    step = 1
    while step < members:
        swapped = swap_blocks(value, value.shape[1] // members * step)
        value = jnp.where((me & step) != 0, swapped, value)
        step *= 2
    return value


def as_columns(line):
    return jnp.broadcast_to(line, (LANES, line.shape[1])).T[:, 0:1]


def logits_of(rows_ref, near_ref, logits_ref, first, count):
    depth = near_ref.shape[0]

    @pl.loop(0, count // WIDE)
    def _(i):
        part = pl.ds(pl.multiple_of(first + i * WIDE, WIDE), WIDE)
        logits_ref[:, part] = jnp.dot(
            rows_ref[:, :depth], near_ref[:, part], preferred_element_type=jnp.float32
        )


def softmax_of(rows_ref, logits_ref, both_ref, columns_ref, first):
    rows, width = logits_ref.shape
    digits = rows_ref.shape[1] - LANES
    chunk = 32
    offset = lax.axis_index(AXIS) * width

    @pl.loop(0, rows // chunk)
    def _(i):
        part = pl.ds(pl.multiple_of(i * chunk, chunk), chunk)
        logits = logits_ref[part, :]
        ids = ids_of(rows_ref[part, digits:]) - offset
        hit = lax.broadcasted_iota(jnp.int32, logits.shape, 1) == ids
        top = jnp.max(logits, axis=1, keepdims=True)
        raised = jnp.exp(logits - top)
        total = jnp.sum(raised, axis=1, keepdims=True)
        pick = jnp.sum(jnp.where(hit, logits, 0.0), axis=1, keepdims=True)
        both_ref[part, :] = jnp.where(hit, 0.0, raised).astype(jnp.bfloat16)
        other = pl.ds(pl.multiple_of(rows + i * chunk, chunk), chunk)
        both_ref[other, :] = jnp.where(hit, 1.0, 0.0).astype(jnp.bfloat16)
        place = lax.broadcasted_iota(jnp.int32, (chunk, LANES), 1)
        slot = pl.ds(pl.multiple_of(first + i * chunk, chunk), chunk)
        columns_ref[slot, :] = jnp.where(place == 0, top, jnp.where(place == 1, total, pick))


def first_kernel(packed_ref, head, held_ref, near_ref, logits_ref, both_ref, columns_ref, sems):
    half = near_ref.shape[1] // 2
    copies = head_copies(head, near_ref, sems, 1)
    for copy in copies:
        copy.start()
    logits_of(packed_ref, near_ref, logits_ref, 0, half)
    for copy in copies:
        copy.wait()
    logits_of(packed_ref, near_ref, logits_ref, half, half)
    softmax_of(packed_ref, logits_ref, both_ref, columns_ref, 0)


def second_kernel(rows_ref, near_ref, before_ref, logits_ref, both_ref, lines_ref, columns_ref):
    first = before_ref.shape[0]
    logits_of(rows_ref, near_ref, logits_ref, 0, near_ref.shape[1])
    softmax_of(rows_ref, logits_ref, both_ref, columns_ref, first)
    columns_ref[pl.ds(0, first), :] = before_ref[...]
    lines_ref[...] = columns_ref[...].T[:8]


def merge_kernel(steps, members, mine_ref, *refs):
    *other_refs, out_ref = refs
    block = mine_ref.shape[1] // members
    me = lax.axis_index(AXIS)
    groups = [mine_ref[...]]
    for step, other_ref in zip(steps, other_refs):
        other, bit = other_ref[...], 1
        while bit <= step:
            if step & bit:
                other = swap_blocks(other, block * bit)
            bit *= 2
        groups.append(other)
    unit, bit = steps[0], 1
    while bit < len(groups):
        upper = (me & (unit * bit)) != 0
        groups = [jnp.where(upper, groups[i ^ bit], group) for i, group in enumerate(groups)]
        bit *= 2
    top = functools.reduce(jnp.maximum, [group[0:1] for group in groups])
    total = sum(group[1:2] * jnp.exp(group[0:1] - top) for group in groups)
    pick = sum(group[2:3] for group in groups)
    place = lax.broadcasted_iota(jnp.int32, out_ref.shape, 0)
    out_ref[...] = jnp.where(place == 0, top, jnp.where(place == 1, total, pick))


def grad_kernel(first, one_ref, two_ref, near_ref, *refs):
    terms_ref = refs[-1]
    tile = min(terms_ref.shape[1], 2**20 // (one_ref.shape[0] + two_ref.shape[0]) // 2)
    both = jnp.concatenate([one_ref[...], two_ref[...]], axis=0)
    for place in range(0, terms_ref.shape[1], tile):
        turned = lax.dot_general(
            near_ref[pl.ds(first + place, tile), :], both, (((1,), (1,)), ((), ())),
            preferred_element_type=jnp.float32,
        )
        terms_ref[:, pl.ds(place, tile)] = turned.T


def join_kernel(scale, first, lines_ref, mine_ref, *refs):
    *terms_refs, out_ref = refs
    rows = mine_ref.shape[1]
    top, total = lines_ref[0:1, :], lines_ref[1:2, :]
    soft = as_columns(jnp.exp(mine_ref[0:1, :] - top) / (total * rows)) * scale
    hard = (jnp.exp(mine_ref[2:3, :] - top) / total - 1.0) / rows
    hard = as_columns(hard.astype(jnp.bfloat16).astype(jnp.float32)) * scale

    count = out_ref.shape[0]
    chunk = min(count, 64)
    end = sum(terms_ref.shape[1] for terms_ref in terms_refs)
    out_ref[:, end:] = jnp.zeros((count, out_ref.shape[1] - end), jnp.float32)
    for place, terms_ref in enumerate(terms_refs):
        columns = pl.ds(place * terms_ref.shape[1], terms_ref.shape[1])
        for i in range(0, count, chunk):
            part = slice(first + i, first + i + chunk)
            out_ref[pl.ds(i, chunk), columns] = (
                soft[part] * terms_ref[pl.ds(2 * first + i, chunk), :]
                + hard[part] * terms_ref[pl.ds(2 * first + count + i, chunk), :]
            )


def loss_kernel(members, lines_ref, loss_ref):
    rows = lines_ref.shape[1]
    lines = shared_order(lines_ref[...], members)
    loss = jnp.sum(lines[0:1] + jnp.log(lines[1:2]) - lines[2:3], axis=1, keepdims=True) / rows
    loss_ref[...] = jnp.broadcast_to(loss, loss_ref.shape)


def frag_kernel(rows_one_ref, rows_two_ref, ids_one_ref, ids_two_ref, lines_ref, one_ref, two_ref, head_ref,
                global_ref, momentum_ref, peer_ref, new_global_ref, new_momentum_ref):
    logits = jnp.concatenate([one_ref[...], two_ref[...]], axis=0)
    held = jnp.concatenate([rows_one_ref[...], rows_two_ref[...]], axis=0)
    ids = jnp.concatenate([ids_of(ids_one_ref[...]), ids_of(ids_two_ref[...])], axis=0)
    rows, tile = logits.shape
    top, total = as_columns(lines_ref[0:1, :]), as_columns(lines_ref[1:2, :])
    offset = (lax.axis_index(AXIS) * pl.num_programs(0) + pl.program_id(0)) * tile
    hit = lax.broadcasted_iota(jnp.int32, (rows, tile), 1) == ids - offset
    shares = jnp.exp(logits - top) / total
    dlogits = ((shares - jnp.where(hit, 1.0, 0.0)) / rows).astype(jnp.bfloat16)
    turned = held.astype(jnp.float32).T.astype(jnp.bfloat16)
    frag_grad = jnp.dot(turned, dlogits, preferred_element_type=jnp.float32)
    local_frag = head_ref[...].astype(jnp.float32) - 1.0 * frag_grad
    pseudo = (global_ref[...] - local_frag + peer_ref[...]) / REPLICAS
    new_momentum = 0.9 * momentum_ref[...] + pseudo
    new_momentum_ref[...] = new_momentum
    new_global_ref[...] = global_ref[...] - 0.7 * (pseudo + 0.9 * new_momentum)


def frag_update(held, ids, lines, logits, near, global_frag, momentum, peer_delta):
    rows = lines.shape[1]
    width = near.shape[1]
    tile = pl.BlockSpec((FRAG, TILE), lambda i: (0, i))

    return pl.pallas_call(
        frag_kernel,
        grid=(width // TILE,),
        out_shape=[jax.ShapeDtypeStruct((FRAG, width), jnp.float32)] * 2,
        in_specs=[pl.BlockSpec((x.shape[0], FRAG), lambda i: (0, 0)) for x in held]
        + [
            pl.BlockSpec((x.shape[0], LANES), lambda i, last=x.shape[1] // LANES - 1: (0, last))
            for x in ids
        ]
        + [pl.BlockSpec((8, rows), lambda i: (0, 0))]
        + [pl.BlockSpec((x.shape[0], TILE), lambda i: (0, i)) for x in logits]
        + [tile] * 4,
        out_specs=[tile, tile],
        compiler_params=pltpu.CompilerParams(vmem_limit_bytes=16 * 2**20),
        cost_estimate=pl.CostEstimate(
            flops=2 * rows * FRAG * width, bytes_accessed=24 * FRAG * width, transcendentals=0
        ),
    )(
        *held, *ids, lines, *[pltpu.with_memory_space_constraint(x, pltpu.VMEM) for x in logits],
        pltpu.with_memory_space_constraint(near, pltpu.VMEM), global_frag, momentum, peer_delta,
    )


def swap(value, step):
    return lax.ppermute(value, AXIS, [(i, i ^ step) for i in range(lax.axis_size(AXIS))])


def far_steps():
    step = 4
    steps = []
    while step < lax.axis_size(AXIS):
        steps.append(step)
        step *= 2
    return steps


def gather_rows(packed):
    own = packed.shape[0]
    held = packed
    for step in far_steps():
        held = jnp.concatenate([held, swap(held, step)], axis=0)
    far = held[own:]
    near = jnp.concatenate([packed] + [swap(packed, step) for step in (1, 2, 3)], axis=0)
    far = jnp.stack([far] + [swap(far, step) for step in (1, 2, 3)])
    count = far.shape[1] // own
    return near, far.reshape(4, count, own, -1).swapaxes(0, 1).reshape(4 * count * own, -1)


def scatter_sums(grads_near, grads_far, own, depth):
    blocks = [
        grads[i * own : (i + 1) * own]
        for grads in (grads_near, grads_far)
        for i in range(grads.shape[0] // own)
    ]
    members = len(blocks)

    def moved(parts, step, longer=0):
        value = jnp.concatenate([part[:, : depth + longer * LANES].astype(SEND) for part in parts], axis=0)
        value = swap(value, step)[:, :depth].astype(jnp.float32)
        return [value[i * own : (i + 1) * own] for i in range(len(parts))]

    sums = [block[:, :depth] for block in blocks[::4]]
    for part, longer in ((list(range(1, members // 4)), (2, 1, 0)), ([0], (0, 1, 2))):
        for step, more in zip((3, 2, 1), longer):
            for i, value in zip(part, moved([blocks[4 * i + step] for i in part], step, more)):
                sums[i] = sums[i] + value
    for step in far_steps()[::-1]:
        keep = len(sums) // 2
        sums = [a + b for a, b in zip(sums[:keep], moved(sums[keep:], step))]
    return sums[0]


def body(hidden, targets, head, global_frag, momentum, peer_delta):
    members = lax.axis_size(AXIS)
    own, depth = hidden.shape
    rows = own * members
    width = head.shape[1]

    packed = call(
        pack_kernel, [((own, depth + LANES), hidden.dtype)], [targets, hidden],
        scratch=[pltpu.SMEM(targets.shape, targets.dtype), pltpu.SemaphoreType.DMA((2,))],
        sources=[pltpu.HBM, pltpu.HBM],
    )[0]
    rows_near, rows_far = gather_rows(packed)
    near = call(
        load_kernel, [(head.shape, head.dtype)], [head],
        scratch=[pltpu.SemaphoreType.DMA((4,))], sources=[pltpu.HBM],
    )[0]

    count = 4 * own
    near, logits_near, both_near, columns = call(
        first_kernel,
        [(head.shape, head.dtype), ((count, width), jnp.float32), ((2 * count, width), jnp.bfloat16),
         ((count, LANES), jnp.float32)],
        [rows_near, head, near], 2 * count * depth * width,
        scratch=[pltpu.SemaphoreType.DMA((4,))],
        sources=[pltpu.VMEM, pltpu.HBM, pltpu.VMEM], aliases={2: 0},
    )
    count = rows - 4 * own
    logits_far, both_far, mine = call(
        second_kernel,
        [((count, width), jnp.float32), ((2 * count, width), jnp.bfloat16), ((8, rows), jnp.float32)],
        [rows_far, near, columns], 2 * count * depth * width,
        scratch=[pltpu.VMEM((rows, LANES), jnp.float32)],
    )

    lines = mine
    for steps in [[step] for step in far_steps()] + [[1, 2, 3]]:
        before = lines
        lines = call(
            functools.partial(merge_kernel, steps, members),
            [((8, rows), jnp.float32)], [lines] + [swap(lines, step) for step in steps],
        )[0]

    terms = [
        call(
            functools.partial(grad_kernel, first),
            [((2 * rows, depth // 2), jnp.float32)], [both_near, both_far, near, *after],
            2 * rows * depth * width,
        )[0]
        for first, after in ((0, []), (depth // 2, [before]))
    ]

    scale = 2.0**14 * rows
    grads_far, grads_near = (
        call(
            functools.partial(join_kernel, scale, first),
            [((count, depth + 2 * LANES), jnp.float32)], [lines, mine] + terms,
        )[0]
        for first, count in ((4 * own, rows - 4 * own), (0, 4 * own))
    )
    hidden_grad = (scatter_sums(grads_near, grads_far, own, depth) * (1.0 / scale)).astype(jnp.bfloat16)
    loss = call(functools.partial(loss_kernel, members), [((8, LANES), jnp.float32)], [lines])[0]
    new_global, new_momentum = frag_update(
        [rows_near, rows_far], [rows_near, rows_far], lines, [logits_near, logits_far], near,
        global_frag, momentum, peer_delta,
    )
    return (loss[0, :1], hidden_grad, new_global, new_momentum)


def solution(mesh):
    in_specs = (
        P(("outer", "vocab"), None),
        P(("outer", "vocab")),
        P("outer", "vocab"),
        P(None, "vocab"),
        P(None, "vocab"),
        P("outer", "vocab"),
    )
    out_specs = (P("outer"), P(("outer", "vocab"), None), P("outer", "vocab"), P("outer", "vocab"))
    return jax.shard_map(body, mesh=mesh, in_specs=in_specs, out_specs=out_specs, check_vma=False)
```

```python
import functools

import jax
import jax.numpy as jnp
from jax import lax
from jax.experimental import pallas as pl
from jax.experimental.pallas import tpu as pltpu
from jax.sharding import PartitionSpec as P

FRAG = 128
REPLICAS = 4
AXIS = "vocab"
SEND = jnp.float16
LANES = 128
VMEM = pl.BlockSpec(memory_space=pltpu.VMEM)


def call(kernel, outs, operands, flops=0, scratch=(), sources=None, vmem=16 * 2**20, aliases={}):
    outs = [pltpu.VMEM(shape, dtype) for shape, dtype in outs]
    places = sources or [pltpu.VMEM] * len(operands)
    moved = sum(x.size * x.dtype.itemsize for x in operands)
    return pl.pallas_call(
        kernel,
        out_shape=outs,
        in_specs=[pl.BlockSpec(memory_space=place) for place in places],
        out_specs=[VMEM] * len(outs),
        scratch_shapes=list(scratch),
        input_output_aliases=aliases,
        compiler_params=pltpu.CompilerParams(vmem_limit_bytes=vmem),
        cost_estimate=pl.CostEstimate(flops=flops, bytes_accessed=moved, transcendentals=0),
    )(*[pltpu.with_memory_space_constraint(x, place) for x, place in zip(operands, places)])


def head_copies(source, target, sems, half):
    block = source.shape[0] // sems.shape[0]
    columns = pl.ds(half * (source.shape[1] // 2), source.shape[1] // 2)
    copies = []
    for i in range(sems.shape[0]):
        part = pl.ds(i * block, block)
        copies.append(pltpu.make_async_copy(source.at[part, columns], target.at[part, columns], sems.at[i]))
    return copies


def load_kernel(head, near_ref, sems):
    copies = head_copies(head, near_ref, sems, 0)
    for copy in copies:
        copy.start()
    for copy in copies:
        copy.wait()


TILE = 512
WIDE = 1024


def pack_kernel(targets, rows, out_ref, targets_ref, sems):
    own, depth = rows.shape
    ids_copy = pltpu.make_async_copy(targets, targets_ref, sems.at[0])
    rows_copy = pltpu.make_async_copy(rows, out_ref.at[:, pl.ds(0, depth)], sems.at[1])
    ids_copy.start()
    rows_copy.start()
    ids_copy.wait()
    place = lax.broadcasted_iota(jnp.int32, (own, LANES), 0)
    ids = jnp.zeros((own, LANES), jnp.int32)
    for i in range(own):
        ids = jnp.where(place == i, targets_ref[i], ids)
    lane = lax.broadcasted_iota(jnp.int32, (own, LANES), 1)
    digits = jnp.where(lane == 0, ids // 256, ids % 256)
    out_ref[:, depth:] = digits.astype(jnp.float32).astype(jnp.bfloat16)
    rows_copy.wait()


def ids_of(digits):
    digits = digits.astype(jnp.float32)
    return (digits[:, 0:1] * 256.0 + digits[:, 1:2]).astype(jnp.int32)


def swap_blocks(value, group):
    size = value.shape[1]
    lane = lax.broadcasted_iota(jnp.int32, value.shape, 1)
    up, down = pltpu.roll(value, group, 1), pltpu.roll(value, size - group, 1)
    return jnp.where((lane & group) != 0, up, down)


def shared_order(value, members):
    me = lax.axis_index(AXIS)
    step = 1
    while step < members:
        swapped = swap_blocks(value, value.shape[1] // members * step)
        value = jnp.where((me & step) != 0, swapped, value)
        step *= 2
    return value


def as_columns(line):
    return jnp.broadcast_to(line, (LANES, line.shape[1])).T[:, 0:1]


def logits_of(rows_ref, near_ref, logits_ref, first, count):
    depth = near_ref.shape[0]

    @pl.loop(0, count // WIDE)
    def _(i):
        part = pl.ds(pl.multiple_of(first + i * WIDE, WIDE), WIDE)
        logits_ref[:, part] = jnp.dot(
            rows_ref[:, :depth], near_ref[:, part], preferred_element_type=jnp.float32
        )


def softmax_of(rows_ref, logits_ref, both_ref, columns_ref, first):
    rows, width = logits_ref.shape
    digits = rows_ref.shape[1] - LANES
    chunk = 16
    offset = lax.axis_index(AXIS) * width

    @pl.loop(0, rows // chunk)
    def _(i):
        part = pl.ds(pl.multiple_of(i * chunk, chunk), chunk)
        logits = logits_ref[part, :]
        ids = ids_of(rows_ref[part, digits:]) - offset
        hit = lax.broadcasted_iota(jnp.int32, logits.shape, 1) == ids
        top = jnp.max(logits, axis=1, keepdims=True)
        raised = jnp.exp(logits - top)
        total = jnp.sum(raised, axis=1, keepdims=True)
        pick = jnp.sum(jnp.where(hit, logits, 0.0), axis=1, keepdims=True)
        both_ref[part, :] = jnp.where(hit, 0.0, raised).astype(jnp.bfloat16)
        other = pl.ds(pl.multiple_of(rows + i * chunk, chunk), chunk)
        both_ref[other, :] = jnp.where(hit, 1.0, 0.0).astype(jnp.bfloat16)
        place = lax.broadcasted_iota(jnp.int32, (chunk, LANES), 1)
        slot = pl.ds(pl.multiple_of(first + i * chunk, chunk), chunk)
        columns_ref[slot, :] = jnp.where(place == 0, top, jnp.where(place == 1, total, pick))


def first_kernel(packed_ref, head, held_ref, near_ref, logits_ref, both_ref, columns_ref, sems):
    half = near_ref.shape[1] // 2
    copies = head_copies(head, near_ref, sems, 1)
    for copy in copies:
        copy.start()
    logits_of(packed_ref, near_ref, logits_ref, 0, half)
    for copy in copies:
        copy.wait()
    logits_of(packed_ref, near_ref, logits_ref, half, half)
    softmax_of(packed_ref, logits_ref, both_ref, columns_ref, 0)


def second_kernel(rows_ref, near_ref, before_ref, logits_ref, both_ref, lines_ref, columns_ref):
    first = before_ref.shape[0]
    logits_of(rows_ref, near_ref, logits_ref, 0, near_ref.shape[1])
    softmax_of(rows_ref, logits_ref, both_ref, columns_ref, first)
    columns_ref[pl.ds(0, first), :] = before_ref[...]
    lines_ref[...] = columns_ref[...].T[:8]


def merge_kernel(steps, members, mine_ref, *refs):
    *other_refs, out_ref = refs
    block = mine_ref.shape[1] // members
    me = lax.axis_index(AXIS)
    groups = [mine_ref[...]]
    for step, other_ref in zip(steps, other_refs):
        other, bit = other_ref[...], 1
        while bit <= step:
            if step & bit:
                other = swap_blocks(other, block * bit)
            bit *= 2
        groups.append(other)
    unit, bit = steps[0], 1
    while bit < len(groups):
        upper = (me & (unit * bit)) != 0
        groups = [jnp.where(upper, groups[i ^ bit], group) for i, group in enumerate(groups)]
        bit *= 2
    top = functools.reduce(jnp.maximum, [group[0:1] for group in groups])
    total = sum(group[1:2] * jnp.exp(group[0:1] - top) for group in groups)
    pick = sum(group[2:3] for group in groups)
    place = lax.broadcasted_iota(jnp.int32, out_ref.shape, 0)
    out_ref[...] = jnp.where(place == 0, top, jnp.where(place == 1, total, pick))


def grad_kernel(first, one_ref, two_ref, near_ref, *refs):
    terms_ref = refs[-1]
    tile = min(terms_ref.shape[1], 2**20 // (one_ref.shape[0] + two_ref.shape[0]) // 2)
    both = jnp.concatenate([one_ref[...], two_ref[...]], axis=0)
    for place in range(0, terms_ref.shape[1], tile):
        turned = lax.dot_general(
            near_ref[pl.ds(first + place, tile), :], both, (((1,), (1,)), ((), ())),
            preferred_element_type=jnp.float32,
        )
        terms_ref[:, pl.ds(place, tile)] = turned.T


def join_kernel(scale, first, head_rows, lines_ref, mine_ref, *refs):
    *terms_refs, out_ref = refs
    rows = mine_ref.shape[1]
    top, total = lines_ref[0:1, :], lines_ref[1:2, :]
    soft = as_columns(jnp.exp(mine_ref[0:1, :] - top) / (total * rows)) * scale
    hard = (jnp.exp(mine_ref[2:3, :] - top) / total - 1.0) / rows
    hard = as_columns(hard.astype(jnp.bfloat16).astype(jnp.float32)) * scale

    chunk = 16
    for place, terms_ref in enumerate(terms_refs):
        columns = pl.ds(place * terms_ref.shape[1], terms_ref.shape[1])
        for i in range(0, out_ref.shape[0], chunk):
            at = first + i
            part = slice(at, at + chunk)
            held, other = (at, head_rows) if at < head_rows else (head_rows + at, rows - head_rows)
            out_ref[pl.ds(i, chunk), columns] = (
                soft[part] * terms_ref[pl.ds(held, chunk), :]
                + hard[part] * terms_ref[pl.ds(held + other, chunk), :]
            )


def loss_kernel(members, lines_ref, loss_ref):
    rows = lines_ref.shape[1]
    lines = shared_order(lines_ref[...], members)
    loss = jnp.sum(lines[0:1] + jnp.log(lines[1:2]) - lines[2:3], axis=1, keepdims=True) / rows
    loss_ref[...] = jnp.broadcast_to(loss, loss_ref.shape)


def frag_kernel(rows_one_ref, rows_two_ref, ids_one_ref, ids_two_ref, lines_ref, one_ref, two_ref, head_ref,
                global_ref, momentum_ref, peer_ref, new_global_ref, new_momentum_ref):
    logits = jnp.concatenate([one_ref[...], two_ref[...]], axis=0)
    held = jnp.concatenate([rows_one_ref[...], rows_two_ref[...]], axis=0)
    ids = jnp.concatenate([ids_of(ids_one_ref[...]), ids_of(ids_two_ref[...])], axis=0)
    rows, tile = logits.shape
    top, total = as_columns(lines_ref[0:1, :]), as_columns(lines_ref[1:2, :])
    offset = (lax.axis_index(AXIS) * pl.num_programs(0) + pl.program_id(0)) * tile
    hit = lax.broadcasted_iota(jnp.int32, (rows, tile), 1) == ids - offset
    shares = jnp.exp(logits - top) / total
    dlogits = ((shares - jnp.where(hit, 1.0, 0.0)) / rows).astype(jnp.bfloat16)
    turned = held.astype(jnp.float32).T.astype(jnp.bfloat16)
    frag_grad = jnp.dot(turned, dlogits, preferred_element_type=jnp.float32)
    local_frag = head_ref[...].astype(jnp.float32) - 1.0 * frag_grad
    pseudo = (global_ref[...] - local_frag + peer_ref[...]) / REPLICAS
    new_momentum = 0.9 * momentum_ref[...] + pseudo
    new_momentum_ref[...] = new_momentum
    new_global_ref[...] = global_ref[...] - 0.7 * (pseudo + 0.9 * new_momentum)


def frag_update(held, ids, lines, logits, near, global_frag, momentum, peer_delta):
    rows = lines.shape[1]
    width = near.shape[1]
    tile = pl.BlockSpec((FRAG, TILE), lambda i: (0, i))

    return pl.pallas_call(
        frag_kernel,
        grid=(width // TILE,),
        out_shape=[jax.ShapeDtypeStruct((FRAG, width), jnp.float32)] * 2,
        in_specs=[pl.BlockSpec((x.shape[0], FRAG), lambda i: (0, 0)) for x in held]
        + [
            pl.BlockSpec((x.shape[0], LANES), lambda i, last=x.shape[1] // LANES - 1: (0, last))
            for x in ids
        ]
        + [pl.BlockSpec((8, rows), lambda i: (0, 0))]
        + [pl.BlockSpec((x.shape[0], TILE), lambda i: (0, i)) for x in logits]
        + [tile] * 4,
        out_specs=[tile, tile],
        compiler_params=pltpu.CompilerParams(vmem_limit_bytes=16 * 2**20),
        cost_estimate=pl.CostEstimate(
            flops=2 * rows * FRAG * width, bytes_accessed=24 * FRAG * width, transcendentals=0
        ),
    )(
        *held, *ids, lines, *[pltpu.with_memory_space_constraint(x, pltpu.VMEM) for x in logits],
        pltpu.with_memory_space_constraint(near, pltpu.VMEM), global_frag, momentum, peer_delta,
    )


def swap(value, step):
    return lax.ppermute(value, AXIS, [(i, i ^ step) for i in range(lax.axis_size(AXIS))])


def far_steps():
    step = 4
    steps = []
    while step < lax.axis_size(AXIS):
        steps.append(step)
        step *= 2
    return steps


def gather_rows(packed):
    own = packed.shape[0]
    held = packed
    for step in far_steps():
        held = jnp.concatenate([held, swap(held, step)], axis=0)
    far = held[own:]
    count = far.shape[0] // own
    z_near, y_near = swap(packed, 2), swap(packed, 1)
    both = swap(jnp.concatenate([far, z_near], axis=0), 1)
    parts = [far, both[: count * own], swap(far, 2), swap(far, 3)]
    others = jnp.stack(parts).reshape(4, count, own, -1).swapaxes(0, 1).reshape(4 * count * own, -1)
    return (
        jnp.concatenate([packed, y_near, z_near], axis=0),
        jnp.concatenate([both[count * own :], others], axis=0),
    )


def scatter_sums(grads_near, grads_far, own):
    blocks = [
        grads[i * own : (i + 1) * own]
        for grads in (grads_near, grads_far)
        for i in range(grads.shape[0] // own)
    ]
    far = range(4, len(blocks), 4)

    def moved(parts, step):
        value = jnp.concatenate([part.astype(SEND) for part in parts], axis=0)
        value = swap(value, step).astype(jnp.float32)
        return [value[i * own : (i + 1) * own] for i in range(len(parts))]

    *one, z_near = moved([blocks[i ^ 1] for i in far] + [blocks[3]], 1)
    three = moved([blocks[i ^ 3] for i in far], 3)
    two = moved([blocks[i ^ 2] for i in far], 2)
    sums = [blocks[0]] + [blocks[i] + a + b + c for i, a, b, c in zip(far, one, two, three)]
    y_near = moved([blocks[1]], 1)[0]
    z_near = moved([blocks[2] + z_near], 2)[0]
    sums[0] = sums[0] + y_near + z_near
    for step in far_steps()[::-1]:
        keep = len(sums) // 2
        sums = [a + b for a, b in zip(sums[:keep], moved(sums[keep:], step))]
    return sums[0]


def body(hidden, targets, head, global_frag, momentum, peer_delta):
    members = lax.axis_size(AXIS)
    own, depth = hidden.shape
    rows = own * members
    width = head.shape[1]

    packed = call(
        pack_kernel, [((own, depth + LANES), hidden.dtype)], [targets, hidden],
        scratch=[pltpu.SMEM(targets.shape, targets.dtype), pltpu.SemaphoreType.DMA((2,))],
        sources=[pltpu.HBM, pltpu.HBM],
    )[0]
    rows_near, rows_far = gather_rows(packed)
    near = call(
        load_kernel, [(head.shape, head.dtype)], [head],
        scratch=[pltpu.SemaphoreType.DMA((4,))], sources=[pltpu.HBM],
    )[0]

    count = 3 * own
    near, logits_near, both_near, columns = call(
        first_kernel,
        [(head.shape, head.dtype), ((count, width), jnp.float32), ((2 * count, width), jnp.bfloat16),
         ((count, LANES), jnp.float32)],
        [rows_near, head, near], 2 * count * depth * width,
        scratch=[pltpu.SemaphoreType.DMA((4,))],
        sources=[pltpu.VMEM, pltpu.HBM, pltpu.VMEM], aliases={2: 0},
    )
    count = rows - 3 * own
    logits_far, both_far, mine = call(
        second_kernel,
        [((count, width), jnp.float32), ((2 * count, width), jnp.bfloat16), ((8, rows), jnp.float32)],
        [rows_far, near, columns], 2 * count * depth * width,
        scratch=[pltpu.VMEM((rows, LANES), jnp.float32)],
    )

    lines = mine
    for steps in [[step] for step in far_steps()] + [[1, 2, 3]]:
        before = lines
        lines = call(
            functools.partial(merge_kernel, steps, members),
            [((8, rows), jnp.float32)], [lines] + [swap(lines, step) for step in steps],
        )[0]

    terms = [
        call(
            functools.partial(grad_kernel, first),
            [((2 * rows, depth // 2), jnp.float32)], [both_near, both_far, near, *after],
            2 * rows * depth * width,
        )[0]
        for first, after in ((0, []), (depth // 2, [before]))
    ]

    scale = 2.0**14 * rows
    grads_far, grads_near = (
        call(
            functools.partial(join_kernel, scale, first, 3 * own),
            [((count, depth), jnp.float32)], [lines, mine] + terms,
        )[0]
        for first, count in ((2 * own, rows - 2 * own), (0, 2 * own))
    )
    hidden_grad = (scatter_sums(grads_near, grads_far, own) * (1.0 / scale)).astype(jnp.bfloat16)
    loss = call(functools.partial(loss_kernel, members), [((8, LANES), jnp.float32)], [lines])[0]
    new_global, new_momentum = frag_update(
        [rows_near, rows_far], [rows_near, rows_far], lines, [logits_near, logits_far], near,
        global_frag, momentum, peer_delta,
    )
    return (loss[0, :1], hidden_grad, new_global, new_momentum)


def solution(mesh):
    in_specs = (
        P(("outer", "vocab"), None),
        P(("outer", "vocab")),
        P("outer", "vocab"),
        P(None, "vocab"),
        P(None, "vocab"),
        P("outer", "vocab"),
    )
    out_specs = (P("outer"), P(("outer", "vocab"), None), P("outer", "vocab"), P("outer", "vocab"))
    return jax.shard_map(body, mesh=mesh, in_specs=in_specs, out_specs=out_specs, check_vma=False)
```

```python
import functools

import jax
import jax.numpy as jnp
from jax import lax
from jax.experimental import pallas as pl
from jax.experimental.pallas import tpu as pltpu
from jax.sharding import PartitionSpec as P

FRAG = 128
REPLICAS = 4
AXIS = "vocab"
SEND = jnp.float16
LANES = 128
VMEM = pl.BlockSpec(memory_space=pltpu.VMEM)


def call(kernel, outs, operands, flops=0, scratch=(), sources=None, vmem=16 * 2**20, aliases={}):
    outs = [pltpu.VMEM(shape, dtype) for shape, dtype in outs]
    places = sources or [pltpu.VMEM] * len(operands)
    moved = sum(x.size * x.dtype.itemsize for x in operands)
    return pl.pallas_call(
        kernel,
        out_shape=outs,
        in_specs=[pl.BlockSpec(memory_space=place) for place in places],
        out_specs=[VMEM] * len(outs),
        scratch_shapes=list(scratch),
        input_output_aliases=aliases,
        compiler_params=pltpu.CompilerParams(vmem_limit_bytes=vmem),
        cost_estimate=pl.CostEstimate(flops=flops, bytes_accessed=moved, transcendentals=0),
    )(*[pltpu.with_memory_space_constraint(x, place) for x, place in zip(operands, places)])


def head_copies(source, target, sems, half):
    block = source.shape[0] // sems.shape[0]
    columns = pl.ds(half * (source.shape[1] // 2), source.shape[1] // 2)
    copies = []
    for i in range(sems.shape[0]):
        part = pl.ds(i * block, block)
        copies.append(pltpu.make_async_copy(source.at[part, columns], target.at[part, columns], sems.at[i]))
    return copies


def load_kernel(head, near_ref, sems):
    copies = head_copies(head, near_ref, sems, 0)
    for copy in copies:
        copy.start()
    for copy in copies:
        copy.wait()


TILE = 512
WIDE = 1024


def pack_kernel(targets, rows, out_ref, targets_ref, sems):
    own, depth = rows.shape
    ids_copy = pltpu.make_async_copy(targets, targets_ref, sems.at[0])
    rows_copy = pltpu.make_async_copy(rows, out_ref.at[:, pl.ds(0, depth)], sems.at[1])
    ids_copy.start()
    rows_copy.start()
    ids_copy.wait()
    place = lax.broadcasted_iota(jnp.int32, (own, LANES), 0)
    ids = jnp.zeros((own, LANES), jnp.int32)
    for i in range(own):
        ids = jnp.where(place == i, targets_ref[i], ids)
    lane = lax.broadcasted_iota(jnp.int32, (own, LANES), 1)
    digits = jnp.where(lane == 0, ids // 256, ids % 256)
    out_ref[:, depth:] = digits.astype(jnp.float32).astype(jnp.bfloat16)
    rows_copy.wait()


def ids_of(digits):
    digits = digits.astype(jnp.float32)
    return (digits[:, 0:1] * 256.0 + digits[:, 1:2]).astype(jnp.int32)


def swap_blocks(value, group):
    size = value.shape[1]
    lane = lax.broadcasted_iota(jnp.int32, value.shape, 1)
    up, down = pltpu.roll(value, group, 1), pltpu.roll(value, size - group, 1)
    return jnp.where((lane & group) != 0, up, down)


def shared_order(value, members):
    me = lax.axis_index(AXIS)
    step = 1
    while step < members:
        swapped = swap_blocks(value, value.shape[1] // members * step)
        value = jnp.where((me & step) != 0, swapped, value)
        step *= 2
    return value


def as_columns(line):
    return jnp.broadcast_to(line, (LANES, line.shape[1])).T[:, 0:1]


def logits_of(rows_ref, near_ref, logits_ref, first, count):
    depth = near_ref.shape[0]

    @pl.loop(0, count // WIDE)
    def _(i):
        part = pl.ds(pl.multiple_of(first + i * WIDE, WIDE), WIDE)
        logits_ref[:, part] = jnp.dot(
            rows_ref[:, :depth], near_ref[:, part], preferred_element_type=jnp.float32
        )


def softmax_of(rows_ref, logits_ref, both_ref, columns_ref, first):
    rows, width = logits_ref.shape
    digits = rows_ref.shape[1] - LANES
    chunk = 32
    offset = lax.axis_index(AXIS) * width

    @pl.loop(0, rows // chunk)
    def _(i):
        part = pl.ds(pl.multiple_of(i * chunk, chunk), chunk)
        logits = logits_ref[part, :]
        ids = ids_of(rows_ref[part, digits:]) - offset
        hit = lax.broadcasted_iota(jnp.int32, logits.shape, 1) == ids
        top = jnp.max(logits, axis=1, keepdims=True)
        raised = jnp.exp(logits - top)
        total = jnp.sum(raised, axis=1, keepdims=True)
        pick = jnp.sum(jnp.where(hit, logits, 0.0), axis=1, keepdims=True)
        both_ref[part, :] = jnp.where(hit, 0.0, raised).astype(jnp.bfloat16)
        other = pl.ds(pl.multiple_of(rows + i * chunk, chunk), chunk)
        both_ref[other, :] = jnp.where(hit, 1.0, 0.0).astype(jnp.bfloat16)
        place = lax.broadcasted_iota(jnp.int32, (chunk, LANES), 1)
        slot = pl.ds(pl.multiple_of(first + i * chunk, chunk), chunk)
        columns_ref[slot, :] = jnp.where(place == 0, top, jnp.where(place == 1, total, pick))


def first_kernel(packed_ref, head, held_ref, near_ref, logits_ref, both_ref, columns_ref, sems):
    half = near_ref.shape[1] // 2
    copies = head_copies(head, near_ref, sems, 1)
    for copy in copies:
        copy.start()
    logits_of(packed_ref, near_ref, logits_ref, 0, half)
    for copy in copies:
        copy.wait()
    logits_of(packed_ref, near_ref, logits_ref, half, half)
    softmax_of(packed_ref, logits_ref, both_ref, columns_ref, 0)


def second_kernel(rows_ref, near_ref, before_ref, logits_ref, both_ref, lines_ref, columns_ref):
    first = before_ref.shape[0]
    logits_of(rows_ref, near_ref, logits_ref, 0, near_ref.shape[1])
    softmax_of(rows_ref, logits_ref, both_ref, columns_ref, first)
    columns_ref[pl.ds(0, first), :] = before_ref[...]
    lines_ref[...] = columns_ref[...].T[:8]


def merge_kernel(steps, members, mine_ref, *refs):
    *other_refs, out_ref = refs
    block = mine_ref.shape[1] // members
    me = lax.axis_index(AXIS)
    groups = [mine_ref[...]]
    for step, other_ref in zip(steps, other_refs):
        other, bit = other_ref[...], 1
        while bit <= step:
            if step & bit:
                other = swap_blocks(other, block * bit)
            bit *= 2
        groups.append(other)
    unit, bit = steps[0], 1
    while bit < len(groups):
        upper = (me & (unit * bit)) != 0
        groups = [jnp.where(upper, groups[i ^ bit], group) for i, group in enumerate(groups)]
        bit *= 2
    top = functools.reduce(jnp.maximum, [group[0:1] for group in groups])
    total = sum(group[1:2] * jnp.exp(group[0:1] - top) for group in groups)
    pick = sum(group[2:3] for group in groups)
    place = lax.broadcasted_iota(jnp.int32, out_ref.shape, 0)
    out_ref[...] = jnp.where(place == 0, top, jnp.where(place == 1, total, pick))


def grad_kernel(first, one_ref, two_ref, near_ref, *refs):
    terms_ref = refs[-1]
    tile = min(terms_ref.shape[1], 2**19 // (one_ref.shape[0] + two_ref.shape[0]))
    both = jnp.concatenate([one_ref[...], two_ref[...]], axis=0)
    for place in range(0, terms_ref.shape[1], tile):
        turned = lax.dot_general(
            near_ref[pl.ds(first + place, tile), :], both, (((1,), (1,)), ((), ())),
            preferred_element_type=jnp.float32,
        )
        terms_ref[:, pl.ds(place, tile)] = turned.T


def join_kernel(scale, first, lines_ref, mine_ref, *refs):
    *terms_refs, out_ref = refs
    rows = mine_ref.shape[1]
    top, total = lines_ref[0:1, :], lines_ref[1:2, :]
    soft = as_columns(jnp.exp(mine_ref[0:1, :] - top) / (total * rows)) * scale
    hard = (jnp.exp(mine_ref[2:3, :] - top) / total - 1.0) / rows
    hard = as_columns(hard.astype(jnp.bfloat16).astype(jnp.float32)) * scale

    count = out_ref.shape[0]
    chunk = min(count, 64)
    for place, terms_ref in enumerate(terms_refs):
        columns = pl.ds(place * terms_ref.shape[1], terms_ref.shape[1])
        for i in range(0, count, chunk):
            part = slice(first + i, first + i + chunk)
            out_ref[pl.ds(i, chunk), columns] = (
                soft[part] * terms_ref[pl.ds(2 * first + i, chunk), :]
                + hard[part] * terms_ref[pl.ds(2 * first + count + i, chunk), :]
            )


def loss_kernel(members, lines_ref, loss_ref):
    rows = lines_ref.shape[1]
    lines = shared_order(lines_ref[...], members)
    loss = jnp.sum(lines[0:1] + jnp.log(lines[1:2]) - lines[2:3], axis=1, keepdims=True) / rows
    loss_ref[...] = jnp.broadcast_to(loss, loss_ref.shape)


def frag_kernel(rows_one_ref, rows_two_ref, ids_one_ref, ids_two_ref, lines_ref, one_ref, two_ref, head_ref,
                global_ref, momentum_ref, peer_ref, new_global_ref, new_momentum_ref):
    logits = jnp.concatenate([one_ref[...], two_ref[...]], axis=0)
    held = jnp.concatenate([rows_one_ref[...], rows_two_ref[...]], axis=0)
    ids = jnp.concatenate([ids_of(ids_one_ref[...]), ids_of(ids_two_ref[...])], axis=0)
    rows, tile = logits.shape
    top, total = as_columns(lines_ref[0:1, :]), as_columns(lines_ref[1:2, :])
    offset = (lax.axis_index(AXIS) * pl.num_programs(0) + pl.program_id(0)) * tile
    hit = lax.broadcasted_iota(jnp.int32, (rows, tile), 1) == ids - offset
    shares = jnp.exp(logits - top) / total
    dlogits = ((shares - jnp.where(hit, 1.0, 0.0)) / rows).astype(jnp.bfloat16)
    turned = held.astype(jnp.float32).T.astype(jnp.bfloat16)
    frag_grad = jnp.dot(turned, dlogits, preferred_element_type=jnp.float32)
    local_frag = head_ref[...].astype(jnp.float32) - 1.0 * frag_grad
    pseudo = (global_ref[...] - local_frag + peer_ref[...]) / REPLICAS
    new_momentum = 0.9 * momentum_ref[...] + pseudo
    new_momentum_ref[...] = new_momentum
    new_global_ref[...] = global_ref[...] - 0.7 * (pseudo + 0.9 * new_momentum)


def frag_update(held, ids, lines, logits, near, global_frag, momentum, peer_delta):
    rows = lines.shape[1]
    width = near.shape[1]
    tile = pl.BlockSpec((FRAG, TILE), lambda i: (0, i))

    return pl.pallas_call(
        frag_kernel,
        grid=(width // TILE,),
        out_shape=[jax.ShapeDtypeStruct((FRAG, width), jnp.float32)] * 2,
        in_specs=[pl.BlockSpec((x.shape[0], FRAG), lambda i: (0, 0)) for x in held]
        + [
            pl.BlockSpec((x.shape[0], LANES), lambda i, last=x.shape[1] // LANES - 1: (0, last))
            for x in ids
        ]
        + [pl.BlockSpec((8, rows), lambda i: (0, 0))]
        + [pl.BlockSpec((x.shape[0], TILE), lambda i: (0, i)) for x in logits]
        + [tile] * 4,
        out_specs=[tile, tile],
        compiler_params=pltpu.CompilerParams(vmem_limit_bytes=16 * 2**20),
        cost_estimate=pl.CostEstimate(
            flops=2 * rows * FRAG * width, bytes_accessed=24 * FRAG * width, transcendentals=0
        ),
    )(
        *held, *ids, lines, *[pltpu.with_memory_space_constraint(x, pltpu.VMEM) for x in logits],
        pltpu.with_memory_space_constraint(near, pltpu.VMEM), global_frag, momentum, peer_delta,
    )


def swap(value, step):
    return lax.ppermute(value, AXIS, [(i, i ^ step) for i in range(lax.axis_size(AXIS))])


def far_steps():
    step = 4
    steps = []
    while step < lax.axis_size(AXIS):
        steps.append(step)
        step *= 2
    return steps


def gather_rows(packed):
    own = packed.shape[0]
    held = packed
    for step in far_steps():
        held = jnp.concatenate([held, swap(held, step)], axis=0)
    far = held[own:]
    near = jnp.concatenate([packed] + [swap(packed, step) for step in (1, 2, 3)], axis=0)
    far = jnp.stack([far] + [swap(far, step) for step in (1, 2, 3)])
    count = far.shape[1] // own
    return near, far.reshape(4, count, own, -1).swapaxes(0, 1).reshape(4 * count * own, -1)


def scatter_sums(grads_near, grads_far, own):
    blocks = [
        grads[i * own : (i + 1) * own]
        for grads in (grads_near, grads_far)
        for i in range(grads.shape[0] // own)
    ]
    members = len(blocks)

    def moved(parts, step):
        value = jnp.concatenate([part.astype(SEND) for part in parts], axis=0)
        value = swap(value, step).astype(jnp.float32)
        return [value[i * own : (i + 1) * own] for i in range(len(parts))]

    sums = blocks[::4]
    for part in (list(range(1, members // 4)), [0]):
        for step in (3, 1, 2):
            for i, value in zip(part, moved([blocks[4 * i + step] for i in part], step)):
                sums[i] = sums[i] + value
    for step in far_steps()[::-1]:
        keep = len(sums) // 2
        sums = [a + b for a, b in zip(sums[:keep], moved(sums[keep:], step))]
    return sums[0]


def body(hidden, targets, head, global_frag, momentum, peer_delta):
    members = lax.axis_size(AXIS)
    own, depth = hidden.shape
    rows = own * members
    width = head.shape[1]

    packed = call(
        pack_kernel, [((own, depth + LANES), hidden.dtype)], [targets, hidden],
        scratch=[pltpu.SMEM(targets.shape, targets.dtype), pltpu.SemaphoreType.DMA((2,))],
        sources=[pltpu.HBM, pltpu.HBM],
    )[0]
    rows_near, rows_far = gather_rows(packed)
    near = call(
        load_kernel, [(head.shape, head.dtype)], [head],
        scratch=[pltpu.SemaphoreType.DMA((4,))], sources=[pltpu.HBM],
    )[0]

    count = 4 * own
    near, logits_near, both_near, columns = call(
        first_kernel,
        [(head.shape, head.dtype), ((count, width), jnp.float32), ((2 * count, width), jnp.bfloat16),
         ((count, LANES), jnp.float32)],
        [rows_near, head, near], 2 * count * depth * width,
        scratch=[pltpu.SemaphoreType.DMA((4,))],
        sources=[pltpu.VMEM, pltpu.HBM, pltpu.VMEM], aliases={2: 0},
    )
    count = rows - 4 * own
    logits_far, both_far, mine = call(
        second_kernel,
        [((count, width), jnp.float32), ((2 * count, width), jnp.bfloat16), ((8, rows), jnp.float32)],
        [rows_far, near, columns], 2 * count * depth * width,
        scratch=[pltpu.VMEM((rows, LANES), jnp.float32)],
    )

    lines = mine
    for steps in [[step] for step in far_steps()] + [[1, 2, 3]]:
        before = lines
        lines = call(
            functools.partial(merge_kernel, steps, members),
            [((8, rows), jnp.float32)], [lines] + [swap(lines, step) for step in steps],
        )[0]

    terms = [
        call(
            functools.partial(grad_kernel, first),
            [((2 * rows, depth // 2), jnp.float32)], [both_near, both_far, near, *after],
            2 * rows * depth * width,
        )[0]
        for first, after in ((0, []), (depth // 2, [before]))
    ]

    scale = 2.0**14 * rows
    grads_far, grads_near = (
        call(
            functools.partial(join_kernel, scale, first),
            [((count, depth), jnp.float32)], [lines, mine] + terms,
        )[0]
        for first, count in ((4 * own, rows - 4 * own), (0, 4 * own))
    )
    hidden_grad = (scatter_sums(grads_near, grads_far, own) * (1.0 / scale)).astype(jnp.bfloat16)
    loss = call(functools.partial(loss_kernel, members), [((8, LANES), jnp.float32)], [lines])[0]
    new_global, new_momentum = frag_update(
        [rows_near, rows_far], [rows_near, rows_far], lines, [logits_near, logits_far], near,
        global_frag, momentum, peer_delta,
    )
    return (loss[0, :1], hidden_grad, new_global, new_momentum)


def solution(mesh):
    in_specs = (
        P(("outer", "vocab"), None),
        P(("outer", "vocab")),
        P("outer", "vocab"),
        P(None, "vocab"),
        P(None, "vocab"),
        P("outer", "vocab"),
    )
    out_specs = (P("outer"), P(("outer", "vocab"), None), P("outer", "vocab"), P("outer", "vocab"))
    return jax.shard_map(body, mesh=mesh, in_specs=in_specs, out_specs=out_specs, check_vma=False)
```

```python
import functools

import jax
import jax.numpy as jnp
from jax import lax
from jax.experimental import pallas as pl
from jax.experimental.pallas import tpu as pltpu
from jax.sharding import PartitionSpec as P

FRAG = 128
REPLICAS = 4
AXIS = "vocab"
SEND = jnp.float16
LANES = 128
VMEM = pl.BlockSpec(memory_space=pltpu.VMEM)


def call(kernel, outs, operands, flops=0, scratch=(), sources=None, vmem=16 * 2**20, aliases={}):
    outs = [pltpu.VMEM(shape, dtype) for shape, dtype in outs]
    places = sources or [pltpu.VMEM] * len(operands)
    moved = sum(x.size * x.dtype.itemsize for x in operands)
    return pl.pallas_call(
        kernel,
        out_shape=outs,
        in_specs=[pl.BlockSpec(memory_space=place) for place in places],
        out_specs=[VMEM] * len(outs),
        scratch_shapes=list(scratch),
        input_output_aliases=aliases,
        compiler_params=pltpu.CompilerParams(vmem_limit_bytes=vmem),
        cost_estimate=pl.CostEstimate(flops=flops, bytes_accessed=moved, transcendentals=0),
    )(*[pltpu.with_memory_space_constraint(x, place) for x, place in zip(operands, places)])


def head_copies(source, target, sems, half):
    block = source.shape[0] // sems.shape[0]
    columns = pl.ds(half * (source.shape[1] // 2), source.shape[1] // 2)
    copies = []
    for i in range(sems.shape[0]):
        part = pl.ds(i * block, block)
        copies.append(pltpu.make_async_copy(source.at[part, columns], target.at[part, columns], sems.at[i]))
    return copies


def load_kernel(head, near_ref, sems):
    copies = head_copies(head, near_ref, sems, 0)
    for copy in copies:
        copy.start()
    for copy in copies:
        copy.wait()


TILE = 512
WIDE = 1024


def pack_kernel(targets, rows, out_ref, targets_ref, sems):
    own, depth = rows.shape
    ids_copy = pltpu.make_async_copy(targets, targets_ref, sems.at[0])
    rows_copy = pltpu.make_async_copy(rows, out_ref.at[:, pl.ds(0, depth)], sems.at[1])
    ids_copy.start()
    rows_copy.start()
    ids_copy.wait()
    place = lax.broadcasted_iota(jnp.int32, (own, LANES), 0)
    ids = jnp.zeros((own, LANES), jnp.int32)
    for i in range(own):
        ids = jnp.where(place == i, targets_ref[i], ids)
    lane = lax.broadcasted_iota(jnp.int32, (own, LANES), 1)
    digits = jnp.where(lane == 0, ids // 256, ids % 256)
    out_ref[:, depth:] = digits.astype(jnp.float32).astype(jnp.bfloat16)
    rows_copy.wait()


def ids_of(digits):
    digits = digits.astype(jnp.float32)
    return (digits[:, 0:1] * 256.0 + digits[:, 1:2]).astype(jnp.int32)


def swap_blocks(value, group):
    size = value.shape[1]
    lane = lax.broadcasted_iota(jnp.int32, value.shape, 1)
    up, down = pltpu.roll(value, group, 1), pltpu.roll(value, size - group, 1)
    return jnp.where((lane & group) != 0, up, down)


def shared_order(value, members):
    me = my_label()
    step = 1
    while step < members:
        swapped = swap_blocks(value, value.shape[1] // members * step)
        value = jnp.where((me & step) != 0, swapped, value)
        step *= 2
    return value


def as_columns(line):
    return jnp.broadcast_to(line, (LANES, line.shape[1])).T[:, 0:1]


def logits_of(rows_ref, near_ref, logits_ref, first, count):
    depth = near_ref.shape[0]

    @pl.loop(0, count // WIDE)
    def _(i):
        part = pl.ds(pl.multiple_of(first + i * WIDE, WIDE), WIDE)
        logits_ref[:, part] = jnp.dot(
            rows_ref[:, :depth], near_ref[:, part], preferred_element_type=jnp.float32
        )


def softmax_of(rows_ref, logits_ref, both_ref, columns_ref, first):
    rows, width = logits_ref.shape
    digits = rows_ref.shape[1] - LANES
    chunk = 32
    offset = lax.axis_index(AXIS) * width

    @pl.loop(0, rows // chunk)
    def _(i):
        part = pl.ds(pl.multiple_of(i * chunk, chunk), chunk)
        logits = logits_ref[part, :]
        ids = ids_of(rows_ref[part, digits:]) - offset
        hit = lax.broadcasted_iota(jnp.int32, logits.shape, 1) == ids
        top = jnp.max(logits, axis=1, keepdims=True)
        raised = jnp.exp(logits - top)
        total = jnp.sum(raised, axis=1, keepdims=True)
        pick = jnp.sum(jnp.where(hit, logits, 0.0), axis=1, keepdims=True)
        both_ref[part, :] = jnp.where(hit, 0.0, raised).astype(jnp.bfloat16)
        other = pl.ds(pl.multiple_of(rows + i * chunk, chunk), chunk)
        both_ref[other, :] = jnp.where(hit, 1.0, 0.0).astype(jnp.bfloat16)
        place = lax.broadcasted_iota(jnp.int32, (chunk, LANES), 1)
        slot = pl.ds(pl.multiple_of(first + i * chunk, chunk), chunk)
        columns_ref[slot, :] = jnp.where(place == 0, top, jnp.where(place == 1, total, pick))


def first_kernel(packed_ref, head, held_ref, near_ref, logits_ref, both_ref, columns_ref, sems):
    half = near_ref.shape[1] // 2
    copies = head_copies(head, near_ref, sems, 1)
    for copy in copies:
        copy.start()
    logits_of(packed_ref, near_ref, logits_ref, 0, half)
    for copy in copies:
        copy.wait()
    logits_of(packed_ref, near_ref, logits_ref, half, half)
    softmax_of(packed_ref, logits_ref, both_ref, columns_ref, 0)


def second_kernel(rows_ref, near_ref, before_ref, logits_ref, both_ref, lines_ref, columns_ref):
    first = before_ref.shape[0]
    logits_of(rows_ref, near_ref, logits_ref, 0, near_ref.shape[1])
    softmax_of(rows_ref, logits_ref, both_ref, columns_ref, first)
    columns_ref[pl.ds(0, first), :] = before_ref[...]
    lines_ref[...] = columns_ref[...].T[:8]


def merge_kernel(steps, members, mine_ref, *refs):
    *other_refs, out_ref = refs
    block = mine_ref.shape[1] // members
    me = my_label()
    groups = [mine_ref[...]]
    for step, other_ref in zip(steps, other_refs):
        other, bit = other_ref[...], 1
        while bit <= step:
            if step & bit:
                other = swap_blocks(other, block * bit)
            bit *= 2
        groups.append(other)
    unit, bit = steps[0], 1
    while bit < len(groups):
        upper = (me & (unit * bit)) != 0
        groups = [jnp.where(upper, groups[i ^ bit], group) for i, group in enumerate(groups)]
        bit *= 2
    top = functools.reduce(jnp.maximum, [group[0:1] for group in groups])
    total = sum(group[1:2] * jnp.exp(group[0:1] - top) for group in groups)
    pick = sum(group[2:3] for group in groups)
    place = lax.broadcasted_iota(jnp.int32, out_ref.shape, 0)
    out_ref[...] = jnp.where(place == 0, top, jnp.where(place == 1, total, pick))


def grad_kernel(first, one_ref, two_ref, near_ref, *refs):
    terms_ref = refs[-1]
    tile = min(terms_ref.shape[1], 2**19 // (one_ref.shape[0] + two_ref.shape[0]))
    both = jnp.concatenate([one_ref[...], two_ref[...]], axis=0)
    for place in range(0, terms_ref.shape[1], tile):
        turned = lax.dot_general(
            near_ref[pl.ds(first + place, tile), :], both, (((1,), (1,)), ((), ())),
            preferred_element_type=jnp.float32,
        )
        terms_ref[:, pl.ds(place, tile)] = turned.T


def join_kernel(scale, first, lines_ref, mine_ref, *refs):
    *terms_refs, out_ref = refs
    rows = mine_ref.shape[1]
    top, total = lines_ref[0:1, :], lines_ref[1:2, :]
    soft = as_columns(jnp.exp(mine_ref[0:1, :] - top) / (total * rows)) * scale
    hard = (jnp.exp(mine_ref[2:3, :] - top) / total - 1.0) / rows
    hard = as_columns(hard.astype(jnp.bfloat16).astype(jnp.float32)) * scale

    count = out_ref.shape[0]
    chunk = min(count, 64)
    for place, terms_ref in enumerate(terms_refs):
        columns = pl.ds(place * terms_ref.shape[1], terms_ref.shape[1])
        for i in range(0, count, chunk):
            part = slice(first + i, first + i + chunk)
            out_ref[pl.ds(i, chunk), columns] = (
                soft[part] * terms_ref[pl.ds(2 * first + i, chunk), :]
                + hard[part] * terms_ref[pl.ds(2 * first + count + i, chunk), :]
            )


def loss_kernel(members, lines_ref, loss_ref):
    rows = lines_ref.shape[1]
    lines = shared_order(lines_ref[...], members)
    loss = jnp.sum(lines[0:1] + jnp.log(lines[1:2]) - lines[2:3], axis=1, keepdims=True) / rows
    loss_ref[...] = jnp.broadcast_to(loss, loss_ref.shape)


def frag_kernel(rows_one_ref, rows_two_ref, ids_one_ref, ids_two_ref, lines_ref, one_ref, two_ref, head_ref,
                global_ref, momentum_ref, peer_ref, new_global_ref, new_momentum_ref):
    logits = jnp.concatenate([one_ref[...], two_ref[...]], axis=0)
    held = jnp.concatenate([rows_one_ref[...], rows_two_ref[...]], axis=0)
    ids = jnp.concatenate([ids_of(ids_one_ref[...]), ids_of(ids_two_ref[...])], axis=0)
    rows, tile = logits.shape
    top, total = as_columns(lines_ref[0:1, :]), as_columns(lines_ref[1:2, :])
    offset = (lax.axis_index(AXIS) * pl.num_programs(0) + pl.program_id(0)) * tile
    hit = lax.broadcasted_iota(jnp.int32, (rows, tile), 1) == ids - offset
    shares = jnp.exp(logits - top) / total
    dlogits = ((shares - jnp.where(hit, 1.0, 0.0)) / rows).astype(jnp.bfloat16)
    turned = held.astype(jnp.float32).T.astype(jnp.bfloat16)
    frag_grad = jnp.dot(turned, dlogits, preferred_element_type=jnp.float32)
    local_frag = head_ref[...].astype(jnp.float32) - 1.0 * frag_grad
    pseudo = (global_ref[...] - local_frag + peer_ref[...]) / REPLICAS
    new_momentum = 0.9 * momentum_ref[...] + pseudo
    new_momentum_ref[...] = new_momentum
    new_global_ref[...] = global_ref[...] - 0.7 * (pseudo + 0.9 * new_momentum)


def frag_update(held, ids, lines, logits, near, global_frag, momentum, peer_delta):
    rows = lines.shape[1]
    width = near.shape[1]
    tile = pl.BlockSpec((FRAG, TILE), lambda i: (0, i))

    return pl.pallas_call(
        frag_kernel,
        grid=(width // TILE,),
        out_shape=[jax.ShapeDtypeStruct((FRAG, width), jnp.float32)] * 2,
        in_specs=[pl.BlockSpec((x.shape[0], FRAG), lambda i: (0, 0)) for x in held]
        + [
            pl.BlockSpec((x.shape[0], LANES), lambda i, last=x.shape[1] // LANES - 1: (0, last))
            for x in ids
        ]
        + [pl.BlockSpec((8, rows), lambda i: (0, 0))]
        + [pl.BlockSpec((x.shape[0], TILE), lambda i: (0, i)) for x in logits]
        + [tile] * 4,
        out_specs=[tile, tile],
        compiler_params=pltpu.CompilerParams(vmem_limit_bytes=16 * 2**20),
        cost_estimate=pl.CostEstimate(
            flops=2 * rows * FRAG * width, bytes_accessed=24 * FRAG * width, transcendentals=0
        ),
    )(
        *held, *ids, lines, *[pltpu.with_memory_space_constraint(x, pltpu.VMEM) for x in logits],
        pltpu.with_memory_space_constraint(near, pltpu.VMEM), global_frag, momentum, peer_delta,
    )


def turned(label):
    return label // 4 * 4 + label % 2 * 2 + label // 2 % 2


def my_label():
    me = lax.axis_index(AXIS)
    return jnp.where(lax.rem(lax.axis_index("outer"), 2) == 1, turned(me), me)


def swap(value, step):
    members = lax.axis_size(AXIS)
    pairs = []
    for outer in range(lax.axis_size("outer")):
        flip = turned(step) if outer % 2 else step
        pairs += [(outer * members + i, outer * members + (i ^ flip)) for i in range(members)]
    return lax.ppermute(value, ("outer", AXIS), pairs)


def far_steps():
    step = 4
    steps = []
    while step < lax.axis_size(AXIS):
        steps.append(step)
        step *= 2
    return steps


def gather_rows(packed):
    own = packed.shape[0]
    held = packed
    for step in far_steps():
        held = jnp.concatenate([held, swap(held, step)], axis=0)
    far = held[own:]
    near = jnp.concatenate([packed] + [swap(packed, step) for step in (1, 2, 3)], axis=0)
    far = jnp.stack([far] + [swap(far, step) for step in (1, 2, 3)])
    count = far.shape[1] // own
    return near, far.reshape(4, count, own, -1).swapaxes(0, 1).reshape(4 * count * own, -1)


def scatter_sums(grads_near, grads_far, own):
    blocks = [
        grads[i * own : (i + 1) * own]
        for grads in (grads_near, grads_far)
        for i in range(grads.shape[0] // own)
    ]
    members = len(blocks)

    def moved(parts, step):
        value = jnp.concatenate([part.astype(SEND) for part in parts], axis=0)
        value = swap(value, step).astype(jnp.float32)
        return [value[i * own : (i + 1) * own] for i in range(len(parts))]

    sums = blocks[::4]
    for part in (list(range(1, members // 4)), [0]):
        for step in (3, 1, 2):
            for i, value in zip(part, moved([blocks[4 * i + step] for i in part], step)):
                sums[i] = sums[i] + value
    for step in far_steps()[::-1]:
        keep = len(sums) // 2
        sums = [a + b for a, b in zip(sums[:keep], moved(sums[keep:], step))]
    return sums[0]


def body(hidden, targets, head, global_frag, momentum, peer_delta):
    members = lax.axis_size(AXIS)
    own, depth = hidden.shape
    rows = own * members
    width = head.shape[1]

    packed = call(
        pack_kernel, [((own, depth + LANES), hidden.dtype)], [targets, hidden],
        scratch=[pltpu.SMEM(targets.shape, targets.dtype), pltpu.SemaphoreType.DMA((2,))],
        sources=[pltpu.HBM, pltpu.HBM],
    )[0]
    rows_near, rows_far = gather_rows(packed)
    near = call(
        load_kernel, [(head.shape, head.dtype)], [head],
        scratch=[pltpu.SemaphoreType.DMA((4,))], sources=[pltpu.HBM],
    )[0]

    count = 4 * own
    near, logits_near, both_near, columns = call(
        first_kernel,
        [(head.shape, head.dtype), ((count, width), jnp.float32), ((2 * count, width), jnp.bfloat16),
         ((count, LANES), jnp.float32)],
        [rows_near, head, near], 2 * count * depth * width,
        scratch=[pltpu.SemaphoreType.DMA((4,))],
        sources=[pltpu.VMEM, pltpu.HBM, pltpu.VMEM], aliases={2: 0},
    )
    count = rows - 4 * own
    logits_far, both_far, mine = call(
        second_kernel,
        [((count, width), jnp.float32), ((2 * count, width), jnp.bfloat16), ((8, rows), jnp.float32)],
        [rows_far, near, columns], 2 * count * depth * width,
        scratch=[pltpu.VMEM((rows, LANES), jnp.float32)],
    )

    lines = mine
    for steps in [[step] for step in far_steps()] + [[1, 2, 3]]:
        before = lines
        lines = call(
            functools.partial(merge_kernel, steps, members),
            [((8, rows), jnp.float32)], [lines] + [swap(lines, step) for step in steps],
        )[0]

    terms = [
        call(
            functools.partial(grad_kernel, first),
            [((2 * rows, depth // 2), jnp.float32)], [both_near, both_far, near, *after],
            2 * rows * depth * width,
        )[0]
        for first, after in ((0, []), (depth // 2, [before]))
    ]

    scale = 2.0**14 * rows
    grads_far, grads_near = (
        call(
            functools.partial(join_kernel, scale, first),
            [((count, depth), jnp.float32)], [lines, mine] + terms,
        )[0]
        for first, count in ((4 * own, rows - 4 * own), (0, 4 * own))
    )
    hidden_grad = (scatter_sums(grads_near, grads_far, own) * (1.0 / scale)).astype(jnp.bfloat16)
    loss = call(functools.partial(loss_kernel, members), [((8, LANES), jnp.float32)], [lines])[0]
    new_global, new_momentum = frag_update(
        [rows_near, rows_far], [rows_near, rows_far], lines, [logits_near, logits_far], near,
        global_frag, momentum, peer_delta,
    )
    return (loss[0, :1], hidden_grad, new_global, new_momentum)


def solution(mesh):
    in_specs = (
        P(("outer", "vocab"), None),
        P(("outer", "vocab")),
        P("outer", "vocab"),
        P(None, "vocab"),
        P(None, "vocab"),
        P("outer", "vocab"),
    )
    out_specs = (P("outer"), P(("outer", "vocab"), None), P("outer", "vocab"), P("outer", "vocab"))
    return jax.shard_map(body, mesh=mesh, in_specs=in_specs, out_specs=out_specs, check_vma=False)
```

```python
import functools

import jax
import jax.numpy as jnp
from jax import lax
from jax.experimental import pallas as pl
from jax.experimental.pallas import tpu as pltpu
from jax.sharding import PartitionSpec as P

FRAG = 128
REPLICAS = 4
AXIS = "vocab"
SEND = jnp.float16
LANES = 128
VMEM = pl.BlockSpec(memory_space=pltpu.VMEM)


def call(kernel, outs, operands, flops=0, scratch=(), sources=None, vmem=16 * 2**20):
    outs = [pltpu.VMEM(shape, dtype) for shape, dtype in outs]
    places = sources or [pltpu.VMEM] * len(operands)
    moved = sum(x.size * x.dtype.itemsize for x in operands)
    return pl.pallas_call(
        kernel,
        out_shape=outs,
        in_specs=[pl.BlockSpec(memory_space=place) for place in places],
        out_specs=[VMEM] * len(outs),
        scratch_shapes=list(scratch),
        compiler_params=pltpu.CompilerParams(vmem_limit_bytes=vmem),
        cost_estimate=pl.CostEstimate(flops=flops, bytes_accessed=moved, transcendentals=0),
    )(*[pltpu.with_memory_space_constraint(x, place) for x, place in zip(operands, places)])


def load_kernel(source, target, sems):
    block = source.shape[0] // sems.shape[0]
    copies = []
    for i in range(sems.shape[0]):
        part = pl.ds(i * block, block)
        copies.append(pltpu.make_async_copy(source.at[part], target.at[part], sems.at[i]))
    for copy in copies:
        copy.start()
    for copy in copies:
        copy.wait()


def resident(head):
    return call(
        load_kernel, [(head.shape, head.dtype)], [head],
        scratch=[pltpu.SemaphoreType.DMA((4,))], sources=[pltpu.HBM],
    )[0]


TILE = 512
WIDE = 1024


def pack_kernel(targets, rows, out_ref, targets_ref, sems):
    own, depth = rows.shape
    ids_copy = pltpu.make_async_copy(targets, targets_ref, sems.at[0])
    rows_copy = pltpu.make_async_copy(rows, out_ref.at[:, pl.ds(0, depth)], sems.at[1])
    ids_copy.start()
    rows_copy.start()
    ids_copy.wait()
    place = lax.broadcasted_iota(jnp.int32, (own, LANES), 0)
    ids = jnp.zeros((own, LANES), jnp.int32)
    for i in range(own):
        ids = jnp.where(place == i, targets_ref[i], ids)
    lane = lax.broadcasted_iota(jnp.int32, (own, LANES), 1)
    digits = jnp.where(lane == 0, ids // 256, ids % 256)
    out_ref[:, depth:] = digits.astype(jnp.float32).astype(jnp.bfloat16)
    rows_copy.wait()


def ids_of(digits):
    digits = digits.astype(jnp.float32)
    return (digits[:, 0:1] * 256.0 + digits[:, 1:2]).astype(jnp.int32)


def swap_blocks(value, group):
    size = value.shape[1]
    lane = lax.broadcasted_iota(jnp.int32, value.shape, 1)
    up, down = pltpu.roll(value, group, 1), pltpu.roll(value, size - group, 1)
    return jnp.where((lane & group) != 0, up, down)


def shared_order(value, members):
    me = my_label()
    step = 1
    while step < members:
        swapped = swap_blocks(value, value.shape[1] // members * step)
        value = jnp.where((me & step) != 0, swapped, value)
        step *= 2
    return value


def as_columns(line):
    return jnp.broadcast_to(line, (LANES, line.shape[1])).T[:, 0:1]


def rows_kernel(rows_ref, near_ref, *refs):
    before_ref, (logits_ref, both_ref, stats_ref) = (None, refs) if len(refs) == 3 else (refs[0], refs[1:4])
    rows = rows_ref.shape[0]
    depth, width = near_ref.shape

    @pl.loop(0, width // WIDE)
    def _(i):
        part = pl.ds(pl.multiple_of(i * WIDE, WIDE), WIDE)
        logits_ref[:, part] = jnp.dot(
            rows_ref[:, :depth], near_ref[:, part], preferred_element_type=jnp.float32
        )

    chunk = 32
    offset = lax.axis_index(AXIS) * width
    columns_ref = stats_ref if before_ref is None else refs[4]
    first = 0 if before_ref is None else before_ref.shape[0]

    @pl.loop(0, rows // chunk)
    def _(i):
        part = pl.ds(pl.multiple_of(i * chunk, chunk), chunk)
        logits = logits_ref[part, :]
        ids = ids_of(rows_ref[part, depth:]) - offset
        hit = lax.broadcasted_iota(jnp.int32, logits.shape, 1) == ids
        top = jnp.max(logits, axis=1, keepdims=True)
        raised = jnp.exp(logits - top)
        total = jnp.sum(raised, axis=1, keepdims=True)
        pick = jnp.sum(jnp.where(hit, logits, 0.0), axis=1, keepdims=True)
        both_ref[part, :] = jnp.where(hit, 0.0, raised).astype(jnp.bfloat16)
        other = pl.ds(pl.multiple_of(rows + i * chunk, chunk), chunk)
        both_ref[other, :] = jnp.where(hit, 1.0, 0.0).astype(jnp.bfloat16)
        place = lax.broadcasted_iota(jnp.int32, (chunk, LANES), 1)
        slot = pl.ds(pl.multiple_of(first + i * chunk, chunk), chunk)
        columns_ref[slot, :] = jnp.where(place == 0, top, jnp.where(place == 1, total, pick))

    if before_ref is not None:
        columns_ref[pl.ds(0, first), :] = before_ref[...]
        stats_ref[...] = columns_ref[...].T[:8]


def merge_kernel(steps, members, mine_ref, *refs):
    *other_refs, out_ref = refs
    block = mine_ref.shape[1] // members
    me = my_label()
    groups = [mine_ref[...]]
    for step, other_ref in zip(steps, other_refs):
        other, bit = other_ref[...], 1
        while bit <= step:
            if step & bit:
                other = swap_blocks(other, block * bit)
            bit *= 2
        groups.append(other)
    unit, bit = steps[0], 1
    while bit < len(groups):
        upper = (me & (unit * bit)) != 0
        groups = [jnp.where(upper, groups[i ^ bit], group) for i, group in enumerate(groups)]
        bit *= 2
    top = functools.reduce(jnp.maximum, [group[0:1] for group in groups])
    total = sum(group[1:2] * jnp.exp(group[0:1] - top) for group in groups)
    pick = sum(group[2:3] for group in groups)
    place = lax.broadcasted_iota(jnp.int32, out_ref.shape, 0)
    out_ref[...] = jnp.where(place == 0, top, jnp.where(place == 1, total, pick))


def grad_kernel(first, one_ref, two_ref, near_ref, *refs):
    terms_ref = refs[-1]
    tile = min(terms_ref.shape[1], 2**19 // (one_ref.shape[0] + two_ref.shape[0]))
    both = jnp.concatenate([one_ref[...], two_ref[...]], axis=0)
    for place in range(0, terms_ref.shape[1], tile):
        turned = lax.dot_general(
            near_ref[pl.ds(first + place, tile), :], both, (((1,), (1,)), ((), ())),
            preferred_element_type=jnp.float32,
        )
        terms_ref[:, pl.ds(place, tile)] = turned.T


def join_kernel(scale, first, lines_ref, mine_ref, *refs):
    *terms_refs, out_ref = refs
    rows = mine_ref.shape[1]
    top, total = lines_ref[0:1, :], lines_ref[1:2, :]
    soft = as_columns(jnp.exp(mine_ref[0:1, :] - top) / (total * rows)) * scale
    hard = (jnp.exp(mine_ref[2:3, :] - top) / total - 1.0) / rows
    hard = as_columns(hard.astype(jnp.bfloat16).astype(jnp.float32)) * scale

    count = out_ref.shape[0]
    chunk = min(count, 64)
    for place, terms_ref in enumerate(terms_refs):
        columns = pl.ds(place * terms_ref.shape[1], terms_ref.shape[1])
        for i in range(0, count, chunk):
            part = slice(first + i, first + i + chunk)
            out_ref[pl.ds(i, chunk), columns] = (
                soft[part] * terms_ref[pl.ds(2 * first + i, chunk), :]
                + hard[part] * terms_ref[pl.ds(2 * first + count + i, chunk), :]
            )


def loss_kernel(members, lines_ref, loss_ref):
    rows = lines_ref.shape[1]
    lines = shared_order(lines_ref[...], members)
    loss = jnp.sum(lines[0:1] + jnp.log(lines[1:2]) - lines[2:3], axis=1, keepdims=True) / rows
    loss_ref[...] = jnp.broadcast_to(loss, loss_ref.shape)


def frag_kernel(rows_ref, digits_ref, lines_ref, one_ref, two_ref, head_ref, global_ref, momentum_ref,
                peer_ref, new_global_ref, new_momentum_ref):
    logits = jnp.concatenate([one_ref[...], two_ref[...]], axis=0)
    rows, tile = logits.shape
    top, total = as_columns(lines_ref[0:1, :]), as_columns(lines_ref[1:2, :])
    offset = (lax.axis_index(AXIS) * pl.num_programs(0) + pl.program_id(0)) * tile
    hit = lax.broadcasted_iota(jnp.int32, (rows, tile), 1) == ids_of(digits_ref[...]) - offset
    shares = jnp.exp(logits - top) / total
    dlogits = ((shares - jnp.where(hit, 1.0, 0.0)) / rows).astype(jnp.bfloat16)
    turned = rows_ref[...].astype(jnp.float32).T.astype(jnp.bfloat16)
    frag_grad = jnp.dot(turned, dlogits, preferred_element_type=jnp.float32)
    local_frag = head_ref[...].astype(jnp.float32) - 1.0 * frag_grad
    pseudo = (global_ref[...] - local_frag + peer_ref[...]) / REPLICAS
    new_momentum = 0.9 * momentum_ref[...] + pseudo
    new_momentum_ref[...] = new_momentum
    new_global_ref[...] = global_ref[...] - 0.7 * (pseudo + 0.9 * new_momentum)


def frag_update(rows_all, lines, logits, near, global_frag, momentum, peer_delta):
    rows = rows_all.shape[0]
    width = near.shape[1]
    last = rows_all.shape[1] // LANES - 1
    tile = pl.BlockSpec((FRAG, TILE), lambda i: (0, i))
    return pl.pallas_call(
        frag_kernel,
        grid=(width // TILE,),
        out_shape=[jax.ShapeDtypeStruct((FRAG, width), jnp.float32)] * 2,
        in_specs=[
            pl.BlockSpec((rows, FRAG), lambda i: (0, 0)),
            pl.BlockSpec((rows, LANES), lambda i: (0, last)),
            pl.BlockSpec((8, rows), lambda i: (0, 0)),
        ]
        + [pl.BlockSpec((x.shape[0], TILE), lambda i: (0, i)) for x in logits]
        + [tile] * 4,
        out_specs=[tile, tile],
        compiler_params=pltpu.CompilerParams(vmem_limit_bytes=16 * 2**20),
        cost_estimate=pl.CostEstimate(
            flops=2 * rows * FRAG * width, bytes_accessed=24 * FRAG * width, transcendentals=0
        ),
    )(
        rows_all, rows_all, lines,
        *[pltpu.with_memory_space_constraint(x, pltpu.VMEM) for x in logits],
        pltpu.with_memory_space_constraint(near, pltpu.VMEM), global_frag, momentum, peer_delta,
    )


def turned(label):
    return label // 4 * 4 + label % 2 * 2 + label // 2 % 2


def my_label():
    me = lax.axis_index(AXIS)
    return jnp.where(lax.rem(lax.axis_index("outer"), 2) == 1, turned(me), me)


def swap(value, step):
    members = lax.axis_size(AXIS)
    pairs = []
    for outer in range(lax.axis_size("outer")):
        flip = turned(step) if outer % 2 else step
        pairs += [(outer * members + i, outer * members + (i ^ flip)) for i in range(members)]
    return lax.ppermute(value, ("outer", AXIS), pairs)


def far_steps():
    step = 4
    steps = []
    while step < lax.axis_size(AXIS):
        steps.append(step)
        step *= 2
    return steps


def gather_rows(packed):
    own = packed.shape[0]
    held = packed
    for step in far_steps()[:1]:
        held = jnp.concatenate([held, swap(held, step)], axis=0)
    near = [packed] + [swap(packed, step) for step in (3, 2, 1)][::-1]
    for step in far_steps()[1:]:
        held = jnp.concatenate([held, swap(held, step)], axis=0)
    far = held[own:]
    far = jnp.stack([far] + [swap(far, step) for step in (3, 2, 1)][::-1])
    count = far.shape[1] // own
    far = far.reshape(4, count, own, -1).swapaxes(0, 1).reshape(4 * count * own, -1)
    return jnp.concatenate(near, axis=0), far


def scatter_sums(grads_near, grads_far, own):
    blocks = [
        grads[i * own : (i + 1) * own]
        for grads in (grads_near, grads_far)
        for i in range(grads.shape[0] // own)
    ]
    members = len(blocks)

    def moved(parts, step):
        value = jnp.concatenate([part.astype(SEND) for part in parts], axis=0)
        value = swap(value, step).astype(jnp.float32)
        return [value[i * own : (i + 1) * own] for i in range(len(parts))]

    sums = blocks[::4]
    for part in (list(range(1, members // 4)), [0]):
        for step in (3, 2, 1):
            for i, value in zip(part, moved([blocks[4 * i + step] for i in part], step)):
                sums[i] = sums[i] + value
    for step in far_steps()[::-1]:
        keep = len(sums) // 2
        sums = [a + b for a, b in zip(sums[:keep], moved(sums[keep:], step))]
    return sums[0]


def body(hidden, targets, head, global_frag, momentum, peer_delta):
    members = lax.axis_size(AXIS)
    own, depth = hidden.shape
    rows = own * members
    width = head.shape[1]

    packed = call(
        pack_kernel, [((own, depth + LANES), hidden.dtype)], [targets, hidden],
        scratch=[pltpu.SMEM(targets.shape, targets.dtype), pltpu.SemaphoreType.DMA((2,))],
        sources=[pltpu.HBM, pltpu.HBM],
    )[0]
    rows_near, rows_far = gather_rows(packed)
    near = resident(head)

    def part(held, *before):
        count = held.shape[0]
        stats = (8, rows) if before else (count, LANES)
        return call(
            rows_kernel,
            [((count, width), jnp.float32), ((2 * count, width), jnp.bfloat16), (stats, jnp.float32)],
            [held, near, *before], 2 * count * depth * width,
            scratch=[pltpu.VMEM((rows, LANES), jnp.float32)] if before else [],
        )

    logits_near, both_near, columns = part(rows_near)
    logits_far, both_far, mine = part(rows_far, columns)

    lines = mine
    for steps in [[step] for step in far_steps()] + [[1, 2, 3]]:
        before = lines
        lines = call(
            functools.partial(merge_kernel, steps, members),
            [((8, rows), jnp.float32)], [lines] + [swap(lines, step) for step in steps],
        )[0]

    terms = [
        call(
            functools.partial(grad_kernel, first),
            [((2 * rows, depth // 2), jnp.float32)], [both_near, both_far, near, *after],
            2 * rows * depth * width,
        )[0]
        for first, after in ((0, []), (depth // 2, [before]))
    ]

    scale = 2.0**14 * rows
    grads_far, grads_near = (
        call(
            functools.partial(join_kernel, scale, first),
            [((count, depth), jnp.float32)], [lines, mine] + terms,
        )[0]
        for first, count in ((4 * own, rows - 4 * own), (0, 4 * own))
    )
    hidden_grad = (scatter_sums(grads_near, grads_far, own) * (1.0 / scale)).astype(jnp.bfloat16)
    loss = call(functools.partial(loss_kernel, members), [((8, LANES), jnp.float32)], [lines])[0]
    new_global, new_momentum = frag_update(
        jnp.concatenate([rows_near, rows_far], axis=0), lines, [logits_near, logits_far], near,
        global_frag, momentum, peer_delta,
    )
    return (loss[0, :1], hidden_grad, new_global, new_momentum)


def solution(mesh):
    in_specs = (
        P(("outer", "vocab"), None),
        P(("outer", "vocab")),
        P("outer", "vocab"),
        P(None, "vocab"),
        P(None, "vocab"),
        P("outer", "vocab"),
    )
    out_specs = (P("outer"), P(("outer", "vocab"), None), P("outer", "vocab"), P("outer", "vocab"))
    return jax.shard_map(body, mesh=mesh, in_specs=in_specs, out_specs=out_specs, check_vma=False)
```

```python
import functools

import jax
import jax.numpy as jnp
from jax import lax
from jax.experimental import pallas as pl
from jax.experimental.pallas import tpu as pltpu
from jax.sharding import PartitionSpec as P

FRAG = 128
REPLICAS = 4
AXIS = "vocab"
SEND = jnp.float16
LANES = 128
VMEM = pl.BlockSpec(memory_space=pltpu.VMEM)


def call(kernel, outs, operands, flops=0, scratch=(), sources=None, vmem=16 * 2**20, aliases={}):
    outs = [pltpu.VMEM(shape, dtype) for shape, dtype in outs]
    places = sources or [pltpu.VMEM] * len(operands)
    moved = sum(x.size * x.dtype.itemsize for x in operands)
    return pl.pallas_call(
        kernel,
        out_shape=outs,
        in_specs=[pl.BlockSpec(memory_space=place) for place in places],
        out_specs=[VMEM] * len(outs),
        scratch_shapes=list(scratch),
        input_output_aliases=aliases,
        compiler_params=pltpu.CompilerParams(vmem_limit_bytes=vmem),
        cost_estimate=pl.CostEstimate(flops=flops, bytes_accessed=moved, transcendentals=0),
    )(*[pltpu.with_memory_space_constraint(x, place) for x, place in zip(operands, places)])


PARTS = 8
AHEAD = 6


def head_copies(source, target, sems, first, last):
    width = source.shape[1] // PARTS
    copies = []
    for part in range(first, last):
        columns = pl.ds(part * width, width)
        copies.append(pltpu.make_async_copy(source.at[:, columns], target.at[:, columns], sems.at[part]))
    return copies


def load_kernel(head, near_ref, sems):
    copies = head_copies(head, near_ref, sems, 0, AHEAD)
    for copy in copies:
        copy.start()
    for copy in copies:
        copy.wait()


TILE = 512
WIDE = 1024


def pack_kernel(targets, rows, out_ref, targets_ref, sems):
    own, depth = rows.shape
    ids_copy = pltpu.make_async_copy(targets, targets_ref, sems.at[0])
    rows_copy = pltpu.make_async_copy(rows, out_ref.at[:, pl.ds(0, depth)], sems.at[1])
    ids_copy.start()
    rows_copy.start()
    ids_copy.wait()
    place = lax.broadcasted_iota(jnp.int32, (own, LANES), 0)
    ids = jnp.zeros((own, LANES), jnp.int32)
    for i in range(own):
        ids = jnp.where(place == i, targets_ref[i], ids)
    lane = lax.broadcasted_iota(jnp.int32, (own, LANES), 1)
    digits = jnp.where(lane == 0, ids // 256, ids % 256)
    out_ref[:, depth:] = digits.astype(jnp.float32).astype(jnp.bfloat16)
    rows_copy.wait()


def ids_of(digits):
    digits = digits.astype(jnp.float32)
    return (digits[:, 0:1] * 256.0 + digits[:, 1:2]).astype(jnp.int32)


def swap_blocks(value, group):
    size = value.shape[1]
    lane = lax.broadcasted_iota(jnp.int32, value.shape, 1)
    up, down = pltpu.roll(value, group, 1), pltpu.roll(value, size - group, 1)
    return jnp.where((lane & group) != 0, up, down)


def shared_order(value, members):
    me = lax.axis_index(AXIS)
    step = 1
    while step < members:
        swapped = swap_blocks(value, value.shape[1] // members * step)
        value = jnp.where((me & step) != 0, swapped, value)
        step *= 2
    return value


def as_columns(line):
    return jnp.broadcast_to(line, (LANES, line.shape[1])).T[:, 0:1]


def logits_of(rows_ref, near_ref, logits_ref, first, last):
    depth = near_ref.shape[0]
    while first < last:
        part = pl.ds(first, min(WIDE, last - first))
        logits_ref[:, part] = jnp.dot(
            rows_ref[:, :depth], near_ref[:, part], preferred_element_type=jnp.float32
        )
        first += WIDE


def softmax_of(rows_ref, logits_ref, both_ref, columns_ref, first):
    rows, width = logits_ref.shape
    digits = rows_ref.shape[1] - LANES
    chunk = 32
    offset = lax.axis_index(AXIS) * width

    @pl.loop(0, rows // chunk)
    def _(i):
        part = pl.ds(pl.multiple_of(i * chunk, chunk), chunk)
        logits = logits_ref[part, :]
        ids = ids_of(rows_ref[part, digits:]) - offset
        hit = lax.broadcasted_iota(jnp.int32, logits.shape, 1) == ids
        top = jnp.max(logits, axis=1, keepdims=True)
        raised = jnp.exp(logits - top)
        total = jnp.sum(raised, axis=1, keepdims=True)
        pick = jnp.sum(jnp.where(hit, logits, 0.0), axis=1, keepdims=True)
        both_ref[part, :] = jnp.where(hit, 0.0, raised).astype(jnp.bfloat16)
        other = pl.ds(pl.multiple_of(rows + i * chunk, chunk), chunk)
        both_ref[other, :] = jnp.where(hit, 1.0, 0.0).astype(jnp.bfloat16)
        place = lax.broadcasted_iota(jnp.int32, (chunk, LANES), 1)
        slot = pl.ds(pl.multiple_of(first + i * chunk, chunk), chunk)
        columns_ref[slot, :] = jnp.where(place == 0, top, jnp.where(place == 1, total, pick))


def first_kernel(packed_ref, head, held_ref, near_ref, logits_ref, both_ref, columns_ref, sems):
    width = near_ref.shape[1]
    there = width // PARTS * AHEAD
    copies = head_copies(head, near_ref, sems, AHEAD, PARTS)
    for copy in copies:
        copy.start()
    logits_of(packed_ref, near_ref, logits_ref, 0, there)
    for copy in copies:
        copy.wait()
    logits_of(packed_ref, near_ref, logits_ref, there, width)
    softmax_of(packed_ref, logits_ref, both_ref, columns_ref, 0)


def second_kernel(rows_ref, near_ref, before_ref, logits_ref, both_ref, lines_ref, columns_ref):
    first = before_ref.shape[0]
    logits_of(rows_ref, near_ref, logits_ref, 0, near_ref.shape[1])
    softmax_of(rows_ref, logits_ref, both_ref, columns_ref, first)
    columns_ref[pl.ds(0, first), :] = before_ref[...]
    lines_ref[...] = columns_ref[...].T[:8]


def merge_kernel(steps, members, mine_ref, *refs):
    *other_refs, out_ref = refs
    block = mine_ref.shape[1] // members
    me = lax.axis_index(AXIS)
    groups = [mine_ref[...]]
    for step, other_ref in zip(steps, other_refs):
        other, bit = other_ref[...], 1
        while bit <= step:
            if step & bit:
                other = swap_blocks(other, block * bit)
            bit *= 2
        groups.append(other)
    unit, bit = steps[0], 1
    while bit < len(groups):
        upper = (me & (unit * bit)) != 0
        groups = [jnp.where(upper, groups[i ^ bit], group) for i, group in enumerate(groups)]
        bit *= 2
    top = functools.reduce(jnp.maximum, [group[0:1] for group in groups])
    total = sum(group[1:2] * jnp.exp(group[0:1] - top) for group in groups)
    pick = sum(group[2:3] for group in groups)
    place = lax.broadcasted_iota(jnp.int32, out_ref.shape, 0)
    out_ref[...] = jnp.where(place == 0, top, jnp.where(place == 1, total, pick))


def grad_kernel(first, one_ref, two_ref, near_ref, *refs):
    terms_ref = refs[-1]
    tile = min(terms_ref.shape[1], 2**19 // (one_ref.shape[0] + two_ref.shape[0]))
    both = jnp.concatenate([one_ref[...], two_ref[...]], axis=0)
    for place in range(0, terms_ref.shape[1], tile):
        turned = lax.dot_general(
            near_ref[pl.ds(first + place, tile), :], both, (((1,), (1,)), ((), ())),
            preferred_element_type=jnp.float32,
        )
        terms_ref[:, pl.ds(place, tile)] = turned.T


def join_kernel(scale, first, lines_ref, mine_ref, *refs):
    *terms_refs, out_ref = refs
    rows = mine_ref.shape[1]
    top, total = lines_ref[0:1, :], lines_ref[1:2, :]
    soft = as_columns(jnp.exp(mine_ref[0:1, :] - top) / (total * rows)) * scale
    hard = (jnp.exp(mine_ref[2:3, :] - top) / total - 1.0) / rows
    hard = as_columns(hard.astype(jnp.bfloat16).astype(jnp.float32)) * scale

    count = out_ref.shape[0]
    chunk = min(count, 64)
    for place, terms_ref in enumerate(terms_refs):
        columns = pl.ds(place * terms_ref.shape[1], terms_ref.shape[1])
        for i in range(0, count, chunk):
            part = slice(first + i, first + i + chunk)
            out_ref[pl.ds(i, chunk), columns] = (
                soft[part] * terms_ref[pl.ds(2 * first + i, chunk), :]
                + hard[part] * terms_ref[pl.ds(2 * first + count + i, chunk), :]
            )


def loss_kernel(members, lines_ref, loss_ref):
    rows = lines_ref.shape[1]
    lines = shared_order(lines_ref[...], members)
    loss = jnp.sum(lines[0:1] + jnp.log(lines[1:2]) - lines[2:3], axis=1, keepdims=True) / rows
    loss_ref[...] = jnp.broadcast_to(loss, loss_ref.shape)


def frag_kernel(rows_one_ref, rows_two_ref, ids_one_ref, ids_two_ref, lines_ref, one_ref, two_ref, head_ref,
                global_ref, momentum_ref, peer_ref, new_global_ref, new_momentum_ref):
    logits = jnp.concatenate([one_ref[...], two_ref[...]], axis=0)
    held = jnp.concatenate([rows_one_ref[...], rows_two_ref[...]], axis=0)
    ids = jnp.concatenate([ids_of(ids_one_ref[...]), ids_of(ids_two_ref[...])], axis=0)
    rows, tile = logits.shape
    top, total = as_columns(lines_ref[0:1, :]), as_columns(lines_ref[1:2, :])
    offset = (lax.axis_index(AXIS) * pl.num_programs(0) + pl.program_id(0)) * tile
    hit = lax.broadcasted_iota(jnp.int32, (rows, tile), 1) == ids - offset
    shares = jnp.exp(logits - top) / total
    dlogits = ((shares - jnp.where(hit, 1.0, 0.0)) / rows).astype(jnp.bfloat16)
    turned = held.astype(jnp.float32).T.astype(jnp.bfloat16)
    frag_grad = jnp.dot(turned, dlogits, preferred_element_type=jnp.float32)
    local_frag = head_ref[...].astype(jnp.float32) - 1.0 * frag_grad
    pseudo = (global_ref[...] - local_frag + peer_ref[...]) / REPLICAS
    new_momentum = 0.9 * momentum_ref[...] + pseudo
    new_momentum_ref[...] = new_momentum
    new_global_ref[...] = global_ref[...] - 0.7 * (pseudo + 0.9 * new_momentum)


def frag_update(held, ids, lines, logits, near, global_frag, momentum, peer_delta):
    rows = lines.shape[1]
    width = near.shape[1]
    tile = pl.BlockSpec((FRAG, TILE), lambda i: (0, i))

    return pl.pallas_call(
        frag_kernel,
        grid=(width // TILE,),
        out_shape=[jax.ShapeDtypeStruct((FRAG, width), jnp.float32)] * 2,
        in_specs=[pl.BlockSpec((x.shape[0], FRAG), lambda i: (0, 0)) for x in held]
        + [
            pl.BlockSpec((x.shape[0], LANES), lambda i, last=x.shape[1] // LANES - 1: (0, last))
            for x in ids
        ]
        + [pl.BlockSpec((8, rows), lambda i: (0, 0))]
        + [pl.BlockSpec((x.shape[0], TILE), lambda i: (0, i)) for x in logits]
        + [tile] * 4,
        out_specs=[tile, tile],
        compiler_params=pltpu.CompilerParams(vmem_limit_bytes=16 * 2**20),
        cost_estimate=pl.CostEstimate(
            flops=2 * rows * FRAG * width, bytes_accessed=24 * FRAG * width, transcendentals=0
        ),
    )(
        *held, *ids, lines, *[pltpu.with_memory_space_constraint(x, pltpu.VMEM) for x in logits],
        pltpu.with_memory_space_constraint(near, pltpu.VMEM), global_frag, momentum, peer_delta,
    )


def swap(value, step):
    return lax.ppermute(value, AXIS, [(i, i ^ step) for i in range(lax.axis_size(AXIS))])


def far_steps():
    step = 4
    steps = []
    while step < lax.axis_size(AXIS):
        steps.append(step)
        step *= 2
    return steps


def gather_rows(packed):
    own = packed.shape[0]
    held = packed
    for step in far_steps():
        held = jnp.concatenate([held, swap(held, step)], axis=0)
    far = held[own:]
    near = jnp.concatenate([packed] + [swap(packed, step) for step in (1, 2, 3)], axis=0)
    far = jnp.stack([far] + [swap(far, step) for step in (1, 2, 3)])
    count = far.shape[1] // own
    return near, far.reshape(4, count, own, -1).swapaxes(0, 1).reshape(4 * count * own, -1)


def scatter_sums(grads_near, grads_far, own):
    blocks = [
        grads[i * own : (i + 1) * own]
        for grads in (grads_near, grads_far)
        for i in range(grads.shape[0] // own)
    ]
    members = len(blocks)

    def moved(parts, step):
        value = jnp.concatenate([part.astype(SEND) for part in parts], axis=0)
        value = swap(value, step).astype(jnp.float32)
        return [value[i * own : (i + 1) * own] for i in range(len(parts))]

    sums = blocks[::4]
    for part in (list(range(1, members // 4)), [0]):
        for step in (3, 1, 2):
            for i, value in zip(part, moved([blocks[4 * i + step] for i in part], step)):
                sums[i] = sums[i] + value
    for step in far_steps()[::-1]:
        keep = len(sums) // 2
        sums = [a + b for a, b in zip(sums[:keep], moved(sums[keep:], step))]
    return sums[0]


def body(hidden, targets, head, global_frag, momentum, peer_delta):
    members = lax.axis_size(AXIS)
    own, depth = hidden.shape
    rows = own * members
    width = head.shape[1]

    packed = call(
        pack_kernel, [((own, depth + LANES), hidden.dtype)], [targets, hidden],
        scratch=[pltpu.SMEM(targets.shape, targets.dtype), pltpu.SemaphoreType.DMA((2,))],
        sources=[pltpu.HBM, pltpu.HBM],
    )[0]
    rows_near, rows_far = gather_rows(packed)
    near = call(
        load_kernel, [(head.shape, head.dtype)], [head],
        scratch=[pltpu.SemaphoreType.DMA((PARTS,))], sources=[pltpu.HBM],
    )[0]

    count = 4 * own
    near, logits_near, both_near, columns = call(
        first_kernel,
        [(head.shape, head.dtype), ((count, width), jnp.float32), ((2 * count, width), jnp.bfloat16),
         ((count, LANES), jnp.float32)],
        [rows_near, head, near], 2 * count * depth * width,
        scratch=[pltpu.SemaphoreType.DMA((PARTS,))],
        sources=[pltpu.VMEM, pltpu.HBM, pltpu.VMEM], aliases={2: 0},
    )
    count = rows - 4 * own
    logits_far, both_far, mine = call(
        second_kernel,
        [((count, width), jnp.float32), ((2 * count, width), jnp.bfloat16), ((8, rows), jnp.float32)],
        [rows_far, near, columns], 2 * count * depth * width,
        scratch=[pltpu.VMEM((rows, LANES), jnp.float32)],
    )

    lines = mine
    for steps in [[step] for step in far_steps()] + [[1, 2, 3]]:
        before = lines
        lines = call(
            functools.partial(merge_kernel, steps, members),
            [((8, rows), jnp.float32)], [lines] + [swap(lines, step) for step in steps],
        )[0]

    terms = [
        call(
            functools.partial(grad_kernel, first),
            [((2 * rows, depth // 2), jnp.float32)], [both_near, both_far, near, *after],
            2 * rows * depth * width,
        )[0]
        for first, after in ((0, []), (depth // 2, [before]))
    ]

    scale = 2.0**14 * rows
    grads_far, grads_near = (
        call(
            functools.partial(join_kernel, scale, first),
            [((count, depth), jnp.float32)], [lines, mine] + terms,
        )[0]
        for first, count in ((4 * own, rows - 4 * own), (0, 4 * own))
    )
    hidden_grad = (scatter_sums(grads_near, grads_far, own) * (1.0 / scale)).astype(jnp.bfloat16)
    loss = call(functools.partial(loss_kernel, members), [((8, LANES), jnp.float32)], [lines])[0]
    new_global, new_momentum = frag_update(
        [rows_near, rows_far], [rows_near, rows_far], lines, [logits_near, logits_far], near,
        global_frag, momentum, peer_delta,
    )
    return (loss[0, :1], hidden_grad, new_global, new_momentum)


def solution(mesh):
    in_specs = (
        P(("outer", "vocab"), None),
        P(("outer", "vocab")),
        P("outer", "vocab"),
        P(None, "vocab"),
        P(None, "vocab"),
        P("outer", "vocab"),
    )
    out_specs = (P("outer"), P(("outer", "vocab"), None), P("outer", "vocab"), P("outer", "vocab"))
    return jax.shard_map(body, mesh=mesh, in_specs=in_specs, out_specs=out_specs, check_vma=False)
```

```python
import functools

import jax
import jax.numpy as jnp
from jax import lax
from jax.experimental import pallas as pl
from jax.experimental.pallas import tpu as pltpu
from jax.sharding import PartitionSpec as P

FRAG = 128
REPLICAS = 4
AXIS = "vocab"
SEND = jnp.float16
LANES = 128
VMEM = pl.BlockSpec(memory_space=pltpu.VMEM)


def call(kernel, outs, operands, flops=0, scratch=(), sources=None, vmem=16 * 2**20, aliases={}):
    outs = [pltpu.VMEM(shape, dtype) for shape, dtype in outs]
    places = sources or [pltpu.VMEM] * len(operands)
    moved = sum(x.size * x.dtype.itemsize for x in operands)
    return pl.pallas_call(
        kernel,
        out_shape=outs,
        in_specs=[pl.BlockSpec(memory_space=place) for place in places],
        out_specs=[VMEM] * len(outs),
        scratch_shapes=list(scratch),
        input_output_aliases=aliases,
        compiler_params=pltpu.CompilerParams(vmem_limit_bytes=vmem),
        cost_estimate=pl.CostEstimate(flops=flops, bytes_accessed=moved, transcendentals=0),
    )(*[pltpu.with_memory_space_constraint(x, place) for x, place in zip(operands, places)])


PARTS = 8
AHEAD = 6


def head_copies(source, target, sems, first, last):
    width = source.shape[1] // PARTS
    copies = []
    for part in range(first, last):
        columns = pl.ds(part * width, width)
        copies.append(pltpu.make_async_copy(source.at[:, columns], target.at[:, columns], sems.at[part]))
    return copies


def load_kernel(head, near_ref, sems):
    copies = head_copies(head, near_ref, sems, 0, AHEAD)
    for copy in copies:
        copy.start()
    for copy in copies:
        copy.wait()


TILE = 512
WIDE = 1024


def pack_kernel(targets, rows, out_ref, targets_ref, sems):
    own, depth = rows.shape
    ids_copy = pltpu.make_async_copy(targets, targets_ref, sems.at[0])
    rows_copy = pltpu.make_async_copy(rows, out_ref.at[:, pl.ds(0, depth)], sems.at[1])
    ids_copy.start()
    rows_copy.start()
    ids_copy.wait()
    place = lax.broadcasted_iota(jnp.int32, (own, LANES), 0)
    ids = jnp.zeros((own, LANES), jnp.int32)
    for i in range(own):
        ids = jnp.where(place == i, targets_ref[i], ids)
    lane = lax.broadcasted_iota(jnp.int32, (own, LANES), 1)
    digits = jnp.where(lane == 0, ids // 256, ids % 256)
    out_ref[:, depth:] = digits.astype(jnp.float32).astype(jnp.bfloat16)
    rows_copy.wait()


def ids_of(digits):
    digits = digits.astype(jnp.float32)
    return (digits[:, 0:1] * 256.0 + digits[:, 1:2]).astype(jnp.int32)


def swap_blocks(value, group):
    size = value.shape[1]
    lane = lax.broadcasted_iota(jnp.int32, value.shape, 1)
    up, down = pltpu.roll(value, group, 1), pltpu.roll(value, size - group, 1)
    return jnp.where((lane & group) != 0, up, down)


def shared_order(value, members):
    me = lax.axis_index(AXIS)
    step = 1
    while step < members:
        swapped = swap_blocks(value, value.shape[1] // members * step)
        value = jnp.where((me & step) != 0, swapped, value)
        step *= 2
    return value


def as_columns(line):
    return jnp.broadcast_to(line, (LANES, line.shape[1])).T[:, 0:1]


def logits_of(rows_ref, near_ref, logits_ref, first, last):
    depth = near_ref.shape[0]
    while first < last:
        part = pl.ds(first, min(WIDE, last - first))
        logits_ref[:, part] = jnp.dot(
            rows_ref[:, :depth], near_ref[:, part], preferred_element_type=jnp.float32
        )
        first += WIDE


def softmax_of(rows_ref, logits_ref, both_ref, columns_ref, first):
    rows, width = logits_ref.shape
    digits = rows_ref.shape[1] - LANES
    chunk = 32
    offset = lax.axis_index(AXIS) * width

    @pl.loop(0, rows // chunk)
    def _(i):
        part = pl.ds(pl.multiple_of(i * chunk, chunk), chunk)
        logits = logits_ref[part, :]
        ids = ids_of(rows_ref[part, digits:]) - offset
        hit = lax.broadcasted_iota(jnp.int32, logits.shape, 1) == ids
        top = jnp.max(logits, axis=1, keepdims=True)
        raised = jnp.exp(logits - top)
        total = jnp.sum(raised, axis=1, keepdims=True)
        pick = jnp.sum(jnp.where(hit, logits, 0.0), axis=1, keepdims=True)
        both_ref[part, :] = jnp.where(hit, 0.0, raised).astype(jnp.bfloat16)
        other = pl.ds(pl.multiple_of(rows + i * chunk, chunk), chunk)
        both_ref[other, :] = jnp.where(hit, 1.0, 0.0).astype(jnp.bfloat16)
        place = lax.broadcasted_iota(jnp.int32, (chunk, LANES), 1)
        slot = pl.ds(pl.multiple_of(first + i * chunk, chunk), chunk)
        columns_ref[slot, :] = jnp.where(place == 0, top, jnp.where(place == 1, total, pick))


def first_kernel(packed_ref, head, held_ref, near_ref, logits_ref, both_ref, columns_ref, sems):
    width = near_ref.shape[1]
    there = width // PARTS * AHEAD
    copies = head_copies(head, near_ref, sems, AHEAD, PARTS)
    for copy in copies:
        copy.start()
    logits_of(packed_ref, near_ref, logits_ref, 0, there)
    for copy in copies:
        copy.wait()
    logits_of(packed_ref, near_ref, logits_ref, there, width)
    softmax_of(packed_ref, logits_ref, both_ref, columns_ref, 0)


def second_kernel(rows_ref, near_ref, before_ref, logits_ref, both_ref, lines_ref, columns_ref):
    first = before_ref.shape[0]
    logits_of(rows_ref, near_ref, logits_ref, 0, near_ref.shape[1])
    softmax_of(rows_ref, logits_ref, both_ref, columns_ref, first)
    columns_ref[pl.ds(0, first), :] = before_ref[...]
    lines_ref[...] = columns_ref[...].T[:8]


def merge_kernel(steps, members, mine_ref, *refs):
    *other_refs, out_ref = refs
    block = mine_ref.shape[1] // members
    me = lax.axis_index(AXIS)
    groups = [mine_ref[...]]
    for step, other_ref in zip(steps, other_refs):
        other, bit = other_ref[...], 1
        while bit <= step:
            if step & bit:
                other = swap_blocks(other, block * bit)
            bit *= 2
        groups.append(other)
    unit, bit = steps[0], 1
    while bit < len(groups):
        upper = (me & (unit * bit)) != 0
        groups = [jnp.where(upper, groups[i ^ bit], group) for i, group in enumerate(groups)]
        bit *= 2
    top = functools.reduce(jnp.maximum, [group[0:1] for group in groups])
    total = sum(group[1:2] * jnp.exp(group[0:1] - top) for group in groups)
    pick = sum(group[2:3] for group in groups)
    place = lax.broadcasted_iota(jnp.int32, out_ref.shape, 0)
    out_ref[...] = jnp.where(place == 0, top, jnp.where(place == 1, total, pick))


def grad_kernel(first, one_ref, two_ref, near_ref, *refs):
    terms_ref = refs[-1]
    tile = min(terms_ref.shape[1], 2**19 // (one_ref.shape[0] + two_ref.shape[0]))
    both = jnp.concatenate([one_ref[...], two_ref[...]], axis=0)
    for place in range(0, terms_ref.shape[1], tile):
        turned = lax.dot_general(
            near_ref[pl.ds(first + place, tile), :], both, (((1,), (1,)), ((), ())),
            preferred_element_type=jnp.float32,
        )
        terms_ref[:, pl.ds(place, tile)] = turned.T


def join_kernel(scale, first, lines_ref, mine_ref, *refs):
    *terms_refs, out_ref = refs
    rows = mine_ref.shape[1]
    top, total = lines_ref[0:1, :], lines_ref[1:2, :]
    soft = as_columns(jnp.exp(mine_ref[0:1, :] - top) / (total * rows)) * scale
    hard = (jnp.exp(mine_ref[2:3, :] - top) / total - 1.0) / rows
    hard = as_columns(hard.astype(jnp.bfloat16).astype(jnp.float32)) * scale

    count = out_ref.shape[0]
    chunk = min(count, 64)
    for place, terms_ref in enumerate(terms_refs):
        columns = pl.ds(place * terms_ref.shape[1], terms_ref.shape[1])
        for i in range(0, count, chunk):
            part = slice(first + i, first + i + chunk)
            out_ref[pl.ds(i, chunk), columns] = (
                soft[part] * terms_ref[pl.ds(2 * first + i, chunk), :]
                + hard[part] * terms_ref[pl.ds(2 * first + count + i, chunk), :]
            )


def loss_kernel(members, lines_ref, loss_ref):
    rows = lines_ref.shape[1]
    lines = shared_order(lines_ref[...], members)
    loss = jnp.sum(lines[0:1] + jnp.log(lines[1:2]) - lines[2:3], axis=1, keepdims=True) / rows
    loss_ref[...] = jnp.broadcast_to(loss, loss_ref.shape)


def frag_kernel(rows_one_ref, rows_two_ref, ids_one_ref, ids_two_ref, lines_ref, one_ref, two_ref, head_ref,
                global_ref, momentum_ref, peer_ref, new_global_ref, new_momentum_ref):
    logits = jnp.concatenate([one_ref[...], two_ref[...]], axis=0)
    held = jnp.concatenate([rows_one_ref[...], rows_two_ref[...]], axis=0)
    ids = jnp.concatenate([ids_of(ids_one_ref[...]), ids_of(ids_two_ref[...])], axis=0)
    rows, tile = logits.shape
    top, total = as_columns(lines_ref[0:1, :]), as_columns(lines_ref[1:2, :])
    offset = (lax.axis_index(AXIS) * pl.num_programs(0) + pl.program_id(0)) * tile
    hit = lax.broadcasted_iota(jnp.int32, (rows, tile), 1) == ids - offset
    shares = jnp.exp(logits - top) / total
    dlogits = ((shares - jnp.where(hit, 1.0, 0.0)) / rows).astype(jnp.bfloat16)
    turned = held.astype(jnp.float32).T.astype(jnp.bfloat16)
    frag_grad = jnp.dot(turned, dlogits, preferred_element_type=jnp.float32)
    local_frag = head_ref[...].astype(jnp.float32) - 1.0 * frag_grad
    pseudo = (global_ref[...] - local_frag + peer_ref[...]) / REPLICAS
    new_momentum = 0.9 * momentum_ref[...] + pseudo
    new_momentum_ref[...] = new_momentum
    new_global_ref[...] = global_ref[...] - 0.7 * (pseudo + 0.9 * new_momentum)


def frag_update(held, ids, lines, logits, near, global_frag, momentum, peer_delta):
    rows = lines.shape[1]
    width = near.shape[1]
    tile = pl.BlockSpec((FRAG, TILE), lambda i: (0, i))

    return pl.pallas_call(
        frag_kernel,
        grid=(width // TILE,),
        out_shape=[jax.ShapeDtypeStruct((FRAG, width), jnp.float32)] * 2,
        in_specs=[pl.BlockSpec((x.shape[0], FRAG), lambda i: (0, 0)) for x in held]
        + [
            pl.BlockSpec((x.shape[0], LANES), lambda i, last=x.shape[1] // LANES - 1: (0, last))
            for x in ids
        ]
        + [pl.BlockSpec((8, rows), lambda i: (0, 0))]
        + [pl.BlockSpec((x.shape[0], TILE), lambda i: (0, i)) for x in logits]
        + [tile] * 4,
        out_specs=[tile, tile],
        compiler_params=pltpu.CompilerParams(vmem_limit_bytes=16 * 2**20),
        cost_estimate=pl.CostEstimate(
            flops=2 * rows * FRAG * width, bytes_accessed=24 * FRAG * width, transcendentals=0
        ),
    )(
        *held, *ids, lines, *[pltpu.with_memory_space_constraint(x, pltpu.VMEM) for x in logits],
        pltpu.with_memory_space_constraint(near, pltpu.VMEM), global_frag, momentum, peer_delta,
    )


def swap(value, step):
    return lax.ppermute(value, AXIS, [(i, i ^ step) for i in range(lax.axis_size(AXIS))])


def far_steps():
    step = 4
    steps = []
    while step < lax.axis_size(AXIS):
        steps.append(step)
        step *= 2
    return steps


def gather_rows(packed):
    own = packed.shape[0]
    held = packed
    for step in far_steps():
        held = jnp.concatenate([held, swap(held, step)], axis=0)
    far = held[own:]
    near = jnp.concatenate([packed] + [swap(packed, step) for step in (1, 2, 3)], axis=0)
    far = jnp.stack([far] + [swap(far, step) for step in (1, 2, 3)])
    count = far.shape[1] // own
    return near, far.reshape(4, count, own, -1).swapaxes(0, 1).reshape(4 * count * own, -1)


def scatter_sums(grads_near, grads_far, own):
    blocks = [
        grads[i * own : (i + 1) * own]
        for grads in (grads_near, grads_far)
        for i in range(grads.shape[0] // own)
    ]
    members = len(blocks)

    def moved(parts, step):
        value = jnp.concatenate([part.astype(SEND) for part in parts], axis=0)
        value = swap(value, step).astype(jnp.float32)
        return [value[i * own : (i + 1) * own] for i in range(len(parts))]

    far = range(4, members, 4)
    three = moved([blocks[i ^ 3] for i in far], 3)
    two = moved([blocks[i ^ 2] for i in far], 2)
    one = moved([blocks[i ^ 1] for i in far], 1)
    relayed = moved([blocks[3]], 1)[0]
    y_near = moved([blocks[1]], 1)[0]
    z_near = moved([blocks[2] + relayed], 2)[0]
    sums = [blocks[0] + z_near + y_near]
    sums += [blocks[i] + a + b + c for i, a, b, c in zip(far, three, one, two)]
    for step in far_steps()[::-1]:
        keep = len(sums) // 2
        sums = [a + b for a, b in zip(sums[:keep], moved(sums[keep:], step))]
    return sums[0]


def body(hidden, targets, head, global_frag, momentum, peer_delta):
    members = lax.axis_size(AXIS)
    own, depth = hidden.shape
    rows = own * members
    width = head.shape[1]

    packed = call(
        pack_kernel, [((own, depth + LANES), hidden.dtype)], [targets, hidden],
        scratch=[pltpu.SMEM(targets.shape, targets.dtype), pltpu.SemaphoreType.DMA((2,))],
        sources=[pltpu.HBM, pltpu.HBM],
    )[0]
    rows_near, rows_far = gather_rows(packed)
    near = call(
        load_kernel, [(head.shape, head.dtype)], [head],
        scratch=[pltpu.SemaphoreType.DMA((PARTS,))], sources=[pltpu.HBM],
    )[0]

    count = 4 * own
    near, logits_near, both_near, columns = call(
        first_kernel,
        [(head.shape, head.dtype), ((count, width), jnp.float32), ((2 * count, width), jnp.bfloat16),
         ((count, LANES), jnp.float32)],
        [rows_near, head, near], 2 * count * depth * width,
        scratch=[pltpu.SemaphoreType.DMA((PARTS,))],
        sources=[pltpu.VMEM, pltpu.HBM, pltpu.VMEM], aliases={2: 0},
    )
    count = rows - 4 * own
    logits_far, both_far, mine = call(
        second_kernel,
        [((count, width), jnp.float32), ((2 * count, width), jnp.bfloat16), ((8, rows), jnp.float32)],
        [rows_far, near, columns], 2 * count * depth * width,
        scratch=[pltpu.VMEM((rows, LANES), jnp.float32)],
    )

    lines = mine
    for steps in [[step] for step in far_steps()] + [[1, 2, 3]]:
        before = lines
        lines = call(
            functools.partial(merge_kernel, steps, members),
            [((8, rows), jnp.float32)], [lines] + [swap(lines, step) for step in steps],
        )[0]

    terms = [
        call(
            functools.partial(grad_kernel, first),
            [((2 * rows, depth // 2), jnp.float32)], [both_near, both_far, near, *after],
            2 * rows * depth * width,
        )[0]
        for first, after in ((0, []), (depth // 2, [before]))
    ]

    scale = 2.0**14 * rows
    grads_far, grads_near = (
        call(
            functools.partial(join_kernel, scale, first),
            [((count, depth), jnp.float32)], [lines, mine] + terms,
        )[0]
        for first, count in ((4 * own, rows - 4 * own), (0, 4 * own))
    )
    hidden_grad = (scatter_sums(grads_near, grads_far, own) * (1.0 / scale)).astype(jnp.bfloat16)
    loss = call(functools.partial(loss_kernel, members), [((8, LANES), jnp.float32)], [lines])[0]
    new_global, new_momentum = frag_update(
        [rows_near, rows_far], [rows_near, rows_far], lines, [logits_near, logits_far], near,
        global_frag, momentum, peer_delta,
    )
    return (loss[0, :1], hidden_grad, new_global, new_momentum)


def solution(mesh):
    in_specs = (
        P(("outer", "vocab"), None),
        P(("outer", "vocab")),
        P("outer", "vocab"),
        P(None, "vocab"),
        P(None, "vocab"),
        P("outer", "vocab"),
    )
    out_specs = (P("outer"), P(("outer", "vocab"), None), P("outer", "vocab"), P("outer", "vocab"))
    return jax.shard_map(body, mesh=mesh, in_specs=in_specs, out_specs=out_specs, check_vma=False)
```

```python
import functools

import jax
import jax.numpy as jnp
from jax import lax
from jax.experimental import pallas as pl
from jax.experimental.pallas import tpu as pltpu
from jax.sharding import PartitionSpec as P

FRAG = 128
REPLICAS = 4
AXIS = "vocab"
SEND = jnp.float16
LANES = 128
VMEM = pl.BlockSpec(memory_space=pltpu.VMEM)


def call(kernel, outs, operands, flops=0, scratch=(), sources=None, vmem=16 * 2**20, aliases={}):
    outs = [pltpu.VMEM(shape, dtype) for shape, dtype in outs]
    places = sources or [pltpu.VMEM] * len(operands)
    moved = sum(x.size * x.dtype.itemsize for x in operands)
    return pl.pallas_call(
        kernel,
        out_shape=outs,
        in_specs=[pl.BlockSpec(memory_space=place) for place in places],
        out_specs=[VMEM] * len(outs),
        scratch_shapes=list(scratch),
        input_output_aliases=aliases,
        compiler_params=pltpu.CompilerParams(vmem_limit_bytes=vmem),
        cost_estimate=pl.CostEstimate(flops=flops, bytes_accessed=moved, transcendentals=0),
    )(*[pltpu.with_memory_space_constraint(x, place) for x, place in zip(operands, places)])


PARTS = 8
AHEAD = 6


def head_copies(source, target, sems, first, last):
    width = source.shape[1] // PARTS
    copies = []
    for part in range(first, last):
        columns = pl.ds(part * width, width)
        copies.append(pltpu.make_async_copy(source.at[:, columns], target.at[:, columns], sems.at[part]))
    return copies


def load_kernel(head, near_ref, sems):
    copies = head_copies(head, near_ref, sems, 0, AHEAD)
    for copy in copies:
        copy.start()
    for copy in copies:
        copy.wait()


TILE = 1024
WIDE = 1024


def pack_kernel(targets, rows, out_ref, targets_ref, sems):
    own, depth = rows.shape
    ids_copy = pltpu.make_async_copy(targets, targets_ref, sems.at[0])
    rows_copy = pltpu.make_async_copy(rows, out_ref.at[:, pl.ds(0, depth)], sems.at[1])
    ids_copy.start()
    rows_copy.start()
    ids_copy.wait()
    place = lax.broadcasted_iota(jnp.int32, (own, LANES), 0)
    ids = jnp.zeros((own, LANES), jnp.int32)
    for i in range(own):
        ids = jnp.where(place == i, targets_ref[i], ids)
    lane = lax.broadcasted_iota(jnp.int32, (own, LANES), 1)
    digits = jnp.where(lane == 0, ids // 256, ids % 256)
    out_ref[:, depth:] = digits.astype(jnp.float32).astype(jnp.bfloat16)
    rows_copy.wait()


def ids_of(digits):
    digits = digits.astype(jnp.float32)
    return (digits[:, 0:1] * 256.0 + digits[:, 1:2]).astype(jnp.int32)


def swap_blocks(value, group):
    size = value.shape[1]
    lane = lax.broadcasted_iota(jnp.int32, value.shape, 1)
    up, down = pltpu.roll(value, group, 1), pltpu.roll(value, size - group, 1)
    return jnp.where((lane & group) != 0, up, down)


def shared_order(value, members):
    me = lax.axis_index(AXIS)
    step = 1
    while step < members:
        swapped = swap_blocks(value, value.shape[1] // members * step)
        value = jnp.where((me & step) != 0, swapped, value)
        step *= 2
    return value


def as_columns(line):
    return jnp.broadcast_to(line, (LANES, line.shape[1])).T[:, 0:1]


def logits_of(rows_ref, near_ref, logits_ref, first, last):
    depth = near_ref.shape[0]
    while first < last:
        part = pl.ds(first, min(WIDE, last - first))
        logits_ref[:, part] = jnp.dot(
            rows_ref[:, :depth], near_ref[:, part], preferred_element_type=jnp.float32
        )
        first += WIDE


def softmax_of(rows_ref, logits_ref, both_ref, columns_ref, first):
    rows, width = logits_ref.shape
    digits = rows_ref.shape[1] - LANES
    chunk = 32
    offset = lax.axis_index(AXIS) * width

    @pl.loop(0, rows // chunk)
    def _(i):
        part = pl.ds(pl.multiple_of(i * chunk, chunk), chunk)
        logits = logits_ref[part, :]
        ids = ids_of(rows_ref[part, digits:]) - offset
        hit = lax.broadcasted_iota(jnp.int32, logits.shape, 1) == ids
        top = jnp.max(logits, axis=1, keepdims=True)
        raised = jnp.exp(logits - top)
        total = jnp.sum(raised, axis=1, keepdims=True)
        pick = jnp.sum(jnp.where(hit, logits, 0.0), axis=1, keepdims=True)
        both_ref[part, :] = jnp.where(hit, 0.0, raised).astype(jnp.bfloat16)
        other = pl.ds(pl.multiple_of(rows + i * chunk, chunk), chunk)
        both_ref[other, :] = jnp.where(hit, 1.0, 0.0).astype(jnp.bfloat16)
        place = lax.broadcasted_iota(jnp.int32, (chunk, LANES), 1)
        slot = pl.ds(pl.multiple_of(first + i * chunk, chunk), chunk)
        columns_ref[slot, :] = jnp.where(place == 0, top, jnp.where(place == 1, total, pick))


def first_kernel(packed_ref, head, held_ref, near_ref, logits_ref, both_ref, columns_ref, sems):
    width = near_ref.shape[1]
    there = width // PARTS * AHEAD
    copies = head_copies(head, near_ref, sems, AHEAD, PARTS)
    for copy in copies:
        copy.start()
    logits_of(packed_ref, near_ref, logits_ref, 0, there)
    for copy in copies:
        copy.wait()
    logits_of(packed_ref, near_ref, logits_ref, there, width)
    softmax_of(packed_ref, logits_ref, both_ref, columns_ref, 0)


def second_kernel(rows_ref, near_ref, before_ref, logits_ref, both_ref, lines_ref, columns_ref):
    first = before_ref.shape[0]
    logits_of(rows_ref, near_ref, logits_ref, 0, near_ref.shape[1])
    softmax_of(rows_ref, logits_ref, both_ref, columns_ref, first)
    columns_ref[pl.ds(0, first), :] = before_ref[...]
    lines_ref[...] = columns_ref[...].T[:8]


def merge_kernel(steps, members, mine_ref, *refs):
    *other_refs, out_ref = refs
    block = mine_ref.shape[1] // members
    me = lax.axis_index(AXIS)
    groups = [mine_ref[...]]
    for step, other_ref in zip(steps, other_refs):
        other, bit = other_ref[...], 1
        while bit <= step:
            if step & bit:
                other = swap_blocks(other, block * bit)
            bit *= 2
        groups.append(other)
    unit, bit = steps[0], 1
    while bit < len(groups):
        upper = (me & (unit * bit)) != 0
        groups = [jnp.where(upper, groups[i ^ bit], group) for i, group in enumerate(groups)]
        bit *= 2
    top = functools.reduce(jnp.maximum, [group[0:1] for group in groups])
    total = sum(group[1:2] * jnp.exp(group[0:1] - top) for group in groups)
    pick = sum(group[2:3] for group in groups)
    place = lax.broadcasted_iota(jnp.int32, out_ref.shape, 0)
    out_ref[...] = jnp.where(place == 0, top, jnp.where(place == 1, total, pick))


def grad_kernel(first, one_ref, two_ref, near_ref, *refs):
    terms_ref = refs[-1]
    tile = min(terms_ref.shape[1], 2**19 // (one_ref.shape[0] + two_ref.shape[0]))
    both = jnp.concatenate([one_ref[...], two_ref[...]], axis=0)
    for place in range(0, terms_ref.shape[1], tile):
        turned = lax.dot_general(
            near_ref[pl.ds(first + place, tile), :], both, (((1,), (1,)), ((), ())),
            preferred_element_type=jnp.float32,
        )
        terms_ref[:, pl.ds(place, tile)] = turned.T


def join_kernel(scale, first, lines_ref, mine_ref, *refs):
    *terms_refs, out_ref = refs
    rows = mine_ref.shape[1]
    top, total = lines_ref[0:1, :], lines_ref[1:2, :]
    soft = as_columns(jnp.exp(mine_ref[0:1, :] - top) / (total * rows)) * scale
    hard = (jnp.exp(mine_ref[2:3, :] - top) / total - 1.0) / rows
    hard = as_columns(hard.astype(jnp.bfloat16).astype(jnp.float32)) * scale

    count = out_ref.shape[0]
    chunk = min(count, 64)
    for place, terms_ref in enumerate(terms_refs):
        columns = pl.ds(place * terms_ref.shape[1], terms_ref.shape[1])
        for i in range(0, count, chunk):
            part = slice(first + i, first + i + chunk)
            out_ref[pl.ds(i, chunk), columns] = (
                soft[part] * terms_ref[pl.ds(2 * first + i, chunk), :]
                + hard[part] * terms_ref[pl.ds(2 * first + count + i, chunk), :]
            )


def frag_kernel(members, rows_one_ref, rows_two_ref, ids_one_ref, ids_two_ref, lines_ref, one_ref, two_ref, head_ref,
                global_ref, momentum_ref, peer_ref, new_global_ref, new_momentum_ref, loss_ref):
    logits = jnp.concatenate([one_ref[...], two_ref[...]], axis=0)
    held = jnp.concatenate([rows_one_ref[...], rows_two_ref[...]], axis=0)
    ids = jnp.concatenate([ids_of(ids_one_ref[...]), ids_of(ids_two_ref[...])], axis=0)
    rows, tile = logits.shape

    @pl.when(pl.program_id(0) == 0)
    def _():
        lines = shared_order(lines_ref[...], members)
        loss_ref[0] = jnp.sum(lines[0:1] + jnp.log(lines[1:2]) - lines[2:3]) / rows

    top, share = as_columns(lines_ref[0:1, :]), as_columns(1.0 / lines_ref[1:2, :])
    offset = (lax.axis_index(AXIS) * pl.num_programs(0) + pl.program_id(0)) * tile
    hit = lax.broadcasted_iota(jnp.int32, (rows, tile), 1) == ids - offset
    shares = jnp.exp(logits - top) * share
    dlogits = ((shares - jnp.where(hit, 1.0, 0.0)) * (1.0 / rows)).astype(jnp.bfloat16)
    turned = held.astype(jnp.float32).T.astype(jnp.bfloat16)
    frag_grad = jnp.dot(turned, dlogits, preferred_element_type=jnp.float32)
    local_frag = head_ref[...].astype(jnp.float32) - 1.0 * frag_grad
    pseudo = (global_ref[...] - local_frag + peer_ref[...]) / REPLICAS
    new_momentum = 0.9 * momentum_ref[...] + pseudo
    new_momentum_ref[...] = new_momentum
    new_global_ref[...] = global_ref[...] - 0.7 * (pseudo + 0.9 * new_momentum)


def frag_update(members, held, ids, lines, logits, near, global_frag, momentum, peer_delta):
    rows = lines.shape[1]
    width = near.shape[1]
    tile = pl.BlockSpec((FRAG, TILE), lambda i: (0, i))

    return pl.pallas_call(
        functools.partial(frag_kernel, members),
        grid=(width // TILE,),
        out_shape=[jax.ShapeDtypeStruct((FRAG, width), jnp.float32)] * 2
        + [jax.ShapeDtypeStruct((1,), jnp.float32)],
        in_specs=[pl.BlockSpec((x.shape[0], FRAG), lambda i: (0, 0)) for x in held]
        + [
            pl.BlockSpec((x.shape[0], LANES), lambda i, last=x.shape[1] // LANES - 1: (0, last))
            for x in ids
        ]
        + [pl.BlockSpec((8, rows), lambda i: (0, 0))]
        + [pl.BlockSpec((x.shape[0], TILE), lambda i: (0, i)) for x in logits]
        + [tile] * 4,
        out_specs=[tile, tile, pl.BlockSpec(memory_space=pltpu.SMEM)],
        compiler_params=pltpu.CompilerParams(vmem_limit_bytes=16 * 2**20),
        cost_estimate=pl.CostEstimate(
            flops=2 * rows * FRAG * width, bytes_accessed=24 * FRAG * width, transcendentals=0
        ),
    )(
        *held, *ids, lines, *[pltpu.with_memory_space_constraint(x, pltpu.VMEM) for x in logits],
        pltpu.with_memory_space_constraint(near, pltpu.VMEM), global_frag, momentum, peer_delta,
    )


def swap(value, step):
    return lax.ppermute(value, AXIS, [(i, i ^ step) for i in range(lax.axis_size(AXIS))])


def far_steps():
    step = 4
    steps = []
    while step < lax.axis_size(AXIS):
        steps.append(step)
        step *= 2
    return steps


def gather_rows(packed):
    own = packed.shape[0]
    held = packed
    for step in far_steps():
        held = jnp.concatenate([held, swap(held, step)], axis=0)
    far = held[own:]
    near = jnp.concatenate([packed] + [swap(packed, step) for step in (1, 2, 3)], axis=0)
    far = jnp.stack([far] + [swap(far, step) for step in (1, 2, 3)])
    count = far.shape[1] // own
    return near, far.reshape(4, count, own, -1).swapaxes(0, 1).reshape(4 * count * own, -1)


def scatter_sums(grads_near, grads_far, own):
    blocks = [
        grads[i * own : (i + 1) * own]
        for grads in (grads_near, grads_far)
        for i in range(grads.shape[0] // own)
    ]
    members = len(blocks)

    def moved(parts, step):
        value = jnp.concatenate([part.astype(SEND) for part in parts], axis=0)
        value = swap(value, step).astype(jnp.float32)
        return [value[i * own : (i + 1) * own] for i in range(len(parts))]

    far = range(4, members, 4)
    three = moved([blocks[i ^ 3] for i in far], 3)
    two = moved([blocks[i ^ 2] for i in far], 2)
    one = moved([blocks[i ^ 1] for i in far], 1)
    relayed = moved([blocks[3]], 1)[0]
    y_near = moved([blocks[1]], 1)[0]
    z_near = moved([blocks[2] + relayed], 2)[0]
    sums = [blocks[0] + z_near + y_near]
    sums += [blocks[i] + a + b + c for i, a, b, c in zip(far, three, one, two)]
    for step in far_steps()[::-1]:
        keep = len(sums) // 2
        sums = [a + b for a, b in zip(sums[:keep], moved(sums[keep:], step))]
    return sums[0]


def body(hidden, targets, head, global_frag, momentum, peer_delta):
    members = lax.axis_size(AXIS)
    own, depth = hidden.shape
    rows = own * members
    width = head.shape[1]

    packed = call(
        pack_kernel, [((own, depth + LANES), hidden.dtype)], [targets, hidden],
        scratch=[pltpu.SMEM(targets.shape, targets.dtype), pltpu.SemaphoreType.DMA((2,))],
        sources=[pltpu.HBM, pltpu.HBM],
    )[0]
    rows_near, rows_far = gather_rows(packed)
    near = call(
        load_kernel, [(head.shape, head.dtype)], [head],
        scratch=[pltpu.SemaphoreType.DMA((PARTS,))], sources=[pltpu.HBM],
    )[0]

    count = 4 * own
    near, logits_near, both_near, columns = call(
        first_kernel,
        [(head.shape, head.dtype), ((count, width), jnp.float32), ((2 * count, width), jnp.bfloat16),
         ((count, LANES), jnp.float32)],
        [rows_near, head, near], 2 * count * depth * width,
        scratch=[pltpu.SemaphoreType.DMA((PARTS,))],
        sources=[pltpu.VMEM, pltpu.HBM, pltpu.VMEM], aliases={2: 0},
    )
    count = rows - 4 * own
    logits_far, both_far, mine = call(
        second_kernel,
        [((count, width), jnp.float32), ((2 * count, width), jnp.bfloat16), ((8, rows), jnp.float32)],
        [rows_far, near, columns], 2 * count * depth * width,
        scratch=[pltpu.VMEM((rows, LANES), jnp.float32)],
    )

    lines = mine
    for steps in [[step] for step in far_steps()] + [[1, 2, 3]]:
        before = lines
        lines = call(
            functools.partial(merge_kernel, steps, members),
            [((8, rows), jnp.float32)], [lines] + [swap(lines, step) for step in steps],
        )[0]

    terms = [
        call(
            functools.partial(grad_kernel, first),
            [((2 * rows, depth // 2), jnp.float32)], [both_near, both_far, near, *after],
            2 * rows * depth * width,
        )[0]
        for first, after in ((0, []), (depth // 2, [before]))
    ]

    scale = 2.0**14 * rows
    grads_far, grads_near = (
        call(
            functools.partial(join_kernel, scale, first),
            [((count, depth), jnp.float32)], [lines, mine] + terms,
        )[0]
        for first, count in ((4 * own, rows - 4 * own), (0, 4 * own))
    )
    hidden_grad = (scatter_sums(grads_near, grads_far, own) * (1.0 / scale)).astype(jnp.bfloat16)
    new_global, new_momentum, loss = frag_update(
        members, [rows_near, rows_far], [rows_near, rows_far], lines, [logits_near, logits_far], near,
        global_frag, momentum, peer_delta,
    )
    return (loss, hidden_grad, new_global, new_momentum)


def solution(mesh):
    in_specs = (
        P(("outer", "vocab"), None),
        P(("outer", "vocab")),
        P("outer", "vocab"),
        P(None, "vocab"),
        P(None, "vocab"),
        P("outer", "vocab"),
    )
    out_specs = (P("outer"), P(("outer", "vocab"), None), P("outer", "vocab"), P("outer", "vocab"))
    return jax.shard_map(body, mesh=mesh, in_specs=in_specs, out_specs=out_specs, check_vma=False)
```

```python
import functools

import jax
import jax.numpy as jnp
from jax import lax
from jax.experimental import pallas as pl
from jax.experimental.pallas import tpu as pltpu
from jax.sharding import PartitionSpec as P

FRAG = 128
REPLICAS = 4
AXIS = "vocab"
SEND = jnp.float16
LANES = 128
VMEM = pl.BlockSpec(memory_space=pltpu.VMEM)


def call(kernel, outs, operands, flops=0, scratch=(), sources=None, vmem=16 * 2**20, aliases={}):
    outs = [pltpu.VMEM(shape, dtype) for shape, dtype in outs]
    places = sources or [pltpu.VMEM] * len(operands)
    moved = sum(x.size * x.dtype.itemsize for x in operands)
    return pl.pallas_call(
        kernel,
        out_shape=outs,
        in_specs=[pl.BlockSpec(memory_space=place) for place in places],
        out_specs=[VMEM] * len(outs),
        scratch_shapes=list(scratch),
        input_output_aliases=aliases,
        compiler_params=pltpu.CompilerParams(vmem_limit_bytes=vmem),
        cost_estimate=pl.CostEstimate(flops=flops, bytes_accessed=moved, transcendentals=0),
    )(*[pltpu.with_memory_space_constraint(x, place) for x, place in zip(operands, places)])


PARTS = 8
AHEAD = 6


def head_copies(source, target, sems, first, last):
    width = source.shape[1] // PARTS
    copies = []
    for part in range(first, last):
        columns = pl.ds(part * width, width)
        copies.append(pltpu.make_async_copy(source.at[:, columns], target.at[:, columns], sems.at[part]))
    return copies


def load_kernel(head, near_ref, sems):
    copies = head_copies(head, near_ref, sems, 0, AHEAD)
    for copy in copies:
        copy.start()
    for copy in copies:
        copy.wait()


TILE = 1024
WIDE = 1024


def pack_kernel(targets, rows, out_ref, targets_ref, sems):
    own, depth = rows.shape
    ids_copy = pltpu.make_async_copy(targets, targets_ref, sems.at[0])
    rows_copy = pltpu.make_async_copy(rows, out_ref.at[:, pl.ds(0, depth)], sems.at[1])
    ids_copy.start()
    rows_copy.start()
    ids_copy.wait()
    place = lax.broadcasted_iota(jnp.int32, (own, LANES), 0)
    ids = jnp.zeros((own, LANES), jnp.int32)
    for i in range(own):
        ids = jnp.where(place == i, targets_ref[i], ids)
    lane = lax.broadcasted_iota(jnp.int32, (own, LANES), 1)
    digits = jnp.where(lane == 0, ids // 256, ids % 256)
    out_ref[:, depth:] = digits.astype(jnp.float32).astype(jnp.bfloat16)
    rows_copy.wait()


def ids_of(digits):
    digits = digits.astype(jnp.float32)
    return (digits[:, 0:1] * 256.0 + digits[:, 1:2]).astype(jnp.int32)


def swap_blocks(value, group):
    size = value.shape[1]
    lane = lax.broadcasted_iota(jnp.int32, value.shape, 1)
    up, down = pltpu.roll(value, group, 1), pltpu.roll(value, size - group, 1)
    return jnp.where((lane & group) != 0, up, down)


def shared_order(value, members):
    me = my_label()
    step = 1
    while step < members:
        swapped = swap_blocks(value, value.shape[1] // members * step)
        value = jnp.where((me & step) != 0, swapped, value)
        step *= 2
    return value


def as_columns(line):
    return jnp.broadcast_to(line, (LANES, line.shape[1])).T[:, 0:1]


def logits_of(rows_ref, near_ref, logits_ref, first, last):
    depth = near_ref.shape[0]
    while first < last:
        part = pl.ds(first, min(WIDE, last - first))
        logits_ref[:, part] = jnp.dot(
            rows_ref[:, :depth], near_ref[:, part], preferred_element_type=jnp.float32
        )
        first += WIDE


def softmax_of(rows_ref, logits_ref, both_ref, columns_ref, first):
    rows, width = logits_ref.shape
    digits = rows_ref.shape[1] - LANES
    chunk = 32
    offset = lax.axis_index(AXIS) * width

    @pl.loop(0, rows // chunk)
    def _(i):
        part = pl.ds(pl.multiple_of(i * chunk, chunk), chunk)
        logits = logits_ref[part, :]
        ids = ids_of(rows_ref[part, digits:]) - offset
        hit = lax.broadcasted_iota(jnp.int32, logits.shape, 1) == ids
        top = jnp.max(logits, axis=1, keepdims=True)
        raised = jnp.exp(logits - top)
        total = jnp.sum(raised, axis=1, keepdims=True)
        pick = jnp.sum(jnp.where(hit, logits, 0.0), axis=1, keepdims=True)
        both_ref[part, :] = jnp.where(hit, 0.0, raised).astype(jnp.bfloat16)
        other = pl.ds(pl.multiple_of(rows + i * chunk, chunk), chunk)
        both_ref[other, :] = jnp.where(hit, 1.0, 0.0).astype(jnp.bfloat16)
        place = lax.broadcasted_iota(jnp.int32, (chunk, LANES), 1)
        slot = pl.ds(pl.multiple_of(first + i * chunk, chunk), chunk)
        columns_ref[slot, :] = jnp.where(place == 0, top, jnp.where(place == 1, total, pick))


def first_kernel(packed_ref, head, held_ref, near_ref, logits_ref, both_ref, columns_ref, sems):
    width = near_ref.shape[1]
    there = width // PARTS * AHEAD
    copies = head_copies(head, near_ref, sems, AHEAD, PARTS)
    for copy in copies:
        copy.start()
    logits_of(packed_ref, near_ref, logits_ref, 0, there)
    for copy in copies:
        copy.wait()
    logits_of(packed_ref, near_ref, logits_ref, there, width)
    softmax_of(packed_ref, logits_ref, both_ref, columns_ref, 0)


def second_kernel(rows_ref, near_ref, before_ref, logits_ref, both_ref, lines_ref, columns_ref):
    first = before_ref.shape[0]
    logits_of(rows_ref, near_ref, logits_ref, 0, near_ref.shape[1])
    softmax_of(rows_ref, logits_ref, both_ref, columns_ref, first)
    columns_ref[pl.ds(0, first), :] = before_ref[...]
    lines_ref[...] = columns_ref[...].T[:8]


def merge_kernel(steps, members, mine_ref, *refs):
    *other_refs, out_ref = refs
    block = mine_ref.shape[1] // members
    me = my_label()
    groups = [mine_ref[...]]
    for step, other_ref in zip(steps, other_refs):
        other, bit = other_ref[...], 1
        while bit <= step:
            if step & bit:
                other = swap_blocks(other, block * bit)
            bit *= 2
        groups.append(other)
    unit, bit = steps[0], 1
    while bit < len(groups):
        upper = (me & (unit * bit)) != 0
        groups = [jnp.where(upper, groups[i ^ bit], group) for i, group in enumerate(groups)]
        bit *= 2
    top = functools.reduce(jnp.maximum, [group[0:1] for group in groups])
    total = sum(group[1:2] * jnp.exp(group[0:1] - top) for group in groups)
    pick = sum(group[2:3] for group in groups)
    place = lax.broadcasted_iota(jnp.int32, out_ref.shape, 0)
    out_ref[...] = jnp.where(place == 0, top, jnp.where(place == 1, total, pick))


def grad_kernel(first, one_ref, two_ref, near_ref, *refs):
    terms_ref = refs[-1]
    tile = min(terms_ref.shape[1], 2**19 // (one_ref.shape[0] + two_ref.shape[0]))
    both = jnp.concatenate([one_ref[...], two_ref[...]], axis=0)
    for place in range(0, terms_ref.shape[1], tile):
        turned = lax.dot_general(
            near_ref[pl.ds(first + place, tile), :], both, (((1,), (1,)), ((), ())),
            preferred_element_type=jnp.float32,
        )
        terms_ref[:, pl.ds(place, tile)] = turned.T


def join_kernel(scale, first, lines_ref, mine_ref, *refs):
    *terms_refs, out_ref = refs
    rows = mine_ref.shape[1]
    top, total = lines_ref[0:1, :], lines_ref[1:2, :]
    soft = as_columns(jnp.exp(mine_ref[0:1, :] - top) / (total * rows)) * scale
    hard = (jnp.exp(mine_ref[2:3, :] - top) / total - 1.0) / rows
    hard = as_columns(hard.astype(jnp.bfloat16).astype(jnp.float32)) * scale

    count = out_ref.shape[0]
    chunk = min(count, 64)
    for place, terms_ref in enumerate(terms_refs):
        columns = pl.ds(place * terms_ref.shape[1], terms_ref.shape[1])
        for i in range(0, count, chunk):
            part = slice(first + i, first + i + chunk)
            out_ref[pl.ds(i, chunk), columns] = (
                soft[part] * terms_ref[pl.ds(2 * first + i, chunk), :]
                + hard[part] * terms_ref[pl.ds(2 * first + count + i, chunk), :]
            )


def frag_kernel(members, rows_one_ref, rows_two_ref, ids_one_ref, ids_two_ref, lines_ref, one_ref, two_ref, head_ref,
                global_ref, momentum_ref, peer_ref, new_global_ref, new_momentum_ref, loss_ref):
    logits = jnp.concatenate([one_ref[...], two_ref[...]], axis=0)
    held = jnp.concatenate([rows_one_ref[...], rows_two_ref[...]], axis=0)
    ids = jnp.concatenate([ids_of(ids_one_ref[...]), ids_of(ids_two_ref[...])], axis=0)
    rows, tile = logits.shape

    @pl.when(pl.program_id(0) == 0)
    def _():
        lines = shared_order(lines_ref[...], members)
        loss_ref[0] = jnp.sum(lines[0:1] + jnp.log(lines[1:2]) - lines[2:3]) / rows

    top, share = as_columns(lines_ref[0:1, :]), as_columns(1.0 / lines_ref[1:2, :])
    offset = (lax.axis_index(AXIS) * pl.num_programs(0) + pl.program_id(0)) * tile
    hit = lax.broadcasted_iota(jnp.int32, (rows, tile), 1) == ids - offset
    shares = jnp.exp(logits - top) * share
    dlogits = ((shares - jnp.where(hit, 1.0, 0.0)) * (1.0 / rows)).astype(jnp.bfloat16)
    turned = held.astype(jnp.float32).T.astype(jnp.bfloat16)
    frag_grad = jnp.dot(turned, dlogits, preferred_element_type=jnp.float32)
    local_frag = head_ref[...].astype(jnp.float32) - 1.0 * frag_grad
    pseudo = (global_ref[...] - local_frag + peer_ref[...]) / REPLICAS
    new_momentum = 0.9 * momentum_ref[...] + pseudo
    new_momentum_ref[...] = new_momentum
    new_global_ref[...] = global_ref[...] - 0.7 * (pseudo + 0.9 * new_momentum)


def frag_update(members, held, ids, lines, logits, near, global_frag, momentum, peer_delta):
    rows = lines.shape[1]
    width = near.shape[1]
    tile = pl.BlockSpec((FRAG, TILE), lambda i: (0, i))

    return pl.pallas_call(
        functools.partial(frag_kernel, members),
        grid=(width // TILE,),
        out_shape=[jax.ShapeDtypeStruct((FRAG, width), jnp.float32)] * 2
        + [jax.ShapeDtypeStruct((1,), jnp.float32)],
        in_specs=[pl.BlockSpec((x.shape[0], FRAG), lambda i: (0, 0)) for x in held]
        + [
            pl.BlockSpec((x.shape[0], LANES), lambda i, last=x.shape[1] // LANES - 1: (0, last))
            for x in ids
        ]
        + [pl.BlockSpec((8, rows), lambda i: (0, 0))]
        + [pl.BlockSpec((x.shape[0], TILE), lambda i: (0, i)) for x in logits]
        + [tile] * 4,
        out_specs=[tile, tile, pl.BlockSpec(memory_space=pltpu.SMEM)],
        compiler_params=pltpu.CompilerParams(vmem_limit_bytes=16 * 2**20),
        cost_estimate=pl.CostEstimate(
            flops=2 * rows * FRAG * width, bytes_accessed=24 * FRAG * width, transcendentals=0
        ),
    )(
        *held, *ids, lines, *[pltpu.with_memory_space_constraint(x, pltpu.VMEM) for x in logits],
        pltpu.with_memory_space_constraint(near, pltpu.VMEM), global_frag, momentum, peer_delta,
    )


def turned(label):
    return label // 4 * 4 + label % 2 * 2 + label // 2 % 2


def my_label():
    me = lax.axis_index(AXIS)
    return jnp.where(lax.rem(lax.axis_index("outer"), 2) == 1, turned(me), me)


def swap(value, step):
    members = lax.axis_size(AXIS)
    pairs = []
    for outer in range(lax.axis_size("outer")):
        flip = turned(step) if outer % 2 else step
        pairs += [(outer * members + i, outer * members + (i ^ flip)) for i in range(members)]
    return lax.ppermute(value, ("outer", AXIS), pairs)


def far_steps():
    step = 4
    steps = []
    while step < lax.axis_size(AXIS):
        steps.append(step)
        step *= 2
    return steps


def gather_rows(packed):
    own = packed.shape[0]
    held = packed
    for step in far_steps():
        held = jnp.concatenate([held, swap(held, step)], axis=0)
    far = held[own:]
    near = jnp.concatenate([packed] + [swap(packed, step) for step in (1, 2, 3)], axis=0)
    far = jnp.stack([far] + [swap(far, step) for step in (1, 2, 3)])
    count = far.shape[1] // own
    return near, far.reshape(4, count, own, -1).swapaxes(0, 1).reshape(4 * count * own, -1)


def scatter_sums(grads_near, grads_far, own):
    blocks = [
        grads[i * own : (i + 1) * own]
        for grads in (grads_near, grads_far)
        for i in range(grads.shape[0] // own)
    ]
    members = len(blocks)

    def moved(parts, step):
        value = jnp.concatenate([part.astype(SEND) for part in parts], axis=0)
        value = swap(value, step).astype(jnp.float32)
        return [value[i * own : (i + 1) * own] for i in range(len(parts))]

    far = range(4, members, 4)
    three = moved([blocks[i ^ 3] for i in far], 3)
    two = moved([blocks[i ^ 2] for i in far], 2)
    one = moved([blocks[i ^ 1] for i in far], 1)
    relayed = moved([blocks[3]], 1)[0]
    y_near = moved([blocks[1]], 1)[0]
    z_near = moved([blocks[2] + relayed], 2)[0]
    sums = [blocks[0] + z_near + y_near]
    sums += [blocks[i] + a + b + c for i, a, b, c in zip(far, three, one, two)]
    for step in far_steps()[::-1]:
        keep = len(sums) // 2
        sums = [a + b for a, b in zip(sums[:keep], moved(sums[keep:], step))]
    return sums[0]


def body(hidden, targets, head, global_frag, momentum, peer_delta):
    members = lax.axis_size(AXIS)
    own, depth = hidden.shape
    rows = own * members
    width = head.shape[1]

    packed = call(
        pack_kernel, [((own, depth + LANES), hidden.dtype)], [targets, hidden],
        scratch=[pltpu.SMEM(targets.shape, targets.dtype), pltpu.SemaphoreType.DMA((2,))],
        sources=[pltpu.HBM, pltpu.HBM],
    )[0]
    rows_near, rows_far = gather_rows(packed)
    near = call(
        load_kernel, [(head.shape, head.dtype)], [head],
        scratch=[pltpu.SemaphoreType.DMA((PARTS,))], sources=[pltpu.HBM],
    )[0]

    count = 4 * own
    near, logits_near, both_near, columns = call(
        first_kernel,
        [(head.shape, head.dtype), ((count, width), jnp.float32), ((2 * count, width), jnp.bfloat16),
         ((count, LANES), jnp.float32)],
        [rows_near, head, near], 2 * count * depth * width,
        scratch=[pltpu.SemaphoreType.DMA((PARTS,))],
        sources=[pltpu.VMEM, pltpu.HBM, pltpu.VMEM], aliases={2: 0},
    )
    count = rows - 4 * own
    logits_far, both_far, mine = call(
        second_kernel,
        [((count, width), jnp.float32), ((2 * count, width), jnp.bfloat16), ((8, rows), jnp.float32)],
        [rows_far, near, columns], 2 * count * depth * width,
        scratch=[pltpu.VMEM((rows, LANES), jnp.float32)],
    )

    lines = mine
    for steps in [[step] for step in far_steps()] + [[1, 2, 3]]:
        before = lines
        lines = call(
            functools.partial(merge_kernel, steps, members),
            [((8, rows), jnp.float32)], [lines] + [swap(lines, step) for step in steps],
        )[0]

    terms = [
        call(
            functools.partial(grad_kernel, first),
            [((2 * rows, depth // 2), jnp.float32)], [both_near, both_far, near, *after],
            2 * rows * depth * width,
        )[0]
        for first, after in ((0, []), (depth // 2, [before]))
    ]

    scale = 2.0**14 * rows
    grads_far, grads_near = (
        call(
            functools.partial(join_kernel, scale, first),
            [((count, depth), jnp.float32)], [lines, mine] + terms,
        )[0]
        for first, count in ((4 * own, rows - 4 * own), (0, 4 * own))
    )
    hidden_grad = (scatter_sums(grads_near, grads_far, own) * (1.0 / scale)).astype(jnp.bfloat16)
    new_global, new_momentum, loss = frag_update(
        members, [rows_near, rows_far], [rows_near, rows_far], lines, [logits_near, logits_far], near,
        global_frag, momentum, peer_delta,
    )
    return (loss, hidden_grad, new_global, new_momentum)


def solution(mesh):
    in_specs = (
        P(("outer", "vocab"), None),
        P(("outer", "vocab")),
        P("outer", "vocab"),
        P(None, "vocab"),
        P(None, "vocab"),
        P("outer", "vocab"),
    )
    out_specs = (P("outer"), P(("outer", "vocab"), None), P("outer", "vocab"), P("outer", "vocab"))
    return jax.shard_map(body, mesh=mesh, in_specs=in_specs, out_specs=out_specs, check_vma=False)
```

```python
import functools

import jax
import jax.numpy as jnp
from jax import lax
from jax.experimental import pallas as pl
from jax.experimental.pallas import tpu as pltpu
from jax.sharding import PartitionSpec as P

FRAG = 128
REPLICAS = 4
AXIS = "vocab"
SEND = jnp.float16
LANES = 128
VMEM = pl.BlockSpec(memory_space=pltpu.VMEM)


def call(kernel, outs, operands, flops=0, scratch=(), sources=None, vmem=16 * 2**20, aliases={}):
    outs = [pltpu.VMEM(shape, dtype) for shape, dtype in outs]
    places = sources or [pltpu.VMEM] * len(operands)
    moved = sum(x.size * x.dtype.itemsize for x in operands)
    return pl.pallas_call(
        kernel,
        out_shape=outs,
        in_specs=[pl.BlockSpec(memory_space=place) for place in places],
        out_specs=[VMEM] * len(outs),
        scratch_shapes=list(scratch),
        input_output_aliases=aliases,
        compiler_params=pltpu.CompilerParams(vmem_limit_bytes=vmem),
        cost_estimate=pl.CostEstimate(flops=flops, bytes_accessed=moved, transcendentals=0),
    )(*[pltpu.with_memory_space_constraint(x, place) for x, place in zip(operands, places)])


PARTS = 8
AHEAD = 5


def head_copies(source, target, sems, first, last):
    width = source.shape[1] // PARTS
    copies = []
    for part in range(first, last):
        columns = pl.ds(part * width, width)
        copies.append(pltpu.make_async_copy(source.at[:, columns], target.at[:, columns], sems.at[part]))
    return copies


def load_kernel(head, near_ref, sems):
    copies = head_copies(head, near_ref, sems, 0, AHEAD)
    for copy in copies:
        copy.start()
    for copy in copies:
        copy.wait()


TILE = 1024
WIDE = 1024


def pack_kernel(targets, rows, out_ref, targets_ref, sems):
    own, depth = rows.shape
    ids_copy = pltpu.make_async_copy(targets, targets_ref, sems.at[0])
    rows_copy = pltpu.make_async_copy(rows, out_ref.at[:, pl.ds(0, depth)], sems.at[1])
    ids_copy.start()
    rows_copy.start()
    ids_copy.wait()
    place = lax.broadcasted_iota(jnp.int32, (own, LANES), 0)
    ids = jnp.zeros((own, LANES), jnp.int32)
    for i in range(own):
        ids = jnp.where(place == i, targets_ref[i], ids)
    lane = lax.broadcasted_iota(jnp.int32, (own, LANES), 1)
    digits = jnp.where(lane == 0, ids // 256, ids % 256)
    out_ref[:, depth:] = digits.astype(jnp.float32).astype(jnp.bfloat16)
    rows_copy.wait()


def ids_of(digits):
    digits = digits.astype(jnp.float32)
    return (digits[:, 0:1] * 256.0 + digits[:, 1:2]).astype(jnp.int32)


def swap_blocks(value, group):
    size = value.shape[1]
    lane = lax.broadcasted_iota(jnp.int32, value.shape, 1)
    up, down = pltpu.roll(value, group, 1), pltpu.roll(value, size - group, 1)
    return jnp.where((lane & group) != 0, up, down)


def shared_order(value, members):
    me = lax.axis_index(AXIS)
    step = 1
    while step < members:
        swapped = swap_blocks(value, value.shape[1] // members * step)
        value = jnp.where((me & step) != 0, swapped, value)
        step *= 2
    return value


def as_columns(line):
    return jnp.broadcast_to(line, (LANES, line.shape[1])).T[:, 0:1]


def logits_of(rows_ref, near_ref, logits_ref, first, last):
    depth = near_ref.shape[0]
    while first < last:
        part = pl.ds(first, min(WIDE, last - first))
        logits_ref[:, part] = jnp.dot(
            rows_ref[:, :depth], near_ref[:, part], preferred_element_type=jnp.float32
        )
        first += WIDE


def softmax_of(rows_ref, logits_ref, both_ref, columns_ref, first):
    rows, width = logits_ref.shape
    digits = rows_ref.shape[1] - LANES
    chunk = 32
    offset = lax.axis_index(AXIS) * width

    @pl.loop(0, rows // chunk)
    def _(i):
        part = pl.ds(pl.multiple_of(i * chunk, chunk), chunk)
        logits = logits_ref[part, :]
        ids = ids_of(rows_ref[part, digits:]) - offset
        hit = lax.broadcasted_iota(jnp.int32, logits.shape, 1) == ids
        top = jnp.max(logits, axis=1, keepdims=True)
        raised = jnp.exp(logits - top)
        total = jnp.sum(raised, axis=1, keepdims=True)
        pick = jnp.sum(jnp.where(hit, logits, 0.0), axis=1, keepdims=True)
        both_ref[part, :] = jnp.where(hit, 0.0, raised).astype(jnp.bfloat16)
        other = pl.ds(pl.multiple_of(rows + i * chunk, chunk), chunk)
        both_ref[other, :] = jnp.where(hit, 1.0, 0.0).astype(jnp.bfloat16)
        place = lax.broadcasted_iota(jnp.int32, (chunk, LANES), 1)
        slot = pl.ds(pl.multiple_of(first + i * chunk, chunk), chunk)
        columns_ref[slot, :] = jnp.where(place == 0, top, jnp.where(place == 1, total, pick))


def first_kernel(packed_ref, head, held_ref, near_ref, logits_ref, both_ref, columns_ref, sems):
    width = near_ref.shape[1]
    there = width // PARTS * AHEAD
    copies = head_copies(head, near_ref, sems, AHEAD, PARTS)
    for copy in copies:
        copy.start()
    logits_of(packed_ref, near_ref, logits_ref, 0, there)
    for copy in copies:
        copy.wait()
    logits_of(packed_ref, near_ref, logits_ref, there, width)
    softmax_of(packed_ref, logits_ref, both_ref, columns_ref, 0)


def second_kernel(rows_ref, near_ref, before_ref, logits_ref, both_ref, lines_ref, columns_ref):
    first = before_ref.shape[0]
    logits_of(rows_ref, near_ref, logits_ref, 0, near_ref.shape[1])
    softmax_of(rows_ref, logits_ref, both_ref, columns_ref, first)
    columns_ref[pl.ds(0, first), :] = before_ref[...]
    lines_ref[...] = columns_ref[...].T[:8]


def merge_kernel(steps, members, mine_ref, *refs):
    *other_refs, out_ref = refs
    block = mine_ref.shape[1] // members
    me = lax.axis_index(AXIS)
    groups = [mine_ref[...]]
    for step, other_ref in zip(steps, other_refs):
        other, bit = other_ref[...], 1
        while bit <= step:
            if step & bit:
                other = swap_blocks(other, block * bit)
            bit *= 2
        groups.append(other)
    unit, bit = steps[0], 1
    while bit < len(groups):
        upper = (me & (unit * bit)) != 0
        groups = [jnp.where(upper, groups[i ^ bit], group) for i, group in enumerate(groups)]
        bit *= 2
    top = functools.reduce(jnp.maximum, [group[0:1] for group in groups])
    total = sum(group[1:2] * jnp.exp(group[0:1] - top) for group in groups)
    pick = sum(group[2:3] for group in groups)
    place = lax.broadcasted_iota(jnp.int32, out_ref.shape, 0)
    out_ref[...] = jnp.where(place == 0, top, jnp.where(place == 1, total, pick))


def grad_kernel(first, one_ref, two_ref, near_ref, *refs):
    terms_ref = refs[-1]
    tile = min(terms_ref.shape[1], 2**19 // (one_ref.shape[0] + two_ref.shape[0]))
    both = jnp.concatenate([one_ref[...], two_ref[...]], axis=0)
    for place in range(0, terms_ref.shape[1], tile):
        turned = lax.dot_general(
            near_ref[pl.ds(first + place, tile), :], both, (((1,), (1,)), ((), ())),
            preferred_element_type=jnp.float32,
        )
        terms_ref[:, pl.ds(place, tile)] = turned.T


def join_kernel(scale, first, lines_ref, mine_ref, *refs):
    *terms_refs, out_ref = refs
    rows = mine_ref.shape[1]
    top, total = lines_ref[0:1, :], lines_ref[1:2, :]
    soft = as_columns(jnp.exp(mine_ref[0:1, :] - top) / (total * rows)) * scale
    hard = (jnp.exp(mine_ref[2:3, :] - top) / total - 1.0) / rows
    hard = as_columns(hard.astype(jnp.bfloat16).astype(jnp.float32)) * scale

    count = out_ref.shape[0]
    chunk = min(count, 64)
    for place, terms_ref in enumerate(terms_refs):
        columns = pl.ds(place * terms_ref.shape[1], terms_ref.shape[1])
        for i in range(0, count, chunk):
            part = slice(first + i, first + i + chunk)
            out_ref[pl.ds(i, chunk), columns] = (
                soft[part] * terms_ref[pl.ds(2 * first + i, chunk), :]
                + hard[part] * terms_ref[pl.ds(2 * first + count + i, chunk), :]
            )


def frag_kernel(members, rows_one_ref, rows_two_ref, ids_one_ref, ids_two_ref, lines_ref, one_ref, two_ref, head_ref,
                global_ref, momentum_ref, peer_ref, new_global_ref, new_momentum_ref, loss_ref):
    logits = jnp.concatenate([one_ref[...], two_ref[...]], axis=0)
    held = jnp.concatenate([rows_one_ref[...], rows_two_ref[...]], axis=0)
    ids = jnp.concatenate([ids_of(ids_one_ref[...]), ids_of(ids_two_ref[...])], axis=0)
    rows, tile = logits.shape

    @pl.when(pl.program_id(0) == 0)
    def _():
        lines = shared_order(lines_ref[...], members)
        loss_ref[0] = jnp.sum(lines[0:1] + jnp.log(lines[1:2]) - lines[2:3]) / rows

    top, share = as_columns(lines_ref[0:1, :]), as_columns(1.0 / lines_ref[1:2, :])
    offset = (lax.axis_index(AXIS) * pl.num_programs(0) + pl.program_id(0)) * tile
    hit = lax.broadcasted_iota(jnp.int32, (rows, tile), 1) == ids - offset
    shares = jnp.exp(logits - top) * share
    dlogits = ((shares - jnp.where(hit, 1.0, 0.0)) * (1.0 / rows)).astype(jnp.bfloat16)
    turned = held.astype(jnp.float32).T.astype(jnp.bfloat16)
    frag_grad = jnp.dot(turned, dlogits, preferred_element_type=jnp.float32)
    local_frag = head_ref[...].astype(jnp.float32) - 1.0 * frag_grad
    pseudo = (global_ref[...] - local_frag + peer_ref[...]) / REPLICAS
    new_momentum = 0.9 * momentum_ref[...] + pseudo
    new_momentum_ref[...] = new_momentum
    new_global_ref[...] = global_ref[...] - 0.7 * (pseudo + 0.9 * new_momentum)


def frag_update(members, held, ids, lines, logits, near, global_frag, momentum, peer_delta):
    rows = lines.shape[1]
    width = near.shape[1]
    tile = pl.BlockSpec((FRAG, TILE), lambda i: (0, i))

    return pl.pallas_call(
        functools.partial(frag_kernel, members),
        grid=(width // TILE,),
        out_shape=[jax.ShapeDtypeStruct((FRAG, width), jnp.float32)] * 2
        + [jax.ShapeDtypeStruct((1,), jnp.float32)],
        in_specs=[pl.BlockSpec((x.shape[0], FRAG), lambda i: (0, 0)) for x in held]
        + [
            pl.BlockSpec((x.shape[0], LANES), lambda i, last=x.shape[1] // LANES - 1: (0, last))
            for x in ids
        ]
        + [pl.BlockSpec((8, rows), lambda i: (0, 0))]
        + [pl.BlockSpec((x.shape[0], TILE), lambda i: (0, i)) for x in logits]
        + [tile] * 4,
        out_specs=[tile, tile, pl.BlockSpec(memory_space=pltpu.SMEM)],
        compiler_params=pltpu.CompilerParams(vmem_limit_bytes=16 * 2**20),
        cost_estimate=pl.CostEstimate(
            flops=2 * rows * FRAG * width, bytes_accessed=24 * FRAG * width, transcendentals=0
        ),
    )(
        *held, *ids, lines, *[pltpu.with_memory_space_constraint(x, pltpu.VMEM) for x in logits],
        pltpu.with_memory_space_constraint(near, pltpu.VMEM), global_frag, momentum, peer_delta,
    )


def swap(value, step):
    return lax.ppermute(value, AXIS, [(i, i ^ step) for i in range(lax.axis_size(AXIS))])


def far_steps():
    step = 4
    steps = []
    while step < lax.axis_size(AXIS):
        steps.append(step)
        step *= 2
    return steps


def gather_rows(packed):
    own = packed.shape[0]
    held = packed
    for step in far_steps():
        held = jnp.concatenate([held, swap(held, step)], axis=0)
    far = held[own:]
    near = jnp.concatenate([packed] + [swap(packed, step) for step in (1, 2, 3)], axis=0)
    far = jnp.stack([far] + [swap(far, step) for step in (1, 2, 3)])
    count = far.shape[1] // own
    return near, far.reshape(4, count, own, -1).swapaxes(0, 1).reshape(4 * count * own, -1)


def scatter_sums(grads_near, grads_far, own):
    blocks = [
        grads[i * own : (i + 1) * own]
        for grads in (grads_near, grads_far)
        for i in range(grads.shape[0] // own)
    ]
    members = len(blocks)

    def moved(parts, step):
        value = jnp.concatenate([part.astype(SEND) for part in parts], axis=0)
        value = swap(value, step).astype(jnp.float32)
        return [value[i * own : (i + 1) * own] for i in range(len(parts))]

    far = range(4, members, 4)
    three = moved([blocks[i ^ 3] for i in far], 3)
    two = moved([blocks[i ^ 2] for i in far], 2)
    one = moved([blocks[i ^ 1] for i in far], 1)
    relayed = moved([blocks[3]], 1)[0]
    y_near = moved([blocks[1]], 1)[0]
    z_near = moved([blocks[2] + relayed], 2)[0]
    sums = [blocks[0] + z_near + y_near]
    sums += [blocks[i] + a + b + c for i, a, b, c in zip(far, three, two, one)]
    for step in far_steps()[::-1]:
        keep = len(sums) // 2
        sums = [a + b for a, b in zip(sums[:keep], moved(sums[keep:], step))]
    return sums[0]


def body(hidden, targets, head, global_frag, momentum, peer_delta):
    members = lax.axis_size(AXIS)
    own, depth = hidden.shape
    rows = own * members
    width = head.shape[1]

    packed = call(
        pack_kernel, [((own, depth + LANES), hidden.dtype)], [targets, hidden],
        scratch=[pltpu.SMEM(targets.shape, targets.dtype), pltpu.SemaphoreType.DMA((2,))],
        sources=[pltpu.HBM, pltpu.HBM],
    )[0]
    rows_near, rows_far = gather_rows(packed)
    near = call(
        load_kernel, [(head.shape, head.dtype)], [head],
        scratch=[pltpu.SemaphoreType.DMA((PARTS,))], sources=[pltpu.HBM],
    )[0]

    count = 4 * own
    near, logits_near, both_near, columns = call(
        first_kernel,
        [(head.shape, head.dtype), ((count, width), jnp.float32), ((2 * count, width), jnp.bfloat16),
         ((count, LANES), jnp.float32)],
        [rows_near, head, near], 2 * count * depth * width,
        scratch=[pltpu.SemaphoreType.DMA((PARTS,))],
        sources=[pltpu.VMEM, pltpu.HBM, pltpu.VMEM], aliases={2: 0},
    )
    count = rows - 4 * own
    logits_far, both_far, mine = call(
        second_kernel,
        [((count, width), jnp.float32), ((2 * count, width), jnp.bfloat16), ((8, rows), jnp.float32)],
        [rows_far, near, columns], 2 * count * depth * width,
        scratch=[pltpu.VMEM((rows, LANES), jnp.float32)],
    )

    lines = mine
    for steps in [[step] for step in far_steps()] + [[1, 2, 3]]:
        before = lines
        lines = call(
            functools.partial(merge_kernel, steps, members),
            [((8, rows), jnp.float32)], [lines] + [swap(lines, step) for step in steps],
        )[0]

    terms = [
        call(
            functools.partial(grad_kernel, first),
            [((2 * rows, depth // 2), jnp.float32)], [both_near, both_far, near, *after],
            2 * rows * depth * width,
        )[0]
        for first, after in ((0, []), (depth // 2, [before]))
    ]

    scale = 2.0**14 * rows
    grads_far, grads_near = (
        call(
            functools.partial(join_kernel, scale, first),
            [((count, depth), jnp.float32)], [lines, mine] + terms,
        )[0]
        for first, count in ((4 * own, rows - 4 * own), (0, 4 * own))
    )
    hidden_grad = (scatter_sums(grads_near, grads_far, own) * (1.0 / scale)).astype(jnp.bfloat16)
    new_global, new_momentum, loss = frag_update(
        members, [rows_near, rows_far], [rows_near, rows_far], lines, [logits_near, logits_far], near,
        global_frag, momentum, peer_delta,
    )
    return (loss, hidden_grad, new_global, new_momentum)


def solution(mesh):
    in_specs = (
        P(("outer", "vocab"), None),
        P(("outer", "vocab")),
        P("outer", "vocab"),
        P(None, "vocab"),
        P(None, "vocab"),
        P("outer", "vocab"),
    )
    out_specs = (P("outer"), P(("outer", "vocab"), None), P("outer", "vocab"), P("outer", "vocab"))
    return jax.shard_map(body, mesh=mesh, in_specs=in_specs, out_specs=out_specs, check_vma=False)
```

```python
import functools

import jax
import jax.numpy as jnp
from jax import lax
from jax.experimental import pallas as pl
from jax.experimental.pallas import tpu as pltpu
from jax.sharding import PartitionSpec as P

FRAG = 128
REPLICAS = 4
AXIS = "vocab"
SEND = jnp.float16
LANES = 128
VMEM = pl.BlockSpec(memory_space=pltpu.VMEM)


def call(kernel, outs, operands, flops=0, scratch=(), sources=None, vmem=16 * 2**20, aliases={}):
    outs = [pltpu.VMEM(shape, dtype) for shape, dtype in outs]
    places = sources or [pltpu.VMEM] * len(operands)
    moved = sum(x.size * x.dtype.itemsize for x in operands)
    return pl.pallas_call(
        kernel,
        out_shape=outs,
        in_specs=[pl.BlockSpec(memory_space=place) for place in places],
        out_specs=[VMEM] * len(outs),
        scratch_shapes=list(scratch),
        input_output_aliases=aliases,
        compiler_params=pltpu.CompilerParams(vmem_limit_bytes=vmem),
        cost_estimate=pl.CostEstimate(flops=flops, bytes_accessed=moved, transcendentals=0),
    )(*[pltpu.with_memory_space_constraint(x, place) for x, place in zip(operands, places)])


PARTS = 8
AHEAD = 6


def head_copies(source, target, sems, first, last):
    width = source.shape[1] // PARTS
    copies = []
    for part in range(first, last):
        columns = pl.ds(part * width, width)
        copies.append(pltpu.make_async_copy(source.at[:, columns], target.at[:, columns], sems.at[part]))
    return copies


def load_kernel(head, near_ref, sems):
    copies = head_copies(head, near_ref, sems, 0, AHEAD)
    for copy in copies:
        copy.start()
    for copy in copies:
        copy.wait()


TILE = 1024
WIDE = 2048


def pack_kernel(targets, rows, out_ref, targets_ref, sems):
    own, depth = rows.shape
    ids_copy = pltpu.make_async_copy(targets, targets_ref, sems.at[0])
    rows_copy = pltpu.make_async_copy(rows, out_ref.at[:, pl.ds(0, depth)], sems.at[1])
    ids_copy.start()
    rows_copy.start()
    ids_copy.wait()
    place = lax.broadcasted_iota(jnp.int32, (own, LANES), 0)
    ids = jnp.zeros((own, LANES), jnp.int32)
    for i in range(own):
        ids = jnp.where(place == i, targets_ref[i], ids)
    lane = lax.broadcasted_iota(jnp.int32, (own, LANES), 1)
    digits = jnp.where(lane == 0, ids // 256, ids % 256)
    out_ref[:, depth:] = digits.astype(jnp.float32).astype(jnp.bfloat16)
    rows_copy.wait()


def ids_of(digits):
    digits = digits.astype(jnp.float32)
    return (digits[:, 0:1] * 256.0 + digits[:, 1:2]).astype(jnp.int32)


def swap_blocks(value, group):
    size = value.shape[1]
    lane = lax.broadcasted_iota(jnp.int32, value.shape, 1)
    up, down = pltpu.roll(value, group, 1), pltpu.roll(value, size - group, 1)
    return jnp.where((lane & group) != 0, up, down)


def shared_order(value, members):
    me = lax.axis_index(AXIS)
    step = 1
    while step < members:
        swapped = swap_blocks(value, value.shape[1] // members * step)
        value = jnp.where((me & step) != 0, swapped, value)
        step *= 2
    return value


def as_columns(line):
    return jnp.broadcast_to(line, (LANES, line.shape[1])).T[:, 0:1]


def logits_of(rows_ref, near_ref, logits_ref, first, last):
    depth = near_ref.shape[0]
    while first < last:
        part = pl.ds(first, min(WIDE, last - first))
        logits_ref[:, part] = jnp.dot(
            rows_ref[:, :depth], near_ref[:, part], preferred_element_type=jnp.float32
        )
        first += WIDE


def softmax_of(rows_ref, logits_ref, both_ref, columns_ref, first):
    rows, width = logits_ref.shape
    digits = rows_ref.shape[1] - LANES
    chunk = 32
    offset = lax.axis_index(AXIS) * width

    @pl.loop(0, rows // chunk)
    def _(i):
        part = pl.ds(pl.multiple_of(i * chunk, chunk), chunk)
        logits = logits_ref[part, :]
        ids = ids_of(rows_ref[part, digits:]) - offset
        hit = lax.broadcasted_iota(jnp.int32, logits.shape, 1) == ids
        top = jnp.max(logits, axis=1, keepdims=True)
        raised = jnp.exp(logits - top)
        total = jnp.sum(raised, axis=1, keepdims=True)
        pick = jnp.sum(jnp.where(hit, logits, 0.0), axis=1, keepdims=True)
        both_ref[part, :] = jnp.where(hit, 0.0, raised).astype(jnp.bfloat16)
        other = pl.ds(pl.multiple_of(rows + i * chunk, chunk), chunk)
        both_ref[other, :] = jnp.where(hit, 1.0, 0.0).astype(jnp.bfloat16)
        place = lax.broadcasted_iota(jnp.int32, (chunk, LANES), 1)
        slot = pl.ds(pl.multiple_of(first + i * chunk, chunk), chunk)
        columns_ref[slot, :] = jnp.where(place == 0, top, jnp.where(place == 1, total, pick))


def first_kernel(packed_ref, head, held_ref, near_ref, logits_ref, both_ref, columns_ref, sems):
    width = near_ref.shape[1]
    there = width // PARTS * AHEAD
    copies = head_copies(head, near_ref, sems, AHEAD, PARTS)
    for copy in copies:
        copy.start()
    logits_of(packed_ref, near_ref, logits_ref, 0, there)
    for copy in copies:
        copy.wait()
    logits_of(packed_ref, near_ref, logits_ref, there, width)
    softmax_of(packed_ref, logits_ref, both_ref, columns_ref, 0)


def second_kernel(rows_ref, near_ref, before_ref, logits_ref, both_ref, lines_ref, columns_ref):
    first = before_ref.shape[0]
    logits_of(rows_ref, near_ref, logits_ref, 0, near_ref.shape[1])
    softmax_of(rows_ref, logits_ref, both_ref, columns_ref, first)
    columns_ref[pl.ds(0, first), :] = before_ref[...]
    lines_ref[...] = columns_ref[...].T[:8]


def merge_kernel(steps, members, mine_ref, *refs):
    *other_refs, out_ref = refs
    block = mine_ref.shape[1] // members
    me = lax.axis_index(AXIS)
    groups = [mine_ref[...]]
    for step, other_ref in zip(steps, other_refs):
        other, bit = other_ref[...], 1
        while bit <= step:
            if step & bit:
                other = swap_blocks(other, block * bit)
            bit *= 2
        groups.append(other)
    unit, bit = steps[0], 1
    while bit < len(groups):
        upper = (me & (unit * bit)) != 0
        groups = [jnp.where(upper, groups[i ^ bit], group) for i, group in enumerate(groups)]
        bit *= 2
    top = functools.reduce(jnp.maximum, [group[0:1] for group in groups])
    total = sum(group[1:2] * jnp.exp(group[0:1] - top) for group in groups)
    pick = sum(group[2:3] for group in groups)
    place = lax.broadcasted_iota(jnp.int32, out_ref.shape, 0)
    out_ref[...] = jnp.where(place == 0, top, jnp.where(place == 1, total, pick))


def grad_kernel(first, one_ref, two_ref, near_ref, *refs):
    terms_ref = refs[-1]
    one, two = one_ref.shape[0] // 2, two_ref.shape[0] // 2
    both = jnp.concatenate([one_ref[:one], two_ref[:two], one_ref[one:], two_ref[two:]], axis=0)
    tile = min(terms_ref.shape[0], 2**19 // both.shape[0])
    for place in range(0, terms_ref.shape[0], tile):
        terms_ref[pl.ds(place, tile), :] = lax.dot_general(
            near_ref[pl.ds(first + place, tile), :], both, (((1,), (1,)), ((), ())),
            preferred_element_type=jnp.float32,
        )


def join_kernel(scale, lines_ref, mine_ref, *refs):
    *terms_refs, far_ref, near_ref = refs
    rows = mine_ref.shape[1]
    near = near_ref.shape[0]
    top, total = lines_ref[0:1, :], lines_ref[1:2, :]
    soft = jnp.exp(mine_ref[0:1, :] - top) / (total * rows) * scale
    hard = (jnp.exp(mine_ref[2:3, :] - top) / total - 1.0) / rows
    hard = hard.astype(jnp.bfloat16).astype(jnp.float32) * scale
    tile = 512
    for place, terms_ref in enumerate(terms_refs):
        for first in range(0, terms_ref.shape[0], tile):
            part = pl.ds(first, tile)
            value = (soft * terms_ref[part, :rows] + hard * terms_ref[part, rows:]).T
            columns = pl.ds(place * terms_ref.shape[0] + first, tile)
            near_ref[:, columns] = value[:near]
            far_ref[:, columns] = value[near:]


def frag_kernel(members, rows_one_ref, rows_two_ref, ids_one_ref, ids_two_ref, lines_ref, one_ref, two_ref, head_ref,
                global_ref, momentum_ref, peer_ref, new_global_ref, new_momentum_ref, loss_ref):
    logits = jnp.concatenate([one_ref[...], two_ref[...]], axis=0)
    held = jnp.concatenate([rows_one_ref[...], rows_two_ref[...]], axis=0)
    ids = jnp.concatenate([ids_of(ids_one_ref[...]), ids_of(ids_two_ref[...])], axis=0)
    rows, tile = logits.shape

    @pl.when(pl.program_id(0) == 0)
    def _():
        lines = shared_order(lines_ref[...], members)
        loss_ref[0] = jnp.sum(lines[0:1] + jnp.log(lines[1:2]) - lines[2:3]) / rows

    top, share = as_columns(lines_ref[0:1, :]), as_columns(1.0 / lines_ref[1:2, :])
    offset = (lax.axis_index(AXIS) * pl.num_programs(0) + pl.program_id(0)) * tile
    hit = lax.broadcasted_iota(jnp.int32, (rows, tile), 1) == ids - offset
    shares = jnp.exp(logits - top) * share
    dlogits = ((shares - jnp.where(hit, 1.0, 0.0)) * (1.0 / rows)).astype(jnp.bfloat16)
    turned = held.astype(jnp.float32).T.astype(jnp.bfloat16)
    frag_grad = jnp.dot(turned, dlogits, preferred_element_type=jnp.float32)
    local_frag = head_ref[...].astype(jnp.float32) - 1.0 * frag_grad
    pseudo = (global_ref[...] - local_frag + peer_ref[...]) / REPLICAS
    new_momentum = 0.9 * momentum_ref[...] + pseudo
    new_momentum_ref[...] = new_momentum
    new_global_ref[...] = global_ref[...] - 0.7 * (pseudo + 0.9 * new_momentum)


def frag_update(members, held, ids, lines, logits, near, global_frag, momentum, peer_delta):
    rows = lines.shape[1]
    width = near.shape[1]
    tile = pl.BlockSpec((FRAG, TILE), lambda i: (0, i))

    return pl.pallas_call(
        functools.partial(frag_kernel, members),
        grid=(width // TILE,),
        out_shape=[jax.ShapeDtypeStruct((FRAG, width), jnp.float32)] * 2
        + [jax.ShapeDtypeStruct((1,), jnp.float32)],
        in_specs=[pl.BlockSpec((x.shape[0], FRAG), lambda i: (0, 0)) for x in held]
        + [
            pl.BlockSpec((x.shape[0], LANES), lambda i, last=x.shape[1] // LANES - 1: (0, last))
            for x in ids
        ]
        + [pl.BlockSpec((8, rows), lambda i: (0, 0))]
        + [pl.BlockSpec((x.shape[0], TILE), lambda i: (0, i)) for x in logits]
        + [tile] * 4,
        out_specs=[tile, tile, pl.BlockSpec(memory_space=pltpu.SMEM)],
        compiler_params=pltpu.CompilerParams(vmem_limit_bytes=16 * 2**20),
        cost_estimate=pl.CostEstimate(
            flops=2 * rows * FRAG * width, bytes_accessed=24 * FRAG * width, transcendentals=0
        ),
    )(
        *held, *ids, lines, *[pltpu.with_memory_space_constraint(x, pltpu.VMEM) for x in logits],
        pltpu.with_memory_space_constraint(near, pltpu.VMEM), global_frag, momentum, peer_delta,
    )


def swap(value, step):
    return lax.ppermute(value, AXIS, [(i, i ^ step) for i in range(lax.axis_size(AXIS))])


def far_steps():
    step = 4
    steps = []
    while step < lax.axis_size(AXIS):
        steps.append(step)
        step *= 2
    return steps


def gather_rows(packed):
    own = packed.shape[0]
    held = packed
    for step in far_steps():
        held = jnp.concatenate([held, swap(held, step)], axis=0)
    far = held[own:]
    near = jnp.concatenate([packed] + [swap(packed, step) for step in (1, 2, 3)], axis=0)
    far = jnp.stack([far] + [swap(far, step) for step in (1, 2, 3)])
    count = far.shape[1] // own
    return near, far.reshape(4, count, own, -1).swapaxes(0, 1).reshape(4 * count * own, -1)


def scatter_sums(grads_near, grads_far, own):
    blocks = [
        grads[i * own : (i + 1) * own]
        for grads in (grads_near, grads_far)
        for i in range(grads.shape[0] // own)
    ]
    members = len(blocks)

    def moved(parts, step):
        value = jnp.concatenate([part.astype(SEND) for part in parts], axis=0)
        value = swap(value, step).astype(jnp.float32)
        return [value[i * own : (i + 1) * own] for i in range(len(parts))]

    far = range(4, members, 4)
    three = moved([blocks[i ^ 3] for i in far], 3)
    two = moved([blocks[i ^ 2] for i in far], 2)
    one = moved([blocks[i ^ 1] for i in far], 1)
    relayed = moved([blocks[3]], 1)[0]
    y_near = moved([blocks[1]], 1)[0]
    z_near = moved([blocks[2] + relayed], 2)[0]
    sums = [blocks[0] + z_near + y_near]
    sums += [blocks[i] + a + b + c for i, a, b, c in zip(far, three, one, two)]
    for step in far_steps()[::-1]:
        keep = len(sums) // 2
        sums = [a + b for a, b in zip(sums[:keep], moved(sums[keep:], step))]
    return sums[0]


def body(hidden, targets, head, global_frag, momentum, peer_delta):
    members = lax.axis_size(AXIS)
    own, depth = hidden.shape
    rows = own * members
    width = head.shape[1]

    packed = call(
        pack_kernel, [((own, depth + LANES), hidden.dtype)], [targets, hidden],
        scratch=[pltpu.SMEM(targets.shape, targets.dtype), pltpu.SemaphoreType.DMA((2,))],
        sources=[pltpu.HBM, pltpu.HBM],
    )[0]
    rows_near, rows_far = gather_rows(packed)
    near = call(
        load_kernel, [(head.shape, head.dtype)], [head],
        scratch=[pltpu.SemaphoreType.DMA((PARTS,))], sources=[pltpu.HBM],
    )[0]

    count = 4 * own
    near, logits_near, both_near, columns = call(
        first_kernel,
        [(head.shape, head.dtype), ((count, width), jnp.float32), ((2 * count, width), jnp.bfloat16),
         ((count, LANES), jnp.float32)],
        [rows_near, head, near], 2 * count * depth * width,
        scratch=[pltpu.SemaphoreType.DMA((PARTS,))],
        sources=[pltpu.VMEM, pltpu.HBM, pltpu.VMEM], aliases={2: 0},
    )
    count = rows - 4 * own
    logits_far, both_far, mine = call(
        second_kernel,
        [((count, width), jnp.float32), ((2 * count, width), jnp.bfloat16), ((8, rows), jnp.float32)],
        [rows_far, near, columns], 2 * count * depth * width,
        scratch=[pltpu.VMEM((rows, LANES), jnp.float32)],
    )

    lines = mine
    for steps in [[step] for step in far_steps()] + [[1, 2, 3]]:
        before = lines
        lines = call(
            functools.partial(merge_kernel, steps, members),
            [((8, rows), jnp.float32)], [lines] + [swap(lines, step) for step in steps],
        )[0]

    terms = [
        call(
            functools.partial(grad_kernel, first),
            [((depth // 2, 2 * rows), jnp.float32)], [both_near, both_far, near, *after],
            2 * rows * depth * width,
        )[0]
        for first, after in ((0, []), (depth // 2, [before]))
    ]

    scale = 2.0**14 * rows
    grads_far, grads_near = call(
        functools.partial(join_kernel, scale),
        [((rows - 4 * own, depth), jnp.float32), ((4 * own, depth), jnp.float32)],
        [lines, mine] + terms,
    )
    hidden_grad = (scatter_sums(grads_near, grads_far, own) * (1.0 / scale)).astype(jnp.bfloat16)
    new_global, new_momentum, loss = frag_update(
        members, [rows_near, rows_far], [rows_near, rows_far], lines, [logits_near, logits_far], near,
        global_frag, momentum, peer_delta,
    )
    return (loss, hidden_grad, new_global, new_momentum)


def solution(mesh):
    in_specs = (
        P(("outer", "vocab"), None),
        P(("outer", "vocab")),
        P("outer", "vocab"),
        P(None, "vocab"),
        P(None, "vocab"),
        P("outer", "vocab"),
    )
    out_specs = (P("outer"), P(("outer", "vocab"), None), P("outer", "vocab"), P("outer", "vocab"))
    return jax.shard_map(body, mesh=mesh, in_specs=in_specs, out_specs=out_specs, check_vma=False)
```

```python
import functools

import jax
import jax.numpy as jnp
from jax import lax
from jax.experimental import pallas as pl
from jax.experimental.pallas import tpu as pltpu
from jax.sharding import PartitionSpec as P

FRAG = 128
REPLICAS = 4
AXIS = "vocab"
SEND = jnp.float16
LANES = 128
VMEM = pl.BlockSpec(memory_space=pltpu.VMEM)


def call(kernel, outs, operands, flops=0, scratch=(), sources=None, vmem=16 * 2**20, aliases={}):
    outs = [pltpu.VMEM(shape, dtype) for shape, dtype in outs]
    places = sources or [pltpu.VMEM] * len(operands)
    moved = sum(x.size * x.dtype.itemsize for x in operands)
    return pl.pallas_call(
        kernel,
        out_shape=outs,
        in_specs=[pl.BlockSpec(memory_space=place) for place in places],
        out_specs=[VMEM] * len(outs),
        scratch_shapes=list(scratch),
        input_output_aliases=aliases,
        compiler_params=pltpu.CompilerParams(vmem_limit_bytes=vmem),
        cost_estimate=pl.CostEstimate(flops=flops, bytes_accessed=moved, transcendentals=0),
    )(*[pltpu.with_memory_space_constraint(x, place) for x, place in zip(operands, places)])


PARTS = 8
AHEAD = 6


def head_copies(source, target, sems, first, last):
    width = source.shape[1] // PARTS
    copies = []
    for part in range(first, last):
        columns = pl.ds(part * width, width)
        copies.append(pltpu.make_async_copy(source.at[:, columns], target.at[:, columns], sems.at[part]))
    return copies


def load_kernel(head, near_ref, sems):
    copies = head_copies(head, near_ref, sems, 0, AHEAD)
    for copy in copies:
        copy.start()
    for copy in copies:
        copy.wait()


TILE = 1024
WIDE = 2048


def pack_kernel(targets, rows, out_ref, targets_ref, sems):
    own, depth = rows.shape
    ids_copy = pltpu.make_async_copy(targets, targets_ref, sems.at[0])
    rows_copy = pltpu.make_async_copy(rows, out_ref.at[:, pl.ds(0, depth)], sems.at[1])
    ids_copy.start()
    rows_copy.start()
    ids_copy.wait()
    place = lax.broadcasted_iota(jnp.int32, (own, LANES), 0)
    ids = jnp.zeros((own, LANES), jnp.int32)
    for i in range(own):
        ids = jnp.where(place == i, targets_ref[i], ids)
    lane = lax.broadcasted_iota(jnp.int32, (own, LANES), 1)
    digits = jnp.where(lane == 0, ids // 256, ids % 256)
    out_ref[:, depth:] = digits.astype(jnp.float32).astype(jnp.bfloat16)
    rows_copy.wait()


def ids_of(digits):
    digits = digits.astype(jnp.float32)
    return (digits[:, 0:1] * 256.0 + digits[:, 1:2]).astype(jnp.int32)


def swap_blocks(value, group):
    size = value.shape[1]
    lane = lax.broadcasted_iota(jnp.int32, value.shape, 1)
    up, down = pltpu.roll(value, group, 1), pltpu.roll(value, size - group, 1)
    return jnp.where((lane & group) != 0, up, down)


def shared_order(value, members):
    me = lax.axis_index(AXIS)
    step = 1
    while step < members:
        swapped = swap_blocks(value, value.shape[1] // members * step)
        value = jnp.where((me & step) != 0, swapped, value)
        step *= 2
    return value


def as_columns(line):
    return jnp.broadcast_to(line, (LANES, line.shape[1])).T[:, 0:1]


def logits_of(rows_ref, near_ref, logits_ref, first, last):
    depth = near_ref.shape[0]
    while first < last:
        part = pl.ds(first, min(WIDE, last - first))
        logits_ref[:, part] = jnp.dot(
            rows_ref[:, :depth], near_ref[:, part], preferred_element_type=jnp.float32
        )
        first += WIDE


def softmax_of(rows_ref, logits_ref, both_ref, columns_ref, first):
    rows, width = logits_ref.shape
    digits = rows_ref.shape[1] - LANES
    chunk = 32
    offset = lax.axis_index(AXIS) * width

    @pl.loop(0, rows // chunk)
    def _(i):
        part = pl.ds(pl.multiple_of(i * chunk, chunk), chunk)
        logits = logits_ref[part, :]
        ids = ids_of(rows_ref[part, digits:]) - offset
        hit = lax.broadcasted_iota(jnp.int32, logits.shape, 1) == ids
        top = jnp.max(logits, axis=1, keepdims=True)
        raised = jnp.exp(logits - top)
        total = jnp.sum(raised, axis=1, keepdims=True)
        pick = jnp.sum(jnp.where(hit, logits, 0.0), axis=1, keepdims=True)
        both_ref[part, :] = jnp.where(hit, 0.0, raised).astype(jnp.bfloat16)
        other = pl.ds(pl.multiple_of(rows + i * chunk, chunk), chunk)
        both_ref[other, :] = jnp.where(hit, 1.0, 0.0).astype(jnp.bfloat16)
        place = lax.broadcasted_iota(jnp.int32, (chunk, LANES), 1)
        slot = pl.ds(pl.multiple_of(first + i * chunk, chunk), chunk)
        columns_ref[slot, :] = jnp.where(place == 0, top, jnp.where(place == 1, total, pick))


def first_kernel(packed_ref, head, held_ref, near_ref, logits_ref, both_ref, columns_ref, sems):
    width = near_ref.shape[1]
    there = width // PARTS * AHEAD
    copies = head_copies(head, near_ref, sems, AHEAD, PARTS)
    for copy in copies:
        copy.start()
    logits_of(packed_ref, near_ref, logits_ref, 0, there)
    for copy in copies:
        copy.wait()
    logits_of(packed_ref, near_ref, logits_ref, there, width)
    softmax_of(packed_ref, logits_ref, both_ref, columns_ref, 0)


def second_kernel(rows_ref, near_ref, before_ref, logits_ref, both_ref, lines_ref, columns_ref):
    first = before_ref.shape[0]
    logits_of(rows_ref, near_ref, logits_ref, 0, near_ref.shape[1])
    softmax_of(rows_ref, logits_ref, both_ref, columns_ref, first)
    columns_ref[pl.ds(0, first), :] = before_ref[...]
    lines_ref[...] = columns_ref[...].T[:8]


def merge_kernel(steps, members, mine_ref, *refs):
    *other_refs, out_ref = refs
    block = mine_ref.shape[1] // members
    me = lax.axis_index(AXIS)
    groups = [mine_ref[...]]
    for step, other_ref in zip(steps, other_refs):
        other, bit = other_ref[...], 1
        while bit <= step:
            if step & bit:
                other = swap_blocks(other, block * bit)
            bit *= 2
        groups.append(other)
    unit, bit = steps[0], 1
    while bit < len(groups):
        upper = (me & (unit * bit)) != 0
        groups = [jnp.where(upper, groups[i ^ bit], group) for i, group in enumerate(groups)]
        bit *= 2
    top = functools.reduce(jnp.maximum, [group[0:1] for group in groups])
    total = sum(group[1:2] * jnp.exp(group[0:1] - top) for group in groups)
    pick = sum(group[2:3] for group in groups)
    place = lax.broadcasted_iota(jnp.int32, out_ref.shape, 0)
    out_ref[...] = jnp.where(place == 0, top, jnp.where(place == 1, total, pick))


def grad_kernel(first, one_ref, two_ref, near_ref, *refs):
    terms_ref = refs[-1]
    one, two = one_ref.shape[0] // 2, two_ref.shape[0] // 2
    both = jnp.concatenate([one_ref[:one], two_ref[:two], one_ref[one:], two_ref[two:]], axis=0)
    tile = min(terms_ref.shape[0], 2**19 // both.shape[0])
    for place in range(0, terms_ref.shape[0], tile):
        terms_ref[pl.ds(place, tile), :] = lax.dot_general(
            near_ref[pl.ds(first + place, tile), :], both, (((1,), (1,)), ((), ())),
            preferred_element_type=jnp.float32,
        )


def join_kernel(scale, lines_ref, mine_ref, *refs):
    *terms_refs, far_ref, near_ref = refs
    rows = mine_ref.shape[1]
    near = near_ref.shape[0]
    top, total = lines_ref[0:1, :], lines_ref[1:2, :]
    soft = jnp.exp(mine_ref[0:1, :] - top) / (total * rows) * scale
    hard = (jnp.exp(jnp.minimum(mine_ref[2:3, :] - top, 0.0)) / total - 1.0) / rows
    hard = hard.astype(jnp.bfloat16).astype(jnp.float32) * scale
    tile = 512
    for place, terms_ref in enumerate(terms_refs):
        for first in range(0, terms_ref.shape[0], tile):
            part = pl.ds(first, tile)
            value = (soft * terms_ref[part, :rows] + hard * terms_ref[part, rows:]).T
            columns = pl.ds(place * terms_ref.shape[0] + first, tile)
            near_ref[:, columns] = value[:near]
            far_ref[:, columns] = value[near:]


def frag_kernel(members, rows_one_ref, rows_two_ref, ids_one_ref, ids_two_ref, lines_ref, one_ref, two_ref, head_ref,
                global_ref, momentum_ref, peer_ref, new_global_ref, new_momentum_ref, loss_ref):
    logits = jnp.concatenate([one_ref[...], two_ref[...]], axis=0)
    held = jnp.concatenate([rows_one_ref[...], rows_two_ref[...]], axis=0)
    ids = jnp.concatenate([ids_of(ids_one_ref[...]), ids_of(ids_two_ref[...])], axis=0)
    rows, tile = logits.shape

    @pl.when(pl.program_id(0) == 0)
    def _():
        lines = shared_order(lines_ref[...], members)
        loss_ref[0] = jnp.sum(lines[0:1] + jnp.log(lines[1:2]) - lines[2:3]) / rows

    top, share = as_columns(lines_ref[0:1, :]), as_columns(1.0 / lines_ref[1:2, :])
    offset = (lax.axis_index(AXIS) * pl.num_programs(0) + pl.program_id(0)) * tile
    hit = lax.broadcasted_iota(jnp.int32, (rows, tile), 1) == ids - offset
    shares = jnp.exp(logits - top) * share
    dlogits = ((shares - jnp.where(hit, 1.0, 0.0)) * (1.0 / rows)).astype(jnp.bfloat16)
    turned = held.astype(jnp.float32).T.astype(jnp.bfloat16)
    frag_grad = jnp.dot(turned, dlogits, preferred_element_type=jnp.float32)
    local_frag = head_ref[...].astype(jnp.float32) - 1.0 * frag_grad
    pseudo = (global_ref[...] - local_frag + peer_ref[...]) / REPLICAS
    new_momentum = 0.9 * momentum_ref[...] + pseudo
    new_momentum_ref[...] = new_momentum
    new_global_ref[...] = global_ref[...] - 0.7 * (pseudo + 0.9 * new_momentum)


def frag_update(members, held, ids, lines, logits, near, global_frag, momentum, peer_delta):
    rows = lines.shape[1]
    width = near.shape[1]
    tile = pl.BlockSpec((FRAG, TILE), lambda i: (0, i))

    return pl.pallas_call(
        functools.partial(frag_kernel, members),
        grid=(width // TILE,),
        out_shape=[jax.ShapeDtypeStruct((FRAG, width), jnp.float32)] * 2
        + [jax.ShapeDtypeStruct((1,), jnp.float32)],
        in_specs=[pl.BlockSpec((x.shape[0], FRAG), lambda i: (0, 0)) for x in held]
        + [
            pl.BlockSpec((x.shape[0], LANES), lambda i, last=x.shape[1] // LANES - 1: (0, last))
            for x in ids
        ]
        + [pl.BlockSpec((8, rows), lambda i: (0, 0))]
        + [pl.BlockSpec((x.shape[0], TILE), lambda i: (0, i)) for x in logits]
        + [tile] * 4,
        out_specs=[tile, tile, pl.BlockSpec(memory_space=pltpu.SMEM)],
        compiler_params=pltpu.CompilerParams(vmem_limit_bytes=16 * 2**20),
        cost_estimate=pl.CostEstimate(
            flops=2 * rows * FRAG * width, bytes_accessed=24 * FRAG * width, transcendentals=0
        ),
    )(
        *held, *ids, lines, *[pltpu.with_memory_space_constraint(x, pltpu.VMEM) for x in logits],
        pltpu.with_memory_space_constraint(near, pltpu.VMEM), global_frag, momentum, peer_delta,
    )


def swap(value, step):
    return lax.ppermute(value, AXIS, [(i, i ^ step) for i in range(lax.axis_size(AXIS))])


def far_steps():
    step = 4
    steps = []
    while step < lax.axis_size(AXIS):
        steps.append(step)
        step *= 2
    return steps


def gather_rows(packed):
    own = packed.shape[0]
    held = packed
    for step in far_steps():
        held = jnp.concatenate([held, swap(held, step)], axis=0)
    far = held[own:]
    near = jnp.concatenate([packed] + [swap(packed, step) for step in (1, 2, 3)], axis=0)
    far = jnp.stack([far] + [swap(far, step) for step in (1, 2, 3)])
    count = far.shape[1] // own
    return near, far.reshape(4, count, own, -1).swapaxes(0, 1).reshape(4 * count * own, -1)


def scatter_sums(grads_near, grads_far, own):
    blocks = [
        grads[i * own : (i + 1) * own]
        for grads in (grads_near, grads_far)
        for i in range(grads.shape[0] // own)
    ]
    members = len(blocks)

    def moved(parts, step):
        value = jnp.concatenate([part.astype(SEND) for part in parts], axis=0)
        value = swap(value, step).astype(jnp.float32)
        return [value[i * own : (i + 1) * own] for i in range(len(parts))]

    far = range(4, members, 4)
    three = moved([blocks[i ^ 3] for i in far], 3)
    two = moved([blocks[i ^ 2] for i in far], 2)
    one = moved([blocks[i ^ 1] for i in far], 1)
    relayed = moved([blocks[3]], 1)[0]
    y_near = moved([blocks[1]], 1)[0]
    z_near = moved([blocks[2] + relayed], 2)[0]
    sums = [blocks[0] + z_near + y_near]
    sums += [blocks[i] + a + b + c for i, a, b, c in zip(far, three, one, two)]
    for step in far_steps()[::-1]:
        keep = len(sums) // 2
        sums = [a + b for a, b in zip(sums[:keep], moved(sums[keep:], step))]
    return sums[0]


def body(hidden, targets, head, global_frag, momentum, peer_delta):
    members = lax.axis_size(AXIS)
    own, depth = hidden.shape
    rows = own * members
    width = head.shape[1]

    packed = call(
        pack_kernel, [((own, depth + LANES), hidden.dtype)], [targets, hidden],
        scratch=[pltpu.SMEM(targets.shape, targets.dtype), pltpu.SemaphoreType.DMA((2,))],
        sources=[pltpu.HBM, pltpu.HBM],
    )[0]
    rows_near, rows_far = gather_rows(packed)
    near = call(
        load_kernel, [(head.shape, head.dtype)], [head],
        scratch=[pltpu.SemaphoreType.DMA((PARTS,))], sources=[pltpu.HBM],
    )[0]

    count = 4 * own
    near, logits_near, both_near, columns = call(
        first_kernel,
        [(head.shape, head.dtype), ((count, width), jnp.float32), ((2 * count, width), jnp.bfloat16),
         ((count, LANES), jnp.float32)],
        [rows_near, head, near], 2 * count * depth * width,
        scratch=[pltpu.SemaphoreType.DMA((PARTS,))],
        sources=[pltpu.VMEM, pltpu.HBM, pltpu.VMEM], aliases={2: 0},
    )
    count = rows - 4 * own
    logits_far, both_far, mine = call(
        second_kernel,
        [((count, width), jnp.float32), ((2 * count, width), jnp.bfloat16), ((8, rows), jnp.float32)],
        [rows_far, near, columns], 2 * count * depth * width,
        scratch=[pltpu.VMEM((rows, LANES), jnp.float32)],
    )

    lines = mine
    for steps in [[step] for step in far_steps()] + [[1, 2, 3]]:
        before = lines
        lines = call(
            functools.partial(merge_kernel, steps, members),
            [((8, rows), jnp.float32)], [lines] + [swap(lines, step) for step in steps],
        )[0]

    terms = [
        call(
            functools.partial(grad_kernel, first),
            [((depth // 2, 2 * rows), jnp.float32)], [both_near, both_far, near, *after],
            2 * rows * depth * width,
        )[0]
        for first, after in ((0, []), (depth // 2, [before]))
    ]

    scale = 2.0**14 * rows
    grads_far, grads_near = call(
        functools.partial(join_kernel, scale),
        [((rows - 4 * own, depth), jnp.float32), ((4 * own, depth), jnp.float32)],
        [lines, mine] + terms,
    )
    hidden_grad = (scatter_sums(grads_near, grads_far, own) * (1.0 / scale)).astype(jnp.bfloat16)
    new_global, new_momentum, loss = frag_update(
        members, [rows_near, rows_far], [rows_near, rows_far], lines, [logits_near, logits_far], near,
        global_frag, momentum, peer_delta,
    )
    return (loss, hidden_grad, new_global, new_momentum)


def solution(mesh):
    in_specs = (
        P(("outer", "vocab"), None),
        P(("outer", "vocab")),
        P("outer", "vocab"),
        P(None, "vocab"),
        P(None, "vocab"),
        P("outer", "vocab"),
    )
    out_specs = (P("outer"), P(("outer", "vocab"), None), P("outer", "vocab"), P("outer", "vocab"))
    return jax.shard_map(body, mesh=mesh, in_specs=in_specs, out_specs=out_specs, check_vma=False)
```

```python
import functools

import jax
import jax.numpy as jnp
from jax import lax
from jax.experimental import pallas as pl
from jax.experimental.pallas import tpu as pltpu
from jax.sharding import PartitionSpec as P

FRAG = 128
REPLICAS = 4
AXIS = "vocab"
SEND = jnp.float16
LANES = 128
VMEM = pl.BlockSpec(memory_space=pltpu.VMEM)


def call(kernel, outs, operands, flops=0, scratch=(), sources=None, vmem=16 * 2**20, aliases={}):
    outs = [pltpu.VMEM(shape, dtype) for shape, dtype in outs]
    places = sources or [pltpu.VMEM] * len(operands)
    moved = sum(x.size * x.dtype.itemsize for x in operands)
    return pl.pallas_call(
        kernel,
        out_shape=outs,
        in_specs=[pl.BlockSpec(memory_space=place) for place in places],
        out_specs=[VMEM] * len(outs),
        scratch_shapes=list(scratch),
        input_output_aliases=aliases,
        compiler_params=pltpu.CompilerParams(vmem_limit_bytes=vmem),
        cost_estimate=pl.CostEstimate(flops=flops, bytes_accessed=moved, transcendentals=0),
    )(*[pltpu.with_memory_space_constraint(x, place) for x, place in zip(operands, places)])


PARTS = 8
AHEAD = 6


def head_copies(source, target, sems, first, last):
    width = source.shape[1] // PARTS
    copies = []
    for part in range(first, last):
        columns = pl.ds(part * width, width)
        copies.append(pltpu.make_async_copy(source.at[:, columns], target.at[:, columns], sems.at[part]))
    return copies


def load_kernel(head, near_ref, sems):
    copies = head_copies(head, near_ref, sems, 0, AHEAD)
    for copy in copies:
        copy.start()
    for copy in copies:
        copy.wait()


TILE = 1024
WIDE = 2048


def pack_kernel(targets, rows, out_ref, targets_ref, sems):
    own, depth = rows.shape
    ids_copy = pltpu.make_async_copy(targets, targets_ref, sems.at[0])
    rows_copy = pltpu.make_async_copy(rows, out_ref.at[:, pl.ds(0, depth)], sems.at[1])
    ids_copy.start()
    rows_copy.start()
    ids_copy.wait()
    place = lax.broadcasted_iota(jnp.int32, (own, LANES), 0)
    ids = jnp.zeros((own, LANES), jnp.int32)
    for i in range(own):
        ids = jnp.where(place == i, targets_ref[i], ids)
    lane = lax.broadcasted_iota(jnp.int32, (own, LANES), 1)
    digits = jnp.where(lane == 0, ids // 256, ids % 256)
    out_ref[:, depth:] = digits.astype(jnp.float32).astype(jnp.bfloat16)
    rows_copy.wait()


def ids_of(digits):
    digits = digits.astype(jnp.float32)
    return (digits[:, 0:1] * 256.0 + digits[:, 1:2]).astype(jnp.int32)


def swap_blocks(value, group):
    size = value.shape[1]
    lane = lax.broadcasted_iota(jnp.int32, value.shape, 1)
    up, down = pltpu.roll(value, group, 1), pltpu.roll(value, size - group, 1)
    return jnp.where((lane & group) != 0, up, down)


def shared_order(value, members):
    me = lax.axis_index(AXIS)
    step = 1
    while step < members:
        swapped = swap_blocks(value, value.shape[1] // members * step)
        value = jnp.where((me & step) != 0, swapped, value)
        step *= 2
    return value


def as_columns(line):
    return jnp.broadcast_to(line, (LANES, line.shape[1])).T[:, 0:1]


def logits_of(rows_ref, near_ref, logits_ref, first, last):
    depth = near_ref.shape[0]
    while first < last:
        part = pl.ds(first, min(WIDE, last - first))
        logits_ref[:, part] = jnp.dot(
            rows_ref[:, :depth], near_ref[:, part], preferred_element_type=jnp.float32
        )
        first += WIDE


def softmax_of(rows_ref, logits_ref, both_ref, columns_ref, first):
    rows, width = logits_ref.shape
    digits = rows_ref.shape[1] - LANES
    chunk = 32
    offset = lax.axis_index(AXIS) * width

    @pl.loop(0, rows // chunk)
    def _(i):
        part = pl.ds(pl.multiple_of(i * chunk, chunk), chunk)
        logits = logits_ref[part, :]
        ids = ids_of(rows_ref[part, digits:]) - offset
        hit = lax.broadcasted_iota(jnp.int32, logits.shape, 1) == ids
        top = jnp.max(logits, axis=1, keepdims=True)
        raised = jnp.exp(logits - top)
        total = jnp.sum(raised, axis=1, keepdims=True)
        pick = jnp.sum(jnp.where(hit, logits, 0.0), axis=1, keepdims=True)
        both_ref[part, :] = jnp.where(hit, 0.0, raised).astype(jnp.bfloat16)
        other = pl.ds(pl.multiple_of(rows + i * chunk, chunk), chunk)
        both_ref[other, :] = jnp.where(hit, 1.0, 0.0).astype(jnp.bfloat16)
        place = lax.broadcasted_iota(jnp.int32, (chunk, LANES), 1)
        slot = pl.ds(pl.multiple_of(first + i * chunk, chunk), chunk)
        columns_ref[slot, :] = jnp.where(place == 0, top, jnp.where(place == 1, total, pick))


def first_kernel(packed_ref, head, held_ref, near_ref, logits_ref, both_ref, columns_ref, sems):
    width = near_ref.shape[1]
    there = width // PARTS * AHEAD
    copies = head_copies(head, near_ref, sems, AHEAD, PARTS)
    for copy in copies:
        copy.start()
    logits_of(packed_ref, near_ref, logits_ref, 0, there)
    for copy in copies:
        copy.wait()
    logits_of(packed_ref, near_ref, logits_ref, there, width)
    softmax_of(packed_ref, logits_ref, both_ref, columns_ref, 0)


def second_kernel(rows_ref, near_ref, before_ref, logits_ref, both_ref, lines_ref, columns_ref):
    first = before_ref.shape[0]
    logits_of(rows_ref, near_ref, logits_ref, 0, near_ref.shape[1])
    softmax_of(rows_ref, logits_ref, both_ref, columns_ref, first)
    columns_ref[pl.ds(0, first), :] = before_ref[...]
    lines_ref[...] = columns_ref[...].T[:8]


def merge_kernel(steps, members, mine_ref, *refs):
    *other_refs, out_ref = refs
    block = mine_ref.shape[1] // members
    me = lax.axis_index(AXIS)
    groups = [mine_ref[...]]
    for step, other_ref in zip(steps, other_refs):
        other, bit = other_ref[...], 1
        while bit <= step:
            if step & bit:
                other = swap_blocks(other, block * bit)
            bit *= 2
        groups.append(other)
    unit, bit = steps[0], 1
    while bit < len(groups):
        upper = (me & (unit * bit)) != 0
        groups = [jnp.where(upper, groups[i ^ bit], group) for i, group in enumerate(groups)]
        bit *= 2
    top = functools.reduce(jnp.maximum, [group[0:1] for group in groups])
    total = sum(group[1:2] * jnp.exp(group[0:1] - top) for group in groups)
    pick = sum(group[2:3] for group in groups)
    place = lax.broadcasted_iota(jnp.int32, out_ref.shape, 0)
    out_ref[...] = jnp.where(place == 0, top, jnp.where(place == 1, total, pick))


def grad_kernel(first, one_ref, two_ref, near_ref, *refs):
    terms_ref = refs[-1]
    one, two = one_ref.shape[0] // 2, two_ref.shape[0] // 2
    both = jnp.concatenate([one_ref[:one], two_ref[:two], one_ref[one:], two_ref[two:]], axis=0)
    tile = min(terms_ref.shape[0], 2**19 // both.shape[0])
    for place in range(0, terms_ref.shape[0], tile):
        terms_ref[pl.ds(place, tile), :] = lax.dot_general(
            near_ref[pl.ds(first + place, tile), :], both, (((1,), (1,)), ((), ())),
            preferred_element_type=jnp.float32,
        )


def join_kernel(scale, lines_ref, mine_ref, *refs):
    *terms_refs, far_ref, near_ref = refs
    rows = mine_ref.shape[1]
    near = near_ref.shape[0]
    top, total = lines_ref[0:1, :], lines_ref[1:2, :]
    soft = jnp.exp(mine_ref[0:1, :] - top) / (total * rows) * scale
    hard = (jnp.exp(jnp.minimum(mine_ref[2:3, :] - top, 0.0)) / total - 1.0) / rows
    hard = hard.astype(jnp.bfloat16).astype(jnp.float32) * scale
    tile = 512
    for place, terms_ref in enumerate(terms_refs):
        for first in range(0, terms_ref.shape[0], tile):
            part = pl.ds(first, tile)
            value = (soft * terms_ref[part, :rows] + hard * terms_ref[part, rows:]).T
            columns = pl.ds(place * terms_ref.shape[0] + first, tile)
            near_ref[:, columns] = value[:near]
            far_ref[:, columns] = value[near:]


def frag_kernel(members, rows_one_ref, rows_two_ref, ids_one_ref, ids_two_ref, lines_ref, one_ref, two_ref, head_ref,
                global_ref, momentum_ref, peer_ref, new_global_ref, new_momentum_ref, loss_ref):
    logits = jnp.concatenate([one_ref[...], two_ref[...]], axis=0)
    held = jnp.concatenate([rows_one_ref[...], rows_two_ref[...]], axis=0)
    ids = jnp.concatenate([ids_of(ids_one_ref[...]), ids_of(ids_two_ref[...])], axis=0)
    rows, tile = logits.shape

    @pl.when(pl.program_id(0) == 0)
    def _():
        lines = shared_order(lines_ref[...], members)
        loss_ref[0] = jnp.sum(lines[0:1] + jnp.log(lines[1:2]) - lines[2:3]) / rows

    top, share = as_columns(lines_ref[0:1, :]), as_columns(1.0 / lines_ref[1:2, :])
    offset = (lax.axis_index(AXIS) * pl.num_programs(0) + pl.program_id(0)) * tile
    hit = lax.broadcasted_iota(jnp.int32, (rows, tile), 1) == ids - offset
    shares = jnp.exp(logits - top) * share
    dlogits = ((shares - jnp.where(hit, 1.0, 0.0)) * (1.0 / rows)).astype(jnp.bfloat16)
    turned = held.astype(jnp.float32).T.astype(jnp.bfloat16)
    frag_grad = jnp.dot(turned, dlogits, preferred_element_type=jnp.float32)
    local_frag = head_ref[...].astype(jnp.float32) - 1.0 * frag_grad
    pseudo = (global_ref[...] - local_frag + peer_ref[...]) / REPLICAS
    new_momentum = 0.9 * momentum_ref[...] + pseudo
    new_momentum_ref[...] = new_momentum
    new_global_ref[...] = global_ref[...] - 0.7 * (pseudo + 0.9 * new_momentum)


def frag_update(members, held, ids, lines, logits, near, global_frag, momentum, peer_delta):
    rows = lines.shape[1]
    width = near.shape[1]
    tile = pl.BlockSpec((FRAG, TILE), lambda i: (0, i))

    return pl.pallas_call(
        functools.partial(frag_kernel, members),
        grid=(width // TILE,),
        out_shape=[jax.ShapeDtypeStruct((FRAG, width), jnp.float32)] * 2
        + [jax.ShapeDtypeStruct((1,), jnp.float32)],
        in_specs=[pl.BlockSpec((x.shape[0], FRAG), lambda i: (0, 0)) for x in held]
        + [
            pl.BlockSpec((x.shape[0], LANES), lambda i, last=x.shape[1] // LANES - 1: (0, last))
            for x in ids
        ]
        + [pl.BlockSpec((8, rows), lambda i: (0, 0))]
        + [pl.BlockSpec((x.shape[0], TILE), lambda i: (0, i)) for x in logits]
        + [tile] * 4,
        out_specs=[tile, tile, pl.BlockSpec(memory_space=pltpu.SMEM)],
        compiler_params=pltpu.CompilerParams(vmem_limit_bytes=16 * 2**20),
        cost_estimate=pl.CostEstimate(
            flops=2 * rows * FRAG * width, bytes_accessed=24 * FRAG * width, transcendentals=0
        ),
    )(
        *held, *ids, lines, *[pltpu.with_memory_space_constraint(x, pltpu.VMEM) for x in logits],
        pltpu.with_memory_space_constraint(near, pltpu.VMEM), global_frag, momentum, peer_delta,
    )


def swap(value, step):
    return lax.ppermute(value, AXIS, [(i, i ^ step) for i in range(lax.axis_size(AXIS))])


def far_steps():
    step = 4
    steps = []
    while step < lax.axis_size(AXIS):
        steps.append(step)
        step *= 2
    return steps


def gather_rows(packed):
    own = packed.shape[0]
    held = packed
    for step in far_steps():
        held = jnp.concatenate([held, swap(held, step)], axis=0)
    far = held[own:]
    near = jnp.concatenate([packed] + [swap(packed, step) for step in (1, 2, 3)], axis=0)
    far = jnp.stack([far] + [swap(far, step) for step in (1, 2, 3)])
    count = far.shape[1] // own
    return near, far.reshape(4, count, own, -1).swapaxes(0, 1).reshape(4 * count * own, -1)


def scatter_sums(grads_near, grads_far, own):
    blocks = [
        grads[i * own : (i + 1) * own]
        for grads in (grads_near, grads_far)
        for i in range(grads.shape[0] // own)
    ]
    members = len(blocks)

    def moved(parts, step):
        value = jnp.concatenate([part.astype(SEND) for part in parts], axis=0)
        value = swap(value, step).astype(jnp.float32)
        return [value[i * own : (i + 1) * own] for i in range(len(parts))]

    far = range(4, members, 4)
    three = moved([blocks[i ^ 3] for i in far], 3)
    two = moved([blocks[i ^ 2] for i in far], 2)
    one = moved([blocks[i ^ 1] for i in far], 1)
    relayed = moved([blocks[3]], 1)[0]
    y_near = moved([blocks[1]], 1)[0]
    z_near = moved([blocks[2] + relayed], 2)[0]
    sums = [blocks[0] + z_near + y_near]
    sums += [blocks[i] + a + b + c for i, a, b, c in zip(far, one, two, three)]
    for step in far_steps()[::-1]:
        keep = len(sums) // 2
        sums = [a + b for a, b in zip(sums[:keep], moved(sums[keep:], step))]
    return sums[0]


def body(hidden, targets, head, global_frag, momentum, peer_delta):
    members = lax.axis_size(AXIS)
    own, depth = hidden.shape
    rows = own * members
    width = head.shape[1]

    packed = call(
        pack_kernel, [((own, depth + LANES), hidden.dtype)], [targets, hidden],
        scratch=[pltpu.SMEM(targets.shape, targets.dtype), pltpu.SemaphoreType.DMA((2,))],
        sources=[pltpu.HBM, pltpu.HBM],
    )[0]
    rows_near, rows_far = gather_rows(packed)
    near = call(
        load_kernel, [(head.shape, head.dtype)], [head],
        scratch=[pltpu.SemaphoreType.DMA((PARTS,))], sources=[pltpu.HBM],
    )[0]

    count = 4 * own
    near, logits_near, both_near, columns = call(
        first_kernel,
        [(head.shape, head.dtype), ((count, width), jnp.float32), ((2 * count, width), jnp.bfloat16),
         ((count, LANES), jnp.float32)],
        [rows_near, head, near], 2 * count * depth * width,
        scratch=[pltpu.SemaphoreType.DMA((PARTS,))],
        sources=[pltpu.VMEM, pltpu.HBM, pltpu.VMEM], aliases={2: 0},
    )
    count = rows - 4 * own
    logits_far, both_far, mine = call(
        second_kernel,
        [((count, width), jnp.float32), ((2 * count, width), jnp.bfloat16), ((8, rows), jnp.float32)],
        [rows_far, near, columns], 2 * count * depth * width,
        scratch=[pltpu.VMEM((rows, LANES), jnp.float32)],
    )

    lines = mine
    for steps in [[step] for step in far_steps()] + [[1, 2, 3]]:
        before = lines
        lines = call(
            functools.partial(merge_kernel, steps, members),
            [((8, rows), jnp.float32)], [lines] + [swap(lines, step) for step in steps],
        )[0]

    terms = [
        call(
            functools.partial(grad_kernel, first),
            [((depth // 2, 2 * rows), jnp.float32)], [both_near, both_far, near, *after],
            2 * rows * depth * width,
        )[0]
        for first, after in ((0, []), (depth // 2, [before]))
    ]

    scale = 2.0**14 * rows
    grads_far, grads_near = call(
        functools.partial(join_kernel, scale),
        [((rows - 4 * own, depth), jnp.float32), ((4 * own, depth), jnp.float32)],
        [lines, mine] + terms,
    )
    hidden_grad = (scatter_sums(grads_near, grads_far, own) * (1.0 / scale)).astype(jnp.bfloat16)
    new_global, new_momentum, loss = frag_update(
        members, [rows_near, rows_far], [rows_near, rows_far], lines, [logits_near, logits_far], near,
        global_frag, momentum, peer_delta,
    )
    return (loss, hidden_grad, new_global, new_momentum)


def solution(mesh):
    in_specs = (
        P(("outer", "vocab"), None),
        P(("outer", "vocab")),
        P("outer", "vocab"),
        P(None, "vocab"),
        P(None, "vocab"),
        P("outer", "vocab"),
    )
    out_specs = (P("outer"), P(("outer", "vocab"), None), P("outer", "vocab"), P("outer", "vocab"))
    return jax.shard_map(body, mesh=mesh, in_specs=in_specs, out_specs=out_specs, check_vma=False)
```

```python
import functools

import jax
import jax.numpy as jnp
from jax import lax
from jax.experimental import pallas as pl
from jax.experimental.pallas import tpu as pltpu
from jax.sharding import PartitionSpec as P

FRAG = 128
REPLICAS = 4
AXIS = "vocab"
SEND = jnp.float16
LANES = 128
VMEM = pl.BlockSpec(memory_space=pltpu.VMEM)


def call(kernel, outs, operands, flops=0, scratch=(), sources=None, vmem=16 * 2**20, aliases={}):
    outs = [pltpu.VMEM(shape, dtype) for shape, dtype in outs]
    places = sources or [pltpu.VMEM] * len(operands)
    moved = sum(x.size * x.dtype.itemsize for x in operands)
    return pl.pallas_call(
        kernel,
        out_shape=outs,
        in_specs=[pl.BlockSpec(memory_space=place) for place in places],
        out_specs=[VMEM] * len(outs),
        scratch_shapes=list(scratch),
        input_output_aliases=aliases,
        compiler_params=pltpu.CompilerParams(vmem_limit_bytes=vmem),
        cost_estimate=pl.CostEstimate(flops=flops, bytes_accessed=moved, transcendentals=0),
    )(*[pltpu.with_memory_space_constraint(x, place) for x, place in zip(operands, places)])


PARTS = 8
AHEAD = 6


def head_copies(source, target, sems, first, last):
    width = source.shape[1] // PARTS
    copies = []
    for part in range(first, last):
        columns = pl.ds(part * width, width)
        copies.append(pltpu.make_async_copy(source.at[:, columns], target.at[:, columns], sems.at[part]))
    return copies


def load_kernel(head, near_ref, sems):
    copies = head_copies(head, near_ref, sems, 0, AHEAD)
    for copy in copies:
        copy.start()
    for copy in copies:
        copy.wait()


TILE = 1024
WIDE = 2048


def pack_kernel(targets, rows, out_ref, targets_ref, sems):
    own, depth = rows.shape
    ids_copy = pltpu.make_async_copy(targets, targets_ref, sems.at[0])
    rows_copy = pltpu.make_async_copy(rows, out_ref.at[:, pl.ds(0, depth)], sems.at[1])
    ids_copy.start()
    rows_copy.start()
    ids_copy.wait()
    place = lax.broadcasted_iota(jnp.int32, (own, LANES), 0)
    ids = jnp.zeros((own, LANES), jnp.int32)
    for i in range(own):
        ids = jnp.where(place == i, targets_ref[i], ids)
    lane = lax.broadcasted_iota(jnp.int32, (own, LANES), 1)
    digits = jnp.where(lane == 0, ids // 256, ids % 256)
    out_ref[:, depth:] = digits.astype(jnp.float32).astype(jnp.bfloat16)
    rows_copy.wait()


def ids_of(digits):
    digits = digits.astype(jnp.float32)
    return (digits[:, 0:1] * 256.0 + digits[:, 1:2]).astype(jnp.int32)


def swap_blocks(value, group):
    size = value.shape[1]
    lane = lax.broadcasted_iota(jnp.int32, value.shape, 1)
    up, down = pltpu.roll(value, group, 1), pltpu.roll(value, size - group, 1)
    return jnp.where((lane & group) != 0, up, down)


def shared_order(value, members):
    me = lax.axis_index(AXIS)
    step = 1
    while step < members:
        swapped = swap_blocks(value, value.shape[1] // members * step)
        value = jnp.where((me & step) != 0, swapped, value)
        step *= 2
    return value


def as_columns(line):
    return jnp.broadcast_to(line, (LANES, line.shape[1])).T[:, 0:1]


def logits_of(rows_ref, near_ref, logits_ref, first, last):
    depth = near_ref.shape[0]
    while first < last:
        part = pl.ds(first, min(WIDE, last - first))
        logits_ref[:, part] = jnp.dot(
            rows_ref[:, :depth], near_ref[:, part], preferred_element_type=jnp.float32
        )
        first += WIDE


def softmax_of(rows_ref, logits_ref, both_ref, columns_ref, first):
    rows, width = logits_ref.shape
    digits = rows_ref.shape[1] - LANES
    chunk = 32
    offset = lax.axis_index(AXIS) * width

    @pl.loop(0, rows // chunk)
    def _(i):
        part = pl.ds(pl.multiple_of(i * chunk, chunk), chunk)
        logits = logits_ref[part, :]
        ids = ids_of(rows_ref[part, digits:]) - offset
        hit = lax.broadcasted_iota(jnp.int32, logits.shape, 1) == ids
        top = jnp.max(logits, axis=1, keepdims=True)
        raised = jnp.exp(logits - top)
        total = jnp.sum(raised, axis=1, keepdims=True)
        pick = jnp.sum(jnp.where(hit, logits, 0.0), axis=1, keepdims=True)
        both_ref[part, :] = jnp.where(hit, 0.0, raised).astype(jnp.bfloat16)
        other = pl.ds(pl.multiple_of(rows + i * chunk, chunk), chunk)
        both_ref[other, :] = jnp.where(hit, 1.0, 0.0).astype(jnp.bfloat16)
        place = lax.broadcasted_iota(jnp.int32, (chunk, LANES), 1)
        slot = pl.ds(pl.multiple_of(first + i * chunk, chunk), chunk)
        columns_ref[slot, :] = jnp.where(place == 0, top, jnp.where(place == 1, total, pick))


def first_kernel(packed_ref, head, held_ref, near_ref, logits_ref, both_ref, columns_ref, sems):
    width = near_ref.shape[1]
    there = width // PARTS * AHEAD
    copies = head_copies(head, near_ref, sems, AHEAD, PARTS)
    for copy in copies:
        copy.start()
    logits_of(packed_ref, near_ref, logits_ref, 0, there)
    for copy in copies:
        copy.wait()
    logits_of(packed_ref, near_ref, logits_ref, there, width)
    softmax_of(packed_ref, logits_ref, both_ref, columns_ref, 0)


def second_kernel(rows_ref, near_ref, before_ref, logits_ref, both_ref, lines_ref, columns_ref):
    first = before_ref.shape[0]
    logits_of(rows_ref, near_ref, logits_ref, 0, near_ref.shape[1])
    softmax_of(rows_ref, logits_ref, both_ref, columns_ref, first)
    columns_ref[pl.ds(0, first), :] = before_ref[...]
    lines_ref[...] = columns_ref[...].T[:8]


def merge_kernel(steps, members, mine_ref, *refs):
    *other_refs, out_ref = refs
    block = mine_ref.shape[1] // members
    me = lax.axis_index(AXIS)
    groups = [mine_ref[...]]
    for step, other_ref in zip(steps, other_refs):
        other, bit = other_ref[...], 1
        while bit <= step:
            if step & bit:
                other = swap_blocks(other, block * bit)
            bit *= 2
        groups.append(other)
    unit, bit = steps[0], 1
    while bit < len(groups):
        upper = (me & (unit * bit)) != 0
        groups = [jnp.where(upper, groups[i ^ bit], group) for i, group in enumerate(groups)]
        bit *= 2
    top = functools.reduce(jnp.maximum, [group[0:1] for group in groups])
    total = sum(group[1:2] * jnp.exp(group[0:1] - top) for group in groups)
    pick = sum(group[2:3] for group in groups)
    place = lax.broadcasted_iota(jnp.int32, out_ref.shape, 0)
    out_ref[...] = jnp.where(place == 0, top, jnp.where(place == 1, total, pick))


def grad_kernel(first, one_ref, two_ref, near_ref, *refs):
    terms_ref = refs[-1]
    one, two = one_ref.shape[0] // 2, two_ref.shape[0] // 2
    both = jnp.concatenate([one_ref[:one], two_ref[:two], one_ref[one:], two_ref[two:]], axis=0)
    tile = min(terms_ref.shape[0], 2**19 // both.shape[0])
    for place in range(0, terms_ref.shape[0], tile):
        terms_ref[pl.ds(place, tile), :] = lax.dot_general(
            near_ref[pl.ds(first + place, tile), :], both, (((1,), (1,)), ((), ())),
            preferred_element_type=jnp.float32,
        )


def join_kernel(scale, lines_ref, mine_ref, *refs):
    *terms_refs, far_ref, near_ref = refs
    rows = mine_ref.shape[1]
    near = near_ref.shape[0]
    top, total = lines_ref[0:1, :], lines_ref[1:2, :]
    soft = jnp.exp(mine_ref[0:1, :] - top) / (total * rows) * scale
    hard = (jnp.exp(jnp.minimum(mine_ref[2:3, :] - top, 0.0)) / total - 1.0) / rows
    hard = hard.astype(jnp.bfloat16).astype(jnp.float32) * scale
    tile = 512
    for place, terms_ref in enumerate(terms_refs):
        for first in range(0, terms_ref.shape[0], tile):
            part = pl.ds(first, tile)
            value = (soft * terms_ref[part, :rows] + hard * terms_ref[part, rows:]).T
            columns = pl.ds(place * terms_ref.shape[0] + first, tile)
            near_ref[:, columns] = value[:near]
            far_ref[:, columns] = value[near:]


def frag_kernel(members, rows_one_ref, rows_two_ref, ids_one_ref, ids_two_ref, lines_ref, one_ref, two_ref, head_ref,
                global_ref, momentum_ref, peer_ref, new_global_ref, new_momentum_ref, loss_ref):
    logits = jnp.concatenate([one_ref[...], two_ref[...]], axis=0)
    held = jnp.concatenate([rows_one_ref[...], rows_two_ref[...]], axis=0)
    ids = jnp.concatenate([ids_of(ids_one_ref[...]), ids_of(ids_two_ref[...])], axis=0)
    rows, tile = logits.shape

    @pl.when(pl.program_id(0) == 0)
    def _():
        lines = shared_order(lines_ref[...], members)
        loss_ref[0] = jnp.sum(lines[0:1] + jnp.log(lines[1:2]) - lines[2:3]) / rows

    top, share = as_columns(lines_ref[0:1, :]), as_columns(1.0 / lines_ref[1:2, :])
    offset = (lax.axis_index(AXIS) * pl.num_programs(0) + pl.program_id(0)) * tile
    hit = lax.broadcasted_iota(jnp.int32, (rows, tile), 1) == ids - offset
    shares = jnp.exp(logits - top) * share
    dlogits = ((shares - jnp.where(hit, 1.0, 0.0)) * (1.0 / rows)).astype(jnp.bfloat16)
    turned = held.astype(jnp.float32).T.astype(jnp.bfloat16)
    frag_grad = jnp.dot(turned, dlogits, preferred_element_type=jnp.float32)
    local_frag = head_ref[...].astype(jnp.float32) - 1.0 * frag_grad
    pseudo = (global_ref[...] - local_frag + peer_ref[...]) / REPLICAS
    new_momentum = 0.9 * momentum_ref[...] + pseudo
    new_momentum_ref[...] = new_momentum
    new_global_ref[...] = global_ref[...] - 0.7 * (pseudo + 0.9 * new_momentum)


def frag_update(members, held, ids, lines, logits, near, global_frag, momentum, peer_delta):
    rows = lines.shape[1]
    width = near.shape[1]
    tile = pl.BlockSpec((FRAG, TILE), lambda i: (0, i))

    return pl.pallas_call(
        functools.partial(frag_kernel, members),
        grid=(width // TILE,),
        out_shape=[jax.ShapeDtypeStruct((FRAG, width), jnp.float32)] * 2
        + [jax.ShapeDtypeStruct((1,), jnp.float32)],
        in_specs=[pl.BlockSpec((x.shape[0], FRAG), lambda i: (0, 0)) for x in held]
        + [
            pl.BlockSpec((x.shape[0], LANES), lambda i, last=x.shape[1] // LANES - 1: (0, last))
            for x in ids
        ]
        + [pl.BlockSpec((8, rows), lambda i: (0, 0))]
        + [pl.BlockSpec((x.shape[0], TILE), lambda i: (0, i)) for x in logits]
        + [tile] * 4,
        out_specs=[tile, tile, pl.BlockSpec(memory_space=pltpu.SMEM)],
        compiler_params=pltpu.CompilerParams(vmem_limit_bytes=16 * 2**20),
        cost_estimate=pl.CostEstimate(
            flops=2 * rows * FRAG * width, bytes_accessed=24 * FRAG * width, transcendentals=0
        ),
    )(
        *held, *ids, lines, *[pltpu.with_memory_space_constraint(x, pltpu.VMEM) for x in logits],
        pltpu.with_memory_space_constraint(near, pltpu.VMEM), global_frag, momentum, peer_delta,
    )


def swap(value, step):
    return lax.ppermute(value, AXIS, [(i, i ^ step) for i in range(lax.axis_size(AXIS))])


def far_steps():
    step = 4
    steps = []
    while step < lax.axis_size(AXIS):
        steps.append(step)
        step *= 2
    return steps


def gather_rows(packed):
    own = packed.shape[0]
    held = packed
    for step in far_steps():
        held = jnp.concatenate([held, swap(held, step)], axis=0)
    far = held[own:]
    near = jnp.concatenate([packed] + [swap(packed, step) for step in (1, 2, 3)], axis=0)
    far = jnp.stack([far] + [swap(far, step) for step in (1, 2, 3)])
    count = far.shape[1] // own
    return near, far.reshape(4, count, own, -1).swapaxes(0, 1).reshape(4 * count * own, -1)


def scatter_sums(grads_near, grads_far, own):
    blocks = [
        grads[i * own : (i + 1) * own]
        for grads in (grads_near, grads_far)
        for i in range(grads.shape[0] // own)
    ]
    members = len(blocks)

    def moved(parts, step):
        value = jnp.concatenate([part.astype(SEND) for part in parts], axis=0)
        value = swap(value, step).astype(jnp.float32)
        return [value[i * own : (i + 1) * own] for i in range(len(parts))]

    far = range(4, members, 4)
    three = moved([blocks[i ^ 3] for i in far], 3)
    two = moved([blocks[i ^ 2] for i in far], 2)
    one = moved([blocks[i ^ 1] for i in far], 1)
    relayed = moved([blocks[3]], 1)[0]
    y_near = moved([blocks[1]], 1)[0]
    z_near = moved([blocks[2] + relayed], 2)[0]
    sums = [blocks[0] + z_near + y_near]
    sums += [blocks[i] + a + b + c for i, a, b, c in zip(far, one, three, two)]
    for step in far_steps()[::-1]:
        keep = len(sums) // 2
        sums = [a + b for a, b in zip(sums[:keep], moved(sums[keep:], step))]
    return sums[0]


def body(hidden, targets, head, global_frag, momentum, peer_delta):
    members = lax.axis_size(AXIS)
    own, depth = hidden.shape
    rows = own * members
    width = head.shape[1]

    packed = call(
        pack_kernel, [((own, depth + LANES), hidden.dtype)], [targets, hidden],
        scratch=[pltpu.SMEM(targets.shape, targets.dtype), pltpu.SemaphoreType.DMA((2,))],
        sources=[pltpu.HBM, pltpu.HBM],
    )[0]
    rows_near, rows_far = gather_rows(packed)
    near = call(
        load_kernel, [(head.shape, head.dtype)], [head],
        scratch=[pltpu.SemaphoreType.DMA((PARTS,))], sources=[pltpu.HBM],
    )[0]

    count = 4 * own
    near, logits_near, both_near, columns = call(
        first_kernel,
        [(head.shape, head.dtype), ((count, width), jnp.float32), ((2 * count, width), jnp.bfloat16),
         ((count, LANES), jnp.float32)],
        [rows_near, head, near], 2 * count * depth * width,
        scratch=[pltpu.SemaphoreType.DMA((PARTS,))],
        sources=[pltpu.VMEM, pltpu.HBM, pltpu.VMEM], aliases={2: 0},
    )
    count = rows - 4 * own
    logits_far, both_far, mine = call(
        second_kernel,
        [((count, width), jnp.float32), ((2 * count, width), jnp.bfloat16), ((8, rows), jnp.float32)],
        [rows_far, near, columns], 2 * count * depth * width,
        scratch=[pltpu.VMEM((rows, LANES), jnp.float32)],
    )

    lines = mine
    for steps in [[step] for step in far_steps()] + [[1, 2, 3]]:
        before = lines
        lines = call(
            functools.partial(merge_kernel, steps, members),
            [((8, rows), jnp.float32)], [lines] + [swap(lines, step) for step in steps],
        )[0]

    terms = [
        call(
            functools.partial(grad_kernel, first),
            [((depth // 2, 2 * rows), jnp.float32)], [both_near, both_far, near, *after],
            2 * rows * depth * width,
        )[0]
        for first, after in ((0, []), (depth // 2, [before]))
    ]

    scale = 2.0**14 * rows
    grads_far, grads_near = call(
        functools.partial(join_kernel, scale),
        [((rows - 4 * own, depth), jnp.float32), ((4 * own, depth), jnp.float32)],
        [lines, mine] + terms,
    )
    hidden_grad = (scatter_sums(grads_near, grads_far, own) * (1.0 / scale)).astype(jnp.bfloat16)
    new_global, new_momentum, loss = frag_update(
        members, [rows_near, rows_far], [rows_near, rows_far], lines, [logits_near, logits_far], near,
        global_frag, momentum, peer_delta,
    )
    return (loss, hidden_grad, new_global, new_momentum)


def solution(mesh):
    in_specs = (
        P(("outer", "vocab"), None),
        P(("outer", "vocab")),
        P("outer", "vocab"),
        P(None, "vocab"),
        P(None, "vocab"),
        P("outer", "vocab"),
    )
    out_specs = (P("outer"), P(("outer", "vocab"), None), P("outer", "vocab"), P("outer", "vocab"))
    return jax.shard_map(body, mesh=mesh, in_specs=in_specs, out_specs=out_specs, check_vma=False)
```
